32 devices in a mesh: section: 2 (over core), dp: 4 (over z), ctx: 4 (over y, x).
Axes of the slice: x: 2, y: 2, z: 4, core: 2. Of those that a mesh axis runs over, the one named last changes fastest.
Arguments:
- ends_in: bfloat16 [2, 6, 2048, 768], P('section', None, ('dp', 'ctx')), may hold values from -6 to 6
- begins: int32 [6, 32], P(None, ('dp', 'ctx')), may hold values from 0 to 1, as said below
- filled: int32 [6, 32], P(None, ('dp', 'ctx')), may hold values from 1 to 64, as said below
- first_gain: bfloat16 [2, 768], P('section'), may hold values from 0.5 to 1.5
- first_shift: bfloat16 [2, 768], P('section'), may hold values from -4 to 4
- qkv_weight: bfloat16 [2, 768, 2304], P('section'), may hold values from -0.21875 to 0.21875
- qkv_bias: bfloat16 [2, 2304], P('section'), may hold values from -4 to 4
- query_map: bfloat16 [2, 64, 768], P('section'), may hold values from -1.5 to 1.5
- key_map: bfloat16 [2, 64, 768], P('section'), may hold values from -1.5 to 1.5
- out_weight: bfloat16 [2, 768, 768], P('section'), may hold values from -3.5 to 3.5
- out_bias: bfloat16 [2, 768], P('section'), may hold values from -4 to 4
- second_gain: bfloat16 [2, 768], P('section'), may hold values from 0.5 to 1.5
- second_shift: bfloat16 [2, 768], P('section'), may hold values from -4 to 4
- up_weight: bfloat16 [2, 768, 3072], P('section'), may hold values from -0.21875 to 0.21875
- up_bias: bfloat16 [2, 3072], P('section'), may hold values from -4 to 4
- down_weight: bfloat16 [2, 3072, 768], P('section'), may hold values from -0.109375 to 0.109375
- down_bias: bfloat16 [2, 768], P('section'), may hold values from -4 to 4
Outputs:
- ends_out: bfloat16 [2, 6, 2048, 768], P('section', None, ('dp', 'ctx'))
- grad_first_gain: float32 [2, 768], P('section')
- grad_first_shift: float32 [2, 768], P('section')
- grad_qkv_weight: float32 [2, 768, 2304], P('section')
- grad_qkv_bias: float32 [2, 2304], P('section')
- grad_query_map: float32 [2, 64, 768], P('section')
- grad_key_map: float32 [2, 64, 768], P('section')
- grad_out_weight: float32 [2, 768, 768], P('section')
- grad_out_bias: float32 [2, 768], P('section')
- grad_second_gain: float32 [2, 768], P('section')
- grad_second_shift: float32 [2, 768], P('section')
- grad_up_weight: float32 [2, 768, 3072], P('section')
- grad_up_bias: float32 [2, 3072], P('section')
- grad_down_weight: float32 [2, 3072, 768], P('section')
- grad_down_bias: float32 [2, 768], P('section')
The draws below stay inside these ranges and needn't reach their ends.
Inputs may be any that keep to these rules, and one draw needn't show every extreme that they name: Each group of 8 blocks (one index of dp) has begins = 1 at its first block. In one micro-batch of each group, drawn from the seed, that is its only start; elsewhere sequences cover 2 to 31 blocks, heavy tailed, the last one cut at the group's end. `filled`: 64 except in the last block of a sequence; valid tokens come first in a block.
All inputs are finite; a program needn't handle non-finite values.
Results may differ from the reference program's by a relative error of at most 0.012.
The reference program's roundings to bfloat16 on the way count: a program that leaves them out, or rounds other values in their place, can miss the bound.
Values may be sent and summed in bfloat16 or wider, within the bound.
A program may use at most 448 MiB of HBM per device.

```python
import jax
import jax.numpy as jnp
from jax import lax

D = 768
H = 12
DH = 64
FF = 3072
F = 128
BLOCK = 64
MICRO = 6
GROUP_BLOCKS = 8
BLOCKS = 32
TOKENS = 2048
N_DP = 4


def sequence_plan(key):
    power_key, extra_key, pick_key, fill_key = jax.random.split(key, 4)
    shape = (MICRO, N_DP, GROUP_BLOCKS)
    powers = jax.random.randint(power_key, shape, 1, 5)
    base = jnp.left_shift(jnp.ones(shape, jnp.int32), powers)
    extras = jax.random.randint(extra_key, shape, 0, base)
    lengths = base + extras
    ends = jnp.cumsum(lengths, 2)
    starts_at = ends - lengths
    places = jnp.arange(GROUP_BLOCKS)
    packed = jnp.sum((starts_at[:, :, :, None] == places[None, None, None, :]).astype(jnp.int32), 2)
    spanning = jax.random.randint(pick_key, (1, N_DP, 1), 0, MICRO)
    micro_ids = jnp.arange(MICRO)[:, None, None]
    whole = jnp.broadcast_to((places == 0).astype(jnp.int32)[None, None, :], shape)
    starts = jnp.where(micro_ids == spanning, whole, jnp.minimum(packed, 1))
    following = jnp.concatenate([starts[:, :, 1:], jnp.ones((MICRO, N_DP, 1), jnp.int32)], 2)
    amounts = jax.random.randint(fill_key, shape, 1, BLOCK + 1)
    counts = jnp.where(following == 1, amounts, BLOCK)
    return (starts.reshape(MICRO, BLOCKS).astype(jnp.int32), counts.reshape(MICRO, BLOCKS).astype(jnp.int32))


def draw_begins(key, part):
    return sequence_plan(key)[0]


def draw_filled(key, part):
    return sequence_plan(key)[1]


def block_levels(key, dims, cuts, smallest, high):
    level, own = 1.0, jax.random.fold_in(key, 6)
    for dim, parts in cuts:
        heights = jnp.exp(jax.random.uniform(jax.random.fold_in(own, dim), (parts,), jnp.float32, smallest / len(cuts), high / len(cuts)))
        level = level * jnp.repeat(heights, dims[dim] // parts).reshape([-1 if axis == dim else 1 for axis in range(len(dims))])
    return level


def normal_values(key, shape, width, bound, cuts=(), held_as=jnp.bfloat16):
    loudness = block_levels(key, shape, cuts, -0.22, 0.18) if cuts else 1.0
    values = jax.random.normal(key, shape, jnp.float32) * width * loudness
    return jnp.minimum(jnp.maximum(values, -bound), bound).astype(held_as)


def setup_inputs(seed: int = 0) -> dict:
    key_of = jax.random.split(jax.random.key(seed), 18)
    return {
        "ends_in": normal_values(key_of[0], (2, MICRO, TOKENS, D), 1.0, 6.0, ((0, 2), (2, 16))),
        "begins": draw_begins(jax.random.fold_in(key_of[17], 71), 0),
        "filled": draw_filled(jax.random.fold_in(key_of[17], 71), 0),
        "first_gain": jnp.clip(1.0 + 0.1 * jax.random.normal(key_of[3], (2, D), jnp.float32), 0.5, 1.5).astype(jnp.bfloat16),
        "first_shift": normal_values(key_of[4], (2, D), 0.3, 4.0, ((0, 2),)),
        "qkv_weight": normal_values(key_of[5], (2, D, 3 * D), D ** -0.5, 0.21875, ((0, 2),)),
        "qkv_bias": normal_values(key_of[6], (2, 3 * D), 0.3, 4.0, ((0, 2),)),
        "query_map": normal_values(key_of[7], (2, DH, D), (DH // 4) ** -0.5, 1.5, ((0, 2),)),
        "key_map": normal_values(key_of[8], (2, DH, D), (DH // 4) ** -0.5, 1.5, ((0, 2),)),
        "out_weight": normal_values(key_of[9], (2, D, D), (max(D // 256, 1)) ** -0.5, 3.5, ((0, 2),)),
        "out_bias": normal_values(key_of[10], (2, D), 0.3, 4.0, ((0, 2),)),
        "second_gain": jnp.clip(1.0 + 0.1 * jax.random.normal(key_of[11], (2, D), jnp.float32), 0.5, 1.5).astype(jnp.bfloat16),
        "second_shift": normal_values(key_of[12], (2, D), 0.3, 4.0, ((0, 2),)),
        "up_weight": normal_values(key_of[13], (2, D, FF), D ** -0.5, 0.21875, ((0, 2),)),
        "up_bias": normal_values(key_of[14], (2, FF), 0.3, 4.0, ((0, 2),)),
        "down_weight": normal_values(key_of[15], (2, FF, D), FF ** -0.5, 0.109375, ((0, 2),)),
        "down_bias": normal_values(key_of[16], (2, D), 0.3, 4.0, ((0, 2),)),
    }


@jax.custom_vjp
def low(v):
    return lax.optimization_barrier(v.astype(jnp.bfloat16)).astype(jnp.float32)

@jax.custom_vjp
def low_back(v):
    return v

def low_keep(v):
    return (low(v), None)

def low_pass(kept, grad):
    return (grad,)

def back_keep(v):
    return (v, None)

def back_low(kept, grad):
    return (low(grad),)
low.defvjp(low_keep, low_pass)
low_back.defvjp(back_keep, back_low)
epsilon = 1e-05
highest = lax.Precision.HIGHEST

def matmul(left, right):
    return jnp.dot(left, right, precision=highest, preferred_element_type=jnp.float32)

def layer_norm(rows, gain, shift):
    average = lax.optimization_barrier(jnp.mean(rows, -1, keepdims=True))
    centred = rows - average
    variance = lax.optimization_barrier(jnp.mean(centred * centred, -1, keepdims=True))
    return centred * lax.rsqrt(variance + epsilon) * gain + shift

def feature_map(logits):
    return jnp.concatenate([jax.nn.softmax(logits, -1), jax.nn.softmax(-logits, -1)], -1)

def features(heads, table):
    logits = low_back(jnp.einsum('rhi,ihj->rhj', heads, table.reshape(DH, H, DH), precision=highest))
    return low(feature_map(logits))

def block_step(carried, inputs_here):
    states, key_sums = carried
    queries, key_rows, values_h, usable, starting = inputs_here
    kept_share = 1.0 - starting
    states = states * kept_share[:, None, None, None]
    key_sums = key_sums * kept_share[:, None, None]
    key_rows = key_rows * usable[:, :, None, None]
    causal = jnp.tril(jnp.ones((BLOCK, BLOCK), jnp.float32))
    scores = jnp.einsum('gthf,gshf->ghts', queries, key_rows, precision=highest) * causal
    numerator = jnp.einsum('ghts,gshd->gthd', scores, values_h, precision=highest)
    numerator = numerator + jnp.einsum('gthf,ghfd->gthd', queries, states, precision=highest)
    denominator = jnp.einsum('ghts->gth', scores) + jnp.einsum('gthf,ghf->gth', queries, key_sums, precision=highest)
    states = states + jnp.einsum('gshf,gshd->ghfd', key_rows, values_h, precision=highest)
    key_sums = key_sums + lax.optimization_barrier(jnp.sum(key_rows, 1))
    return ((states, key_sums), numerator / denominator[..., None])

def grouped(array):
    shaped = array.reshape((N_DP, GROUP_BLOCKS, BLOCK) + array.shape[1:])
    return jnp.moveaxis(shaped, 1, 0)

def attention(queries, key_rows, values_h, starting, usable):
    initial = (jnp.zeros((N_DP, H, F, DH), jnp.float32), jnp.zeros((N_DP, H, F), jnp.float32))
    starts_here = starting.reshape(N_DP, GROUP_BLOCKS).T
    final_states, outputs = lax.scan(jax.checkpoint(block_step), initial, (grouped(queries), grouped(key_rows), grouped(values_h), grouped(usable), starts_here))
    return jnp.moveaxis(outputs, 0, 1).reshape(TOKENS, D)

def block_forward(rows, weights, starting, usable):
    first_gain, first_shift, qkv_weight, qkv_bias, query_map, key_map, out_weight, out_bias, second_gain, second_shift, up_weight, up_bias, down_weight, down_bias = weights
    normed = low(layer_norm(rows, first_gain, first_shift))
    projected = low(low_back(matmul(normed, qkv_weight) + qkv_bias))
    queries = projected[:, :D].reshape(-1, H, DH)
    key_rows = projected[:, D:2 * D].reshape(-1, H, DH)
    values_h = projected[:, 2 * D:].reshape(-1, H, DH)
    attended = attention(features(queries, query_map), features(key_rows, key_map), values_h, starting, usable)
    branch = low_back(matmul(low(attended), out_weight) + out_bias)
    residual = rows + branch
    normed_two = low(layer_norm(residual, second_gain, second_shift))
    hidden = low_back(matmul(normed_two, up_weight) + up_bias)
    activated = low(jax.nn.gelu(hidden, approximate=True))
    return residual + low_back(matmul(activated, down_weight) + down_bias)

def forward(inputs, weights, starting, usable):
    first_layer = tuple((weight[0] for weight in weights))
    second_layer = tuple((weight[1] for weight in weights))
    produced = []
    for micro_index in range(MICRO):
        middle = low(low_back(block_forward(inputs[micro_index], first_layer, starting[micro_index], usable[micro_index])))
        produced.append(low(block_forward(middle, second_layer, starting[micro_index], usable[micro_index])))
    return jnp.stack(produced)

def reference(ends_in, begins, filled, first_gain, first_shift, qkv_weight, qkv_bias, query_map, key_map, out_weight, out_bias, second_gain, second_shift, up_weight, up_bias, down_weight, down_bias):
    weights = tuple((weight.astype(jnp.float32) for weight in (first_gain, first_shift, qkv_weight, qkv_bias, query_map, key_map, out_weight, out_bias, second_gain, second_shift, up_weight, up_bias, down_weight, down_bias)))
    inputs = ends_in[0].astype(jnp.float32)
    cotangent = ends_in[1].astype(jnp.float32)
    starting = begins.astype(jnp.float32)
    usable = (jnp.arange(BLOCK)[None, None, :] < filled[:, :, None]).astype(jnp.float32).reshape(MICRO, TOKENS)
    outputs, backward = jax.vjp(lambda rows, params: forward(rows, params, starting, usable), inputs, weights)
    grad_inputs, grads = backward(cotangent)
    ends_out = jnp.stack([grad_inputs.astype(jnp.bfloat16), outputs.astype(jnp.bfloat16)])
    return (ends_out, grads[0], grads[1], grads[2], grads[3], grads[4], grads[5], grads[6], grads[7], grads[8], grads[9], grads[10], grads[11], grads[12], grads[13])
```

```python
import functools

import jax
import jax.numpy as jnp
from jax import lax
from jax.experimental import pallas as pl
from jax.experimental.pallas import tpu as pltpu
from jax.sharding import PartitionSpec as P

BLOCK = 64


epsilon = 1e-05
highest = lax.Precision.HIGHEST


def prefix(shard, axis, combine, identity, reverse):
    size, mine = (lax.axis_size(axis), lax.axis_index(axis))
    everything = jax.tree.map(lambda part: lax.all_gather(part, axis), shard)
    start = jax.tree.map(
        lambda part, zero: jnp.broadcast_to(jnp.asarray(zero, part.dtype), part.shape),
        shard,
        identity,
    )

    def step(k, before):
        at = size - 1 - k if reverse else k
        reached = at > mine if reverse else at < mine
        new = combine(before, jax.tree.map(lambda part: part[at], everything))
        return jax.tree.map(lambda a, b: jnp.where(reached, a, b), new, before)

    return lax.fori_loop(0, size, step, start)


def passed_along(shard, axis, by):
    size = lax.axis_size(axis)
    pairs = [(i, i + by) for i in range(size) if 0 <= i + by < size]
    return lax.ppermute(shard, axis, pairs)


def matmul(left, right):
    return jnp.dot(left, right, preferred_element_type=jnp.float32)


def times_transposed(left, right):
    return lax.dot_general(
        left, right, (((1,), (1,)), ((), ())), preferred_element_type=jnp.float32
    )


def outer_sum(left, right):
    return lax.dot_general(
        left, right, (((0,), (0,)), ((), ())), preferred_element_type=jnp.float32
    )


def layer_norm(rows, gain, shift):
    average = jnp.mean(rows, -1, keepdims=True)
    centred = rows - average
    variance = jnp.mean(centred * centred, -1, keepdims=True)
    return centred * lax.rsqrt(variance + epsilon) * gain + shift


def feature_map(logits):
    return jnp.concatenate([jax.nn.softmax(logits, -1), jax.nn.softmax(-logits, -1)], -1)


def gelu_tanh(values):
    return jax.nn.gelu(values, approximate=True)


def combine_states(earlier, later):
    kept_share = 1.0 - later[2]
    return (
        later[0] + kept_share * earlier[0],
        later[1] + kept_share * earlier[1],
        jnp.maximum(earlier[2], later[2]),
    )


def empty_like(states):
    return jax.tree.map(jnp.zeros_like, states)


def carry_forward(local):
    return prefix(local, "ctx", combine_states, empty_like(local), False)


def carry_back(local):
    return prefix(local, "ctx", combine_states, empty_like(local), True)


def block_layout(begin_row, filled_row):
    starting = begin_row.astype(jnp.float32)
    counted = jnp.cumsum(starting)
    token_segment = jnp.repeat(counted, BLOCK)
    usable = (jnp.arange(BLOCK)[None, :] < filled_row[:, None]).astype(jnp.float32).reshape(-1)
    before = (token_segment == 0.0).astype(jnp.float32)
    trailing = (token_segment == counted[-1]).astype(jnp.float32) * usable
    positions = jnp.arange(token_segment.shape[0])
    allowed = (
        (token_segment[:, None] == token_segment[None, :])
        & (positions[None, :] <= positions[:, None])
    ).astype(jnp.float32)
    restart = jnp.max(starting)
    return (before, trailing, usable, allowed, restart)


def split_heads(projected, head_size):
    token_count = projected.shape[0]
    head_count = projected.shape[1] // (3 * head_size)
    return projected.reshape(token_count, 3, head_count, head_size)


def front_half(rows, weights):
    normed = layer_norm(
        rows, weights[0].astype(jnp.float32), weights[1].astype(jnp.float32)
    ).astype(jnp.bfloat16)
    projected = (matmul(normed, weights[2]) + weights[3].astype(jnp.float32)).astype(jnp.bfloat16)
    head_size = weights[4].shape[0]
    split = split_heads(projected, head_size)
    head_count = split.shape[2]
    query_logits = jnp.einsum(
        "thi,ihj->thj",
        split[:, 0],
        weights[4].reshape(head_size, head_count, head_size),
        preferred_element_type=jnp.float32,
    )
    key_logits = jnp.einsum(
        "thi,ihj->thj",
        split[:, 1],
        weights[5].reshape(head_size, head_count, head_size),
        preferred_element_type=jnp.float32,
    )
    query_phi = feature_map(query_logits).astype(jnp.bfloat16)
    key_phi = feature_map(key_logits).astype(jnp.bfloat16)
    return (normed, projected, query_logits, key_logits, query_phi, key_phi)


def local_state(key_phi, projected, geometry):
    values_h = split_heads(projected, key_phi.shape[2] // 2)[:, 2]
    weighted = key_phi * geometry[1][:, None, None].astype(jnp.bfloat16)
    states = jnp.einsum("shf,shd->hfd", weighted, values_h, preferred_element_type=jnp.float32)
    key_sums = jnp.sum(weighted.astype(jnp.float32), 0)
    return (states, key_sums, geometry[4])


def back_half(rows, weights, geometry, front, carried):
    normed, projected, query_logits, key_logits, query_phi, key_phi = front
    before, trailing, usable, allowed, restart = geometry
    values_h = split_heads(projected, key_phi.shape[2] // 2)[:, 2]
    key_rows = key_phi * usable[:, None, None].astype(jnp.bfloat16)
    scores = (
        jnp.einsum("thf,shf->hts", query_phi, key_rows, preferred_element_type=jnp.float32)
        * allowed[None]
    )
    value_wide = values_h.astype(jnp.float32)
    query_wide = query_phi.astype(jnp.float32)
    numerator = jnp.einsum("hts,shd->thd", scores, value_wide, precision=highest)
    numerator = numerator + before[:, None, None] * jnp.einsum(
        "thf,hfd->thd", query_wide, carried[0], precision=highest
    )
    denominator = jnp.einsum("hts->th", scores) + before[:, None] * jnp.einsum(
        "thf,hf->th", query_wide, carried[1], precision=highest
    )
    attended = (numerator / denominator[..., None]).reshape(rows.shape[0], -1).astype(jnp.bfloat16)
    residual = rows + matmul(attended, weights[6]) + weights[7].astype(jnp.float32)
    normed_two = layer_norm(
        residual, weights[8].astype(jnp.float32), weights[9].astype(jnp.float32)
    ).astype(jnp.bfloat16)
    hidden = matmul(normed_two, weights[10]) + weights[11].astype(jnp.float32)
    activated = gelu_tanh(hidden).astype(jnp.bfloat16)
    output = residual + matmul(activated, weights[12]) + weights[13].astype(jnp.float32)
    saved = (
        attended,
        residual,
        normed_two,
        hidden,
        activated,
        key_rows,
        scores,
        numerator,
        denominator,
        values_h,
    )
    return (output, saved)


def block_backward(rows, weights, geometry, carried, grad_out):
    front = front_half(rows, weights)
    normed, projected, query_logits, key_logits, query_phi, key_phi = front
    output, saved = back_half(rows, weights, geometry, front, carried)
    (
        attended,
        residual,
        normed_two,
        hidden,
        activated,
        key_rows,
        scores,
        numerator,
        denominator,
        values_h,
    ) = saved
    before, trailing, usable, allowed, restart = geometry
    grad_down = grad_out.astype(jnp.bfloat16)
    down_w_grad = (activated, grad_down)
    down_b_grad = jnp.sum(grad_down.astype(jnp.float32), 0)
    grad_active = times_transposed(grad_down, weights[12])
    grad_hidden = jax.vjp(gelu_tanh, hidden)[1](grad_active)[0].astype(jnp.bfloat16)
    up_w_grad = (normed_two, grad_hidden)
    up_b_grad = jnp.sum(grad_hidden.astype(jnp.float32), 0)
    grad_normed_two = times_transposed(grad_hidden, weights[10])
    second_back = jax.vjp(
        layer_norm, residual, weights[8].astype(jnp.float32), weights[9].astype(jnp.float32)
    )[1](grad_normed_two)
    grad_residual = grad_out + second_back[0]
    grad_branch = grad_residual.astype(jnp.bfloat16)
    out_w_grad = (attended, grad_branch)
    out_b_grad = jnp.sum(grad_branch.astype(jnp.float32), 0)
    head_size = weights[4].shape[0]
    grad_attended = times_transposed(grad_branch, weights[6]).reshape(rows.shape[0], -1, head_size)
    attended_wide = numerator / denominator[..., None]
    grad_numer = grad_attended / denominator[..., None]
    grad_denom = -jnp.sum(grad_attended * attended_wide, -1) / denominator
    query_wide = query_phi.astype(jnp.float32)
    key_wide = key_rows.astype(jnp.float32)
    value_wide = values_h.astype(jnp.float32)
    query_before = query_wide * before[:, None, None]
    local_grads = (
        jnp.einsum("thf,thd->hfd", query_before, grad_numer, precision=highest),
        jnp.einsum("thf,th->hf", query_before, grad_denom, precision=highest),
        restart,
    )
    grad_carried = carry_back(local_grads)
    grad_scores = (
        jnp.einsum("thd,shd->hts", grad_numer, value_wide, precision=highest)
        + grad_denom.T[:, :, None]
    ) * allowed[None]
    weighted = key_phi.astype(jnp.float32) * trailing[:, None, None]
    grad_query_phi = jnp.einsum("hts,shf->thf", grad_scores, key_wide, precision=highest)
    grad_query_phi = grad_query_phi + before[:, None, None] * (
        jnp.einsum("thd,hfd->thf", grad_numer, carried[0], precision=highest)
        + grad_denom[:, :, None] * carried[1][None]
    )
    grad_key_phi = (
        jnp.einsum("hts,thf->shf", grad_scores, query_wide, precision=highest)
        * usable[:, None, None]
    )
    grad_key_phi = grad_key_phi + trailing[:, None, None] * (
        jnp.einsum("shd,hfd->shf", value_wide, grad_carried[0], precision=highest)
        + grad_carried[1][None]
    )
    grad_values = jnp.einsum("hts,thd->shd", scores, grad_numer, precision=highest) + jnp.einsum(
        "shf,hfd->shd", weighted, grad_carried[0], precision=highest
    )
    grad_query_logits = jax.vjp(feature_map, query_logits)[1](grad_query_phi)[0].astype(
        jnp.bfloat16
    )
    grad_key_logits = jax.vjp(feature_map, key_logits)[1](grad_key_phi)[0].astype(jnp.bfloat16)
    split = split_heads(projected, head_size)
    head_count = split.shape[2]
    query_table = weights[4].reshape(head_size, head_count, head_size)
    key_table = weights[5].reshape(head_size, head_count, head_size)
    grad_queries = jnp.einsum(
        "thj,ihj->thi", grad_query_logits, query_table, preferred_element_type=jnp.float32
    )
    grad_keys = jnp.einsum(
        "thj,ihj->thi", grad_key_logits, key_table, preferred_element_type=jnp.float32
    )
    query_map_grad = jnp.einsum(
        "thi,thj->ihj", split[:, 0], grad_query_logits, preferred_element_type=jnp.float32
    ).reshape(head_size, -1)
    key_map_grad = jnp.einsum(
        "thi,thj->ihj", split[:, 1], grad_key_logits, preferred_element_type=jnp.float32
    ).reshape(head_size, -1)
    grad_projected = (
        jnp.stack([grad_queries, grad_keys, grad_values], 1)
        .reshape(rows.shape[0], -1)
        .astype(jnp.bfloat16)
    )
    qkv_w_grad = (normed, grad_projected)
    qkv_b_grad = jnp.sum(grad_projected.astype(jnp.float32), 0)
    grad_normed = times_transposed(grad_projected, weights[2])
    first_back = jax.vjp(
        layer_norm, rows, weights[0].astype(jnp.float32), weights[1].astype(jnp.float32)
    )[1](grad_normed)
    grad_rows = grad_residual + first_back[0]
    grads = (
        first_back[1],
        first_back[2],
        qkv_w_grad,
        qkv_b_grad,
        query_map_grad,
        key_map_grad,
        out_w_grad,
        out_b_grad,
        second_back[1],
        second_back[2],
        up_w_grad,
        up_b_grad,
        down_w_grad,
        down_b_grad,
    )
    return (grad_rows, grads)


MESH = pl.DeviceIdType.MESH
WIDE = 768
HALF = 384


def bit_length(size):
    return (size - 1).bit_length()


def bit_orders(ctx_size, dp_size):
    ctx_bits = [("ctx", k) for k in range(bit_length(ctx_size))]
    dp_bits = [("dp", k) for k in range(bit_length(dp_size))]

    def interleaved(first, second):
        order = []
        for k in range(max(len(first), len(second))):
            order += first[k : k + 1] + second[k : k + 1]
        return order

    return (interleaved(ctx_bits, dp_bits), interleaved(ctx_bits[::-1], dp_bits))


def halvings(rows, count):
    sizes, halved = [rows], []
    for _ in range(count):
        halved.append(sizes[-1] % 32 == 0)
        sizes.append(sizes[-1] // 2 if halved[-1] else sizes[-1])
    return sizes, halved


class Reduction:
    def __init__(self, rows, orders):
        self.rows, self.orders = rows, orders
        self.count = len(orders[0])
        self.sizes, self.halved = halvings(rows, self.count)
        self.steps = [("rs", s) for s in range(self.count)]
        self.steps += [("ag", s) for s in reversed(range(self.count)) if self.halved[s]]
        self.offsets, self.bits = [], []
        for order in orders:
            offset, offsets, bits = 0, [0], []
            for s, (axis, k) in enumerate(order):
                bit = (lax.axis_index(axis) // (1 << k)) % 2
                bits.append(bit)
                if self.halved[s]:
                    offset = offset + bit * self.sizes[s + 1]
                offsets.append(offset)
            self.offsets.append(offsets)
            self.bits.append(bits)

    def partner(self, part, s):
        axis, k = self.orders[part][s]
        return {axis: lax.axis_index(axis) + (1 << k) * (1 - 2 * self.bits[part][s])}

    def rows_at(self, offset, size):
        if isinstance(offset, int):
            return pl.ds(offset, size)
        return pl.ds(pl.multiple_of(offset, 16), size)

    def copy(self, buffer, whole, received, sems, part, step):
        kind, s = self.steps[step]
        columns = pl.ds(part * HALF, HALF)
        size = self.sizes[s + 1]
        if kind == "rs":
            offset = self.offsets[part][s]
            if self.halved[s]:
                offset = offset + (1 - self.bits[part][s]) * size
            source = buffer.at[self.rows_at(offset, size), columns]
            target = received[s]
        else:
            source = whole.at[self.rows_at(self.offsets[part][s + 1], size), columns]
            target = source
        return pltpu.make_async_remote_copy(
            src_ref=source,
            dst_ref=target,
            send_sem=sems[0],
            recv_sem=sems[1],
            device_id=self.partner(part, s),
            device_id_type=MESH,
        )

    def add(self, buffer, whole, received, part, step):
        kind, s = self.steps[step]
        if kind == "rs":
            size = self.sizes[s + 1]
            rows = self.rows_at(self.offsets[part][s + 1], size)
            columns = pl.ds(part * HALF, HALF)
            total = buffer[rows, columns].astype(jnp.float32) + received[s][...].astype(jnp.float32)
            target = whole if s + 1 == self.count else buffer
            target[rows, columns] = total.astype(jnp.bfloat16)


def reduce_kernel(
    orders, chunks, x_ref, small_ref, qkv_out, out_out, up_out, down_out, small_out, *scratch
):
    count = len(orders[0])
    big, big_whole, little, little_whole = scratch[:4]
    scratch = scratch[4:]
    big_recv, little_recv = scratch[:count], scratch[count : 2 * count]
    left, right, wide, send, recv, send_small, recv_small, load, store = scratch[2 * count :]
    large, small = Reduction(WIDE, orders), Reduction(little.shape[0], orders)
    steps = len(large.steps)

    barrier = pltpu.get_barrier_semaphore()
    for s in range(count):
        pl.semaphore_signal(barrier, inc=1, device_id=large.partner(0, s), device_id_type=MESH)
    pl.semaphore_wait(barrier, count)

    def operands(c):
        left_at = jnp.where(c < 4, c, jnp.where(c < 8, 4, jnp.where(c == 8, 5, 6)))
        right_at = jnp.where(c < 4, 7, c + 4)
        slot = c % 2
        return (
            pltpu.make_async_copy(x_ref.at[left_at], left.at[slot], load.at[slot, 0]),
            pltpu.make_async_copy(x_ref.at[right_at], right.at[slot], load.at[slot, 1]),
        )

    def result(c, kind):
        slot = c % 2
        source, sem = wide.at[slot], store.at[slot]
        if kind == "down":
            target = down_out.at[pl.ds(pl.multiple_of(c * WIDE, WIDE), WIDE), :]
        elif kind == "up":
            target = up_out.at[:, pl.ds(pl.multiple_of((c - 4) * WIDE, WIDE), WIDE)]
        elif kind == "out":
            target = out_out
        else:
            target = qkv_out.at[:, pl.ds(pl.multiple_of((c - 9) * WIDE, WIDE), WIDE)]
        return pltpu.make_async_copy(source, target, sem)

    def for_each_kind(c, action):
        for kind, low, high in (("down", 0, 4), ("up", 4, 8), ("out", 8, 9), ("qkv", 9, 12)):
            @pl.when((c >= low) & (c < high))
            def _():
                action(result(c, kind))

    def big_copy(c, part, step):
        received = [r.at[c, part] for r in big_recv]
        sems = (send.at[c, part, step], recv.at[c, part, step])
        return large.copy(big.at[c], big_whole.at[c], received, sems, part, step)

    def small_copy(part, step):
        received = [r.at[part] for r in little_recv]
        sems = (send_small.at[part, step], recv_small.at[part, step])
        return small.copy(little, little_whole, received, sems, part, step)

    for copy in operands(0):
        copy.start()
    little[...] = small_ref[...].astype(jnp.bfloat16)
    for part in range(2):
        small_copy(part, 0).start()

    def tick(t, carry):
        @pl.when(t < chunks)
        def _():
            for copy in operands(t):
                copy.wait()

            @pl.when(t + 1 < chunks)
            def _():
                for copy in operands(t + 1):
                    copy.start()

            slot = t % 2
            big[t] = lax.dot_general(
                left[slot],
                right[slot],
                (((0,), (0,)), ((), ())),
                preferred_element_type=jnp.float32,
            ).astype(jnp.bfloat16)
            for part in range(2):
                big_copy(t, part, 0).start()

        for step in range(steps):
            c = t - 1 - step

            @pl.when((c >= 0) & (c < chunks))
            def _():
                for part in range(2):
                    big_copy(c, part, step).wait()
                    received = [r.at[c, part] for r in big_recv]
                    large.add(big.at[c], big_whole.at[c], received, part, step)
                    if step + 1 < steps:
                        big_copy(c, part, step + 1).start()
                if step + 1 == steps:
                    @pl.when(c >= 2)
                    def _():
                        for_each_kind(c - 2, lambda copy: copy.wait())

                    wide[c % 2] = big_whole[c].astype(jnp.float32)
                    for_each_kind(c, lambda copy: copy.start())

            if step < len(small.steps):
                @pl.when(t == step)
                def _():
                    for part in range(2):
                        small_copy(part, step).wait()
                        received = [r.at[part] for r in little_recv]
                        small.add(little, little_whole, received, part, step)
                        if step + 1 < len(small.steps):
                            small_copy(part, step + 1).start()

        return carry

    lax.fori_loop(0, chunks + steps, tick, 0)
    for c in (chunks - 2, chunks - 1):
        result(c, "qkv").wait()
    small_out[...] = little_whole[...].astype(jnp.float32)


def reduced(x, small, mesh):
    orders = bit_orders(mesh.shape["ctx"], mesh.shape["dp"])
    count, chunks, tokens = len(orders[0]), 12, x.shape[1]
    sizes, _ = halvings(WIDE, count)
    small_rows = small.shape[0]
    small_sizes, small_halved = halvings(small_rows, count)
    steps = count + sum(halvings(WIDE, count)[1])
    small_steps = count + sum(small_halved)
    any_space = pl.BlockSpec(memory_space=pl.ANY)
    in_vmem = pl.BlockSpec(memory_space=pltpu.VMEM)
    f32, bf16 = jnp.float32, jnp.bfloat16
    return pl.pallas_call(
        functools.partial(reduce_kernel, orders, chunks),
        out_shape=(
            jax.ShapeDtypeStruct((WIDE, 3 * WIDE), f32),
            jax.ShapeDtypeStruct((WIDE, WIDE), f32),
            jax.ShapeDtypeStruct((WIDE, 4 * WIDE), f32),
            jax.ShapeDtypeStruct((4 * WIDE, WIDE), f32),
            jax.ShapeDtypeStruct((small_rows, WIDE), f32),
        ),
        in_specs=[any_space, in_vmem],
        out_specs=(any_space,) * 4 + (in_vmem,),
        scratch_shapes=[
            pltpu.VMEM((chunks, WIDE, WIDE), bf16),
            pltpu.VMEM((chunks, WIDE, WIDE), bf16),
            pltpu.VMEM((small_rows, WIDE), bf16),
            pltpu.VMEM((small_rows, WIDE), bf16),
            *(pltpu.VMEM((chunks, 2, size, HALF), bf16) for size in sizes[1:]),
            *(pltpu.VMEM((2, size, HALF), bf16) for size in small_sizes[1:]),
            pltpu.VMEM((2, tokens, WIDE), bf16),
            pltpu.VMEM((2, tokens, WIDE), bf16),
            pltpu.VMEM((2, WIDE, WIDE), f32),
            pltpu.SemaphoreType.DMA((chunks, 2, steps)),
            pltpu.SemaphoreType.DMA((chunks, 2, steps)),
            pltpu.SemaphoreType.DMA((2, small_steps)),
            pltpu.SemaphoreType.DMA((2, small_steps)),
            pltpu.SemaphoreType.DMA((2, 2)),
            pltpu.SemaphoreType.DMA((2,)),
        ],
        compiler_params=pltpu.CompilerParams(
            collective_id=0, has_side_effects=True, vmem_limit_bytes=60 * 1024 * 1024
        ),
    )(x, small)


def select_section(first_section, early, late):
    return jax.tree.map(
        lambda early_leaf, late_leaf: jnp.where(first_section, early_leaf, late_leaf), early, late
    )


def sum_up(collected, mesh):
    wide = {}
    for index in (2, 6, 10, 12):
        for side in (0, 1):
            rows = jnp.concatenate([grads[index][side] for grads in collected])
            wide[index, side] = [rows[:, k : k + WIDE] for k in range(0, rows.shape[1], WIDE)]
    x = jnp.stack(
        wide[12, 0] + wide[10, 0] + wide[6, 0] + wide[2, 0]
        + wide[12, 1] + wide[10, 1] + wide[6, 1] + wide[2, 1]
    )
    narrow = (0, 1, 3, 4, 5, 7, 8, 9, 11, 13)
    parts = [sum(grads[index] for grads in collected) for index in narrow]
    flat = jnp.concatenate([part.reshape(-1, WIDE) for part in parts])
    small = jnp.pad(flat, ((0, 256 - flat.shape[0]), (0, 0)))
    qkv_grad, out_grad, up_grad, down_grad, small = reduced(x, small, mesh)
    totals, at = {2: qkv_grad, 6: out_grad, 10: up_grad, 12: down_grad}, 0
    for index, part in zip(narrow, parts):
        count = part.size // WIDE
        totals[index] = small[at : at + count].reshape(part.shape)
        at += count
    return tuple(totals[index] for index in range(14))


def body(
    mesh,
    ends_in,
    begins,
    filled,
    first_gain,
    first_shift,
    qkv_weight,
    qkv_bias,
    query_map,
    key_map,
    out_weight,
    out_bias,
    second_gain,
    second_shift,
    up_weight,
    up_bias,
    down_weight,
    down_bias,
):
    weights = tuple(
        (
            weight[0]
            for weight in (
                first_gain,
                first_shift,
                qkv_weight,
                qkv_bias,
                query_map,
                key_map,
                out_weight,
                out_bias,
                second_gain,
                second_shift,
                up_weight,
                up_bias,
                down_weight,
                down_bias,
            )
        )
    )
    first_section = lax.axis_index("section") == 0
    local_rows = ends_in[0]
    micro_count = local_rows.shape[0]
    layouts = [
        block_layout(begins[micro_index], filled[micro_index]) for micro_index in range(micro_count)
    ]
    received = jnp.zeros_like(local_rows[0])
    kept_rows, kept_states, produced = ([], [], [])
    for position in range(micro_count + 1):
        geometry = select_section(
            first_section, layouts[min(position, micro_count - 1)], layouts[max(position - 1, 0)]
        )
        current = jnp.where(first_section, local_rows[min(position, micro_count - 1)], received)
        rows = current.astype(jnp.float32)
        front = front_half(rows, weights)
        carried = carry_forward(local_state(front[5], front[1], geometry))
        output = back_half(rows, weights, geometry, front, carried)[0].astype(jnp.bfloat16)
        kept_rows.append(current)
        kept_states.append(carried)
        produced.append(output)
        if position < micro_count:
            received = passed_along(output, "section", 1)
    incoming = jnp.zeros(local_rows.shape[1:], jnp.float32)
    collected = []
    back_rows = []
    for position in range(micro_count + 1):
        early = max(position - 1, 0)
        late = min(position + 1, micro_count)
        rows = select_section(first_section, kept_rows[early], kept_rows[late]).astype(jnp.float32)
        carried = select_section(first_section, kept_states[early], kept_states[late])
        geometry = select_section(
            first_section,
            layouts[min(early, micro_count - 1)],
            layouts[min(position, micro_count - 1)],
        )
        own_grad = local_rows[min(position, micro_count - 1)].astype(jnp.float32) * float(
            position < micro_count
        )
        grad_out = jnp.where(first_section, incoming, own_grad)
        grad_rows, grads = block_backward(rows, weights, geometry, carried, grad_out)
        back_rows.append(grad_rows.astype(jnp.bfloat16))
        collected.append(grads)
        if position < micro_count:
            incoming = passed_along(back_rows[-1], "section", -1).astype(jnp.float32)
    totals = sum_up(collected, mesh)
    ends_out = jnp.where(first_section, jnp.stack(back_rows[1:]), jnp.stack(produced[1:]))[None]
    return (ends_out,) + tuple((total[None] for total in totals))


def solution(mesh):
    placed = (
        P("section", None, ("dp", "ctx"), None),
        P(None, ("dp", "ctx")),
        P(None, ("dp", "ctx")),
        P("section", None),
        P("section", None),
        P("section", None, None),
        P("section", None),
        P("section", None, None),
        P("section", None, None),
        P("section", None, None),
        P("section", None),
        P("section", None),
        P("section", None),
        P("section", None, None),
        P("section", None),
        P("section", None, None),
        P("section", None),
    )
    return jax.shard_map(
        functools.partial(body, mesh),
        mesh=mesh,
        in_specs=placed,
        out_specs=(
            P("section", None, ("dp", "ctx"), None),
            P("section", None),
            P("section", None),
            P("section", None, None),
            P("section", None),
            P("section", None, None),
            P("section", None, None),
            P("section", None, None),
            P("section", None),
            P("section", None),
            P("section", None),
            P("section", None, None),
            P("section", None),
            P("section", None, None),
            P("section", None),
        ),
        check_vma=False,
    )
```

```python
import functools

import jax
import jax.numpy as jnp
from jax import lax
from jax.experimental import pallas as pl
from jax.experimental.pallas import tpu as pltpu
from jax.sharding import PartitionSpec as P

BLOCK = 64
ROWS = 128
HEADS = 12
PAIRS = 6
EPSILON = 1e-05
F32, BF16 = jnp.float32, jnp.bfloat16

MESH = pl.DeviceIdType.MESH
WIDE = 768
HALF = 384


def bit_length(size):
    return (size - 1).bit_length()


def bit_orders(ctx_size, dp_size):
    ctx_bits = [("ctx", k) for k in range(bit_length(ctx_size))]
    dp_bits = [("dp", k) for k in range(bit_length(dp_size))]

    def interleaved(first, second):
        order = []
        for k in range(max(len(first), len(second))):
            order += first[k : k + 1] + second[k : k + 1]
        return order

    return (interleaved(ctx_bits, dp_bits), interleaved(ctx_bits[::-1], dp_bits))


def halvings(rows, count):
    sizes, halved = [rows], []
    for _ in range(count):
        halved.append(sizes[-1] % 32 == 0)
        sizes.append(sizes[-1] // 2 if halved[-1] else sizes[-1])
    return sizes, halved


class Reduction:
    def __init__(self, rows, orders):
        self.rows, self.orders = rows, orders
        self.count = len(orders[0])
        self.sizes, self.halved = halvings(rows, self.count)
        self.steps = [("rs", s) for s in range(self.count)]
        self.steps += [("ag", s) for s in reversed(range(self.count)) if self.halved[s]]
        self.offsets, self.bits = [], []
        for order in orders:
            offset, offsets, bits = 0, [0], []
            for s, (axis, k) in enumerate(order):
                bit = (lax.axis_index(axis) // (1 << k)) % 2
                bits.append(bit)
                if self.halved[s]:
                    offset = offset + bit * self.sizes[s + 1]
                offsets.append(offset)
            self.offsets.append(offsets)
            self.bits.append(bits)

    def partner(self, part, s):
        axis, k = self.orders[part][s]
        return {axis: lax.axis_index(axis) + (1 << k) * (1 - 2 * self.bits[part][s])}

    def rows_at(self, offset, size):
        if isinstance(offset, int):
            return pl.ds(offset, size)
        return pl.ds(pl.multiple_of(offset, 16), size)

    def copy(self, buffer, whole, received, sems, part, step):
        kind, s = self.steps[step]
        columns = pl.ds(part * HALF, HALF)
        size = self.sizes[s + 1]
        if kind == "rs":
            offset = self.offsets[part][s]
            if self.halved[s]:
                offset = offset + (1 - self.bits[part][s]) * size
            source = buffer.at[self.rows_at(offset, size), columns]
            target = received[s]
        else:
            source = whole.at[self.rows_at(self.offsets[part][s + 1], size), columns]
            target = source
        return pltpu.make_async_remote_copy(
            src_ref=source,
            dst_ref=target,
            send_sem=sems[0],
            recv_sem=sems[1],
            device_id=self.partner(part, s),
            device_id_type=MESH,
        )

    def add(self, buffer, whole, received, part, step):
        kind, s = self.steps[step]
        if kind == "rs":
            size = self.sizes[s + 1]
            rows = self.rows_at(self.offsets[part][s + 1], size)
            columns = pl.ds(part * HALF, HALF)
            total = buffer[rows, columns].astype(jnp.float32) + received[s][...].astype(jnp.float32)
            target = whole if s + 1 == self.count else buffer
            target[rows, columns] = total.astype(jnp.bfloat16)


def reduce_kernel(
    orders, chunks, x_ref, small_ref, qkv_out, out_out, up_out, down_out, small_out, *scratch
):
    count = len(orders[0])
    big, big_whole, little, little_whole = scratch[:4]
    scratch = scratch[4:]
    big_recv, little_recv = scratch[:count], scratch[count : 2 * count]
    left, right, wide, send, recv, send_small, recv_small, load, store = scratch[2 * count :]
    large, small = Reduction(WIDE, orders), Reduction(little.shape[0], orders)
    steps = len(large.steps)

    barrier = pltpu.get_barrier_semaphore()
    for s in range(count):
        pl.semaphore_signal(barrier, inc=1, device_id=large.partner(0, s), device_id_type=MESH)
    pl.semaphore_wait(barrier, count)

    def operands(c):
        left_at = jnp.where(c < 4, c, jnp.where(c < 8, 4, jnp.where(c == 8, 5, 6)))
        right_at = jnp.where(c < 4, 7, c + 4)
        slot = c % 2
        return (
            pltpu.make_async_copy(x_ref.at[left_at], left.at[slot], load.at[slot, 0]),
            pltpu.make_async_copy(x_ref.at[right_at], right.at[slot], load.at[slot, 1]),
        )

    def result(c, kind):
        slot = c % 2
        source, sem = wide.at[slot], store.at[slot]
        if kind == "down":
            target = down_out.at[pl.ds(pl.multiple_of(c * WIDE, WIDE), WIDE), :]
        elif kind == "up":
            target = up_out.at[:, pl.ds(pl.multiple_of((c - 4) * WIDE, WIDE), WIDE)]
        elif kind == "out":
            target = out_out
        else:
            target = qkv_out.at[:, pl.ds(pl.multiple_of((c - 9) * WIDE, WIDE), WIDE)]
        return pltpu.make_async_copy(source, target, sem)

    def for_each_kind(c, action):
        for kind, low, high in (("down", 0, 4), ("up", 4, 8), ("out", 8, 9), ("qkv", 9, 12)):
            @pl.when((c >= low) & (c < high))
            def _():
                action(result(c, kind))

    def big_copy(c, part, step):
        received = [r.at[c, part] for r in big_recv]
        sems = (send.at[c, part, step], recv.at[c, part, step])
        return large.copy(big.at[c], big_whole.at[c], received, sems, part, step)

    def small_copy(part, step):
        received = [r.at[part] for r in little_recv]
        sems = (send_small.at[part, step], recv_small.at[part, step])
        return small.copy(little, little_whole, received, sems, part, step)

    for copy in operands(0):
        copy.start()
    little[...] = small_ref[...].astype(jnp.bfloat16)
    for part in range(2):
        small_copy(part, 0).start()

    def tick(t, carry):
        @pl.when(t < chunks)
        def _():
            for copy in operands(t):
                copy.wait()

            @pl.when(t + 1 < chunks)
            def _():
                for copy in operands(t + 1):
                    copy.start()

            slot = t % 2
            big[t] = lax.dot_general(
                left[slot],
                right[slot],
                (((0,), (0,)), ((), ())),
                preferred_element_type=jnp.float32,
            ).astype(jnp.bfloat16)
            for part in range(2):
                big_copy(t, part, 0).start()

        for step in range(steps):
            c = t - 1 - step

            @pl.when((c >= 0) & (c < chunks))
            def _():
                for part in range(2):
                    big_copy(c, part, step).wait()
                    received = [r.at[c, part] for r in big_recv]
                    large.add(big.at[c], big_whole.at[c], received, part, step)
                    if step + 1 < steps:
                        big_copy(c, part, step + 1).start()
                if step + 1 == steps:
                    @pl.when(c >= 2)
                    def _():
                        for_each_kind(c - 2, lambda copy: copy.wait())

                    wide[c % 2] = big_whole[c].astype(jnp.float32)
                    for_each_kind(c, lambda copy: copy.start())

            if step < len(small.steps):
                @pl.when(t == step)
                def _():
                    for part in range(2):
                        small_copy(part, step).wait()
                        received = [r.at[part] for r in little_recv]
                        small.add(little, little_whole, received, part, step)
                        if step + 1 < len(small.steps):
                            small_copy(part, step + 1).start()

        return carry

    lax.fori_loop(0, chunks + steps, tick, 0)
    for c in (chunks - 2, chunks - 1):
        result(c, "qkv").wait()
    small_out[...] = little_whole[...].astype(jnp.float32)


def reduced(x, small, mesh):
    orders = bit_orders(mesh.shape["ctx"], mesh.shape["dp"])
    count, chunks, tokens = len(orders[0]), 12, x.shape[1]
    sizes, _ = halvings(WIDE, count)
    small_rows = small.shape[0]
    small_sizes, small_halved = halvings(small_rows, count)
    steps = count + sum(halvings(WIDE, count)[1])
    small_steps = count + sum(small_halved)
    any_space = pl.BlockSpec(memory_space=pl.ANY)
    in_vmem = pl.BlockSpec(memory_space=pltpu.VMEM)
    f32, bf16 = jnp.float32, jnp.bfloat16
    return pl.pallas_call(
        functools.partial(reduce_kernel, orders, chunks),
        out_shape=(
            jax.ShapeDtypeStruct((WIDE, 3 * WIDE), f32),
            jax.ShapeDtypeStruct((WIDE, WIDE), f32),
            jax.ShapeDtypeStruct((WIDE, 4 * WIDE), f32),
            jax.ShapeDtypeStruct((4 * WIDE, WIDE), f32),
            jax.ShapeDtypeStruct((small_rows, WIDE), f32),
        ),
        in_specs=[any_space, in_vmem],
        out_specs=(any_space,) * 4 + (in_vmem,),
        scratch_shapes=[
            pltpu.VMEM((chunks, WIDE, WIDE), bf16),
            pltpu.VMEM((chunks, WIDE, WIDE), bf16),
            pltpu.VMEM((small_rows, WIDE), bf16),
            pltpu.VMEM((small_rows, WIDE), bf16),
            *(pltpu.VMEM((chunks, 2, size, HALF), bf16) for size in sizes[1:]),
            *(pltpu.VMEM((2, size, HALF), bf16) for size in small_sizes[1:]),
            pltpu.VMEM((2, tokens, WIDE), bf16),
            pltpu.VMEM((2, tokens, WIDE), bf16),
            pltpu.VMEM((2, WIDE, WIDE), f32),
            pltpu.SemaphoreType.DMA((chunks, 2, steps)),
            pltpu.SemaphoreType.DMA((chunks, 2, steps)),
            pltpu.SemaphoreType.DMA((2, small_steps)),
            pltpu.SemaphoreType.DMA((2, small_steps)),
            pltpu.SemaphoreType.DMA((2, 2)),
            pltpu.SemaphoreType.DMA((2,)),
        ],
        compiler_params=pltpu.CompilerParams(
            collective_id=0, has_side_effects=True, vmem_limit_bytes=60 * 1024 * 1024
        ),
    )(x, small)


def dot_nn(left, right):
    return jnp.dot(left, right, preferred_element_type=F32)


def dot_nt(left, right):
    return lax.dot_general(left, right, (((1,), (1,)), ((), ())), preferred_element_type=F32)


def dot_tn(left, right):
    return lax.dot_general(left, right, (((0,), (0,)), ((), ())), preferred_element_type=F32)


def high_low(values):
    high = values.astype(BF16)
    return high, (values - high.astype(F32)).astype(BF16)


def tile(index, size):
    return pl.ds(pl.multiple_of(index * size, size), size)


def loop(count, step, unroll=1):
    def body(k, carry):
        step(k)
        return carry

    lax.fori_loop(0, count, body, 0, unroll=unroll)


def low_lanes(rows):
    return lax.broadcasted_iota(jnp.int32, (rows, 128), 1) < 64


def normalised(rows):
    average = jnp.mean(rows, -1, keepdims=True)
    centred = rows - average
    scale = lax.rsqrt(jnp.mean(centred * centred, -1, keepdims=True) + EPSILON)
    return centred * scale, scale


def norm_input_grad(grad, standard, scale, gain):
    wide = grad * gain
    first = jnp.mean(wide, -1, keepdims=True)
    second = jnp.mean(wide * standard, -1, keepdims=True)
    return scale * (wide - first - standard * second)


def half_sums(values, low):
    first = jnp.sum(jnp.where(low, values, 0.0), -1, keepdims=True)
    second = jnp.sum(jnp.where(low, 0.0, values), -1, keepdims=True)
    return jnp.where(low, first, second)


def half_softmax(logits, low, ones):
    lowest = jnp.float32(-3e38)
    first = jnp.max(jnp.where(low, logits, lowest), -1, keepdims=True)
    second = jnp.max(jnp.where(low, lowest, logits), -1, keepdims=True)
    powers = jnp.exp(logits - jnp.where(low, first, second))
    high, rest = high_low(powers)
    return powers / dot_nn(jnp.concatenate([high, rest], 1), jnp.concatenate([ones, ones], 0))


def layers_kernel(ctx_size, *refs):
    (
        x_in, meta, first_gain, first_shift, qkv_w, qkv_b, map_q, map_k, pair_q, pair_k,
        out_w, out_b, second_gain, second_shift, up_w, up_b, down_w, down_b,
        x_out, ends, small,
        rows, grad_in, normed, proj, phi_q, phi_k, att, att_wide, den, res, act, slope,
        states, back_state, back_in, back_out, grad_wide, branch,
        ones, mask, mask_t, bef, trail, x_sem, in_sem, out_sem, remote,
    ) = refs
    section, me = lax.axis_index("section"), lax.axis_index("ctx")
    has_before = (6 * me) % ctx_size != 0
    has_after = (6 * (me + 1)) % ctx_size != 0
    reach = (6 * me + 5) % ctx_size
    shift = jnp.where(reach <= 5, 5 - reach, 0)
    other = {"section": 1 - section}

    def remote_copy(source, target, index, device):
        return pltpu.make_async_remote_copy(
            src_ref=source,
            dst_ref=target,
            send_sem=remote.at[index, 0],
            recv_sem=remote.at[index, 1],
            device_id=device,
            device_id_type=MESH,
        )

    forward_rows = remote_copy(branch, rows, 0, other)
    backward_rows = remote_copy(rows, grad_in, 1, other)
    state_on = remote_copy(states.at[6], states.at[0], 2, {"ctx": me + 1})
    state_back = remote_copy(back_out, back_in, 3, {"ctx": me - 1})

    barrier = pltpu.get_barrier_semaphore()
    pl.semaphore_signal(barrier, inc=1, device_id=other, device_id_type=MESH)

    @pl.when(has_before)
    def _():
        pl.semaphore_signal(barrier, inc=1, device_id={"ctx": me - 1}, device_id_type=MESH)

    @pl.when(has_after)
    def _():
        pl.semaphore_signal(barrier, inc=1, device_id={"ctx": me + 1}, device_id_type=MESH)

    pl.semaphore_wait(barrier, 1 + has_before.astype(jnp.int32) + has_after.astype(jnp.int32))

    @pl.when(section == 0)
    def _():
        copy = pltpu.make_async_copy(x_in, rows, in_sem)
        copy.start()
        copy.wait()

    @pl.when(section == 1)
    def _():
        copy = pltpu.make_async_copy(x_in, grad_in, in_sem)
        copy.start()

    def put(source, index):
        pltpu.make_async_copy(source, x_out.at[index], x_sem.at[index]).start()

    def put_done(source, index):
        pltpu.make_async_copy(source, x_out.at[index], x_sem.at[index]).wait()

    low = low_lanes(ROWS)
    row_of = lax.broadcasted_iota(jnp.int32, (ROWS, 128), 0).astype(F32)
    lane_of = lax.broadcasted_iota(jnp.int32, (ROWS, 128), 1).astype(F32)
    ones[...] = ((row_of < 64) == (lane_of < 64)).astype(BF16)
    small[...] = jnp.zeros_like(small)

    def usable(tokens, filled_first, filled_second):
        return jnp.where(
            tokens < 64, (tokens < filled_first).astype(F32), (tokens - 64 < filled_second).astype(F32)
        )

    def prepare(j):
        start_first, start_second = meta[j, 0:1, :], meta[j, 1:2, :]
        filled_first, filled_second = meta[j, 2:3, :], meta[j, 3:4, :]
        cut = ((row_of >= 64) & (lane_of < 64)).astype(F32) * start_second
        seen = (lane_of <= row_of).astype(F32) * (1.0 - cut)
        mask[...] = seen * usable(lane_of, filled_first, filled_second)
        cut = ((lane_of >= 64) & (row_of < 64)).astype(F32) * start_second
        seen = (row_of <= lane_of).astype(F32) * (1.0 - cut)
        of_rows = usable(row_of, filled_first, filled_second)
        mask_t[...] = seen * of_rows
        kept = 1.0 - start_first
        bef[...] = jnp.where(row_of < 64, kept, kept * (1.0 - start_second)).astype(BF16)
        tail = jnp.where(row_of < 64, 1.0 - start_second, jnp.ones_like(start_second))
        trail[...] = (tail * of_rows).astype(BF16)
        return kept * (1.0 - start_second)

    @pl.when(jnp.logical_not(has_before))
    def _():
        states[0] = jnp.zeros_like(states[0])

    @pl.when(shift != 0)
    def _():
        states[shift] = jnp.zeros_like(states[0])

    @pl.when(section == 1)
    def _():
        forward_rows.wait_recv()

    def first_norm(k):
        at = tile(k, ROWS)
        standard, _ = normalised(rows[at, :].astype(F32))
        normed[at, :] = (standard * first_gain[...].astype(F32) + first_shift[...].astype(F32)).astype(BF16)

    loop(6, first_norm)

    def project(k):
        at = tile(k, 256)
        proj[:, at] = (dot_nn(normed[...], qkv_w[:, at]) + qkv_b[:, at].astype(F32)).astype(BF16)

    loop(9, project)
    put(normed, 6)

    def features(k):
        at = tile(k % 6, ROWS)
        p = k // 6
        for source, table, target in ((0, map_q, phi_q), (6, map_k, phi_k)):
            logits = dot_nn(proj[at, tile(source + p, 128)], table[p])
            for half in range(2):
                phi = half_softmax(logits[:, half * 128 : half * 128 + 128], low, ones[...])
                target[at, tile(2 * p + half, 128)] = phi.astype(BF16)

    loop(36, features)

    def attend(k):
        j = (shift + k) % 6

        @pl.when((j == 0) & has_before)
        def _():
            state_on.wait_recv()

        keep = prepare(j)
        at = tile(j, ROWS)

        def pair(p):
            values = proj[at, tile(12 + p, 128)]
            results = []
            for half in range(2):
                h = 2 * p + half
                own = low if half == 0 else jnp.logical_not(low)
                extended = jnp.where(own, values, jnp.ones_like(values))
                queries, keys = phi_q[at, tile(h, 128)], phi_k[at, tile(h, 128)]
                high, rest = high_low(dot_nt(queries, keys) * mask[...])
                state = states[j, h]
                state_high, state_low = high_low(state)
                early = queries * bef[...]
                results.append(
                    dot_nn(
                        jnp.concatenate([high, rest, early, early], 1),
                        jnp.concatenate([extended, extended, state_high, state_low], 0),
                    )
                )
                states[j + 1, h] = keep * state + dot_tn(keys * trail[...], extended)
            top = jnp.where(low, results[0], results[1])
            bottom = pltpu.roll(jnp.where(low, results[1], results[0]), 64, 1)
            share = top / bottom
            att_wide[at, tile(p, 128)] = share
            den[at, tile(p, 128)] = bottom
            att[at, tile(p, 128)] = share.astype(BF16)

        loop(PAIRS, pair)

        @pl.when((j == 5) & has_after)
        def _():
            state_on.start()

    loop(6, attend)
    put(att, 5)

    def branch_out(k):
        at = tile(k, 256)
        total = dot_nn(att[...], out_w[:, at]) + out_b[:, at].astype(F32)
        res[:, at] = rows[:, at].astype(F32) + total

    loop(3, branch_out)
    put_done(normed, 6)

    def second_norm(k):
        at = tile(k, ROWS)
        standard, _ = normalised(res[at, :])
        normed[at, :] = (standard * second_gain[...].astype(F32) + second_shift[...].astype(F32)).astype(BF16)

    loop(6, second_norm)
    put(normed, 4)

    def feed(k):
        at, rows_at = tile(k // 3, 256), tile(k % 3, 256)
        hidden = dot_nn(normed[rows_at, :], up_w[:, at]) + up_b[:, at].astype(F32)
        square = hidden * hidden
        inner = 0.7978845608028654 * hidden * (1.0 + 0.044715 * square)
        bent = jnp.tanh(inner)
        half = 0.5 * (1.0 + bent)
        act[rows_at, at] = (hidden * half).astype(BF16)
        steep = 0.7978845608028654 * (1.0 + 3.0 * 0.044715 * square)
        slope[rows_at, at] = (half + 0.5 * hidden * (1.0 - bent * bent) * steep).astype(BF16)

    loop(36, feed)
    for n in range(4):
        put(act.at[:, pl.ds(n * WIDE, WIDE)], n)

    def settle(k):
        at = tile(k, 256)
        total = res[:, at] + dot_nn(act[...], down_w[:, at]) + down_b[:, at].astype(F32)
        branch[:, at] = total.astype(BF16)

    loop(3, settle)

    @pl.when(section == 0)
    def _():
        forward_rows.start()
        forward_rows.wait_send()
        backward_rows.wait_recv()

    @pl.when(section == 1)
    def _():
        pltpu.make_async_copy(x_in, grad_in, in_sem).wait()
        copy = pltpu.make_async_copy(branch, ends, out_sem)
        copy.start()
        copy.wait()

    put(grad_in, 7)

    def column_sums(values):
        return jnp.sum(values.astype(F32), 0, keepdims=True)

    small[140:141, :] = column_sums(grad_in[...])

    def feed_back(k):
        at = tile(k, 256)
        grads = dot_nt(grad_in[...], down_w[at, :])
        grads = (grads * slope[:, at].astype(F32)).astype(BF16)
        slope[:, at] = grads

    loop(12, feed_back)
    for n in range(4):
        put(slope.at[:, pl.ds(n * WIDE, WIDE)], 8 + n)
        small[136 + n : 137 + n, :] = column_sums(slope[:, n * WIDE : n * WIDE + WIDE])

    def second_grad(k):
        at = tile(k, 256)
        grad_wide[:, at] = dot_nt(slope[...], up_w[at, :])

    loop(3, second_grad)

    def second_back(k):
        at = tile(k, ROWS)
        grads = grad_wide[at, :]
        standard, scale = normalised(res[at, :])
        small[134:135, :] += jnp.sum(grads * standard, 0, keepdims=True)
        small[135:136, :] += jnp.sum(grads, 0, keepdims=True)
        grads = norm_input_grad(grads, standard, scale, second_gain[...].astype(F32))
        grads = grad_in[at, :].astype(F32) + grads
        res[at, :] = grads
        rounded = grads.astype(BF16)
        branch[at, :] = rounded
        small[133:134, :] += column_sums(rounded)

    loop(6, second_back)
    put(branch, 12)

    def attended_grad(k):
        at = tile(k, 256)
        grad_wide[:, at] = dot_nt(branch[...], out_w[at, :])

    loop(3, attended_grad)
    for n in range(4):
        put_done(act.at[:, pl.ds(n * WIDE, WIDE)], n)

    put_done(att, 5)
    back_state[...] = jnp.zeros_like(back_state)

    def attend_back(k):
        j = (shift + 5 - k) % 6

        @pl.when(j == 5)
        def _():
            @pl.when(has_after)
            def _():
                state_back.wait_recv()
                back_state[...] = back_in[...]

            @pl.when(jnp.logical_not(has_after))
            def _():
                back_state[...] = jnp.zeros_like(back_state)

        keep = prepare(j)
        at = tile(j, ROWS)

        def pair(p):
            values = proj[at, tile(12 + p, 128)]
            grads = (grad_wide[at, tile(p, 128)] / den[at, tile(p, 128)]).astype(BF16)
            sums = -half_sums(grads.astype(F32) * att_wide[at, tile(p, 128)], low)
            other_sums = pltpu.roll(sums, 64, 1)
            lanes = lax.broadcasted_iota(jnp.int32, (ROWS, 128), 1) % 64
            one = other_sums.astype(BF16).astype(F32)
            two = (other_sums - one).astype(BF16).astype(F32)
            three = other_sums - one - two
            spread = jnp.where(lanes == 0, one, jnp.where(lanes == 1, two, jnp.where(lanes == 2, three, 0.0)))
            spread = spread.astype(BF16)
            value_grads, query_grads, key_grads = [], [], []
            for half in range(2):
                h = 2 * p + half
                own = low if half == 0 else jnp.logical_not(low)
                extended = jnp.where(own, values, jnp.ones_like(values))
                grads_ext = jnp.where(own, grads, spread)
                queries, keys = phi_q[at, tile(h, 128)], phi_k[at, tile(h, 128)]
                high, rest = high_low(dot_nt(grads_ext, extended) * mask[...])
                state_high, state_low = high_low(states[j, h])
                query_grad = dot_nn(
                    jnp.concatenate([high, rest], 1), jnp.concatenate([keys, keys], 0)
                )
                query_grad += bef[...].astype(F32) * dot_nt(
                    jnp.concatenate([grads_ext, grads_ext], 1),
                    jnp.concatenate([state_high, state_low], 1),
                )
                high, rest = high_low(dot_nt(extended, grads_ext) * mask_t[...])
                later = back_state[h]
                later_high, later_low = high_low(later)
                key_grad = dot_nn(
                    jnp.concatenate([high, rest], 1), jnp.concatenate([queries, queries], 0)
                )
                key_grad += trail[...].astype(F32) * dot_nt(
                    jnp.concatenate([extended, extended], 1),
                    jnp.concatenate([later_high, later_low], 1),
                )
                scores_t = (dot_nt(keys, queries) * mask_t[...]).astype(BF16)
                value_grads.append(
                    dot_nn(
                        jnp.concatenate([scores_t, keys * trail[...]], 1),
                        jnp.concatenate([grads_ext, later_high], 0),
                    )
                )
                back_state[h] = keep * later + dot_tn(queries * bef[...], grads_ext)
                for phi, grad, kept in ((queries, query_grad, query_grads), (keys, key_grad, key_grads)):
                    phi = phi.astype(F32)
                    kept.append(phi * (grad - half_sums(phi * grad, low)))
            act[at, tile(12 + p, 128)] = jnp.where(low, value_grads[0], value_grads[1]).astype(BF16)
            for kept, target, first in ((query_grads, act, 18), (key_grads, att, 0)):
                left = kept[0] - pltpu.roll(kept[0], 64, 1)
                right = pltpu.roll(kept[1], 64, 1) - kept[1]
                target[at, tile(first + p, 128)] = jnp.where(low, left, right).astype(BF16)

        loop(PAIRS, pair)

        @pl.when((j == 0) & has_before)
        def _():
            back_out[...] = back_state[...]
            state_back.start()

    loop(6, attend_back)

    def maps_back(p):
        lanes = tile(p, 128)
        first = lax.broadcasted_iota(jnp.int32, (64, 128), 1) < 64
        for offset, target, source, table, at in ((0, act, 18, pair_q, 0), (6, att, 0, pair_k, 64)):
            logit_grads = target[:, tile(source + p, 128)]
            act[:, tile(offset + p, 128)] = dot_nt(logit_grads, table[p]).astype(BF16)
            product = dot_tn(proj[:, tile(offset + p, 128)], logit_grads)
            small[at : at + 64, lanes] = jnp.where(first, product[:64], product[64:])

    loop(PAIRS, maps_back)
    for n in range(3):
        put(act.at[:, pl.ds(n * WIDE, WIDE)], 13 + n)
        small[130 + n : 131 + n, :] = column_sums(act[:, n * WIDE : n * WIDE + WIDE])

    def first_grad(k):
        at = tile(k, 256)
        grad_wide[:, at] = dot_nt(act[:, : 3 * WIDE], qkv_w[at, :])

    loop(3, first_grad)

    def first_back(k):
        at = tile(k, ROWS)
        grads = grad_wide[at, :]
        standard, scale = normalised(rows[at, :].astype(F32))
        small[128:129, :] += jnp.sum(grads * standard, 0, keepdims=True)
        small[129:130, :] += jnp.sum(grads, 0, keepdims=True)
        grads = norm_input_grad(grads, standard, scale, first_gain[...].astype(F32))
        rows[at, :] = (res[at, :] + grads).astype(BF16)

    loop(6, first_back)

    @pl.when(section == 1)
    def _():
        backward_rows.start()
        backward_rows.wait_send()

    @pl.when(section == 0)
    def _():
        copy = pltpu.make_async_copy(rows, ends, out_sem)
        copy.start()
        copy.wait()

    put_done(normed, 4)
    put_done(grad_in, 7)
    put_done(branch, 12)
    for n in range(4):
        put_done(slope.at[:, pl.ds(n * WIDE, WIDE)], 8 + n)
    for n in range(3):
        put_done(act.at[:, pl.ds(n * WIDE, WIDE)], 13 + n)

    @pl.when(has_after)
    def _():
        state_on.wait_send()

    @pl.when(has_before)
    def _():
        state_back.wait_send()


def layers(x_in, meta, weights, mesh):
    (
        first_gain, first_shift, qkv_w, qkv_b, query_map, key_map, out_w, out_b,
        second_gain, second_shift, up_w, up_b, down_w, down_b,
    ) = weights

    def tables(table):
        heads = table.reshape(64, PAIRS, 2, 64).transpose(1, 2, 0, 3)
        both = jnp.concatenate([heads, -heads], -1)
        none, zero = jnp.zeros_like(both[:, 0]), jnp.zeros_like(heads[:, 0])
        signed = jnp.concatenate(
            [
                jnp.concatenate([both[:, 0], none], -1),
                jnp.concatenate([none, both[:, 1]], -1),
            ],
            1,
        )
        plain = jnp.concatenate(
            [
                jnp.concatenate([heads[:, 0], zero], -1),
                jnp.concatenate([zero, heads[:, 1]], -1),
            ],
            1,
        )
        return signed, plain

    map_q, pair_q = tables(query_map[0])
    map_k, pair_k = tables(key_map[0])
    tokens = 6 * ROWS
    any_space = pl.BlockSpec(memory_space=pl.ANY)
    in_vmem = pl.BlockSpec(memory_space=pltpu.VMEM)
    return pl.pallas_call(
        functools.partial(layers_kernel, mesh.shape["ctx"]),
        out_shape=(
            jax.ShapeDtypeStruct((16, tokens, WIDE), BF16),
            jax.ShapeDtypeStruct((tokens, WIDE), BF16),
            jax.ShapeDtypeStruct((256, WIDE), F32),
        ),
        in_specs=[any_space] + [in_vmem] * 17,
        out_specs=(any_space, any_space, in_vmem),
        scratch_shapes=[
            pltpu.VMEM((tokens, WIDE), BF16),
            pltpu.VMEM((tokens, WIDE), BF16),
            pltpu.VMEM((tokens, WIDE), BF16),
            pltpu.VMEM((tokens, 3 * WIDE), BF16),
            pltpu.VMEM((tokens, 2 * WIDE), BF16),
            pltpu.VMEM((tokens, 2 * WIDE), BF16),
            pltpu.VMEM((tokens, WIDE), BF16),
            pltpu.VMEM((tokens, WIDE), F32),
            pltpu.VMEM((tokens, WIDE), F32),
            pltpu.VMEM((tokens, WIDE), F32),
            pltpu.VMEM((tokens, 4 * WIDE), BF16),
            pltpu.VMEM((tokens, 4 * WIDE), BF16),
            pltpu.VMEM((7, HEADS, 128, 128), F32),
            pltpu.VMEM((HEADS, 128, 128), F32),
            pltpu.VMEM((HEADS, 128, 128), F32),
            pltpu.VMEM((HEADS, 128, 128), F32),
            pltpu.VMEM((tokens, WIDE), F32),
            pltpu.VMEM((tokens, WIDE), BF16),
            pltpu.VMEM((128, 128), BF16),
            pltpu.VMEM((128, 128), F32),
            pltpu.VMEM((128, 128), F32),
            pltpu.VMEM((128, 128), BF16),
            pltpu.VMEM((128, 128), BF16),
            pltpu.SemaphoreType.DMA((16,)),
            pltpu.SemaphoreType.DMA,
            pltpu.SemaphoreType.DMA,
            pltpu.SemaphoreType.DMA((4, 2)),
        ],
        compiler_params=pltpu.CompilerParams(
            collective_id=1, has_side_effects=True, vmem_limit_bytes=60 * 1024 * 1024
        ),
    )(
        x_in.reshape(tokens, WIDE), meta, first_gain, first_shift, qkv_w[0], qkv_b, map_q, map_k,
        pair_q, pair_k, out_w[0], out_b, second_gain, second_shift, up_w[0], up_b, down_w[0], down_b,
    )


def move_kernel(ctx_size, gather, count, *refs):
    sources, targets, sems = refs[:count], refs[count : 2 * count], refs[2 * count]
    me = lax.axis_index("ctx")
    barrier = pltpu.get_barrier_semaphore()

    def greet(k):
        device = {"ctx": (me + 1 + k) % ctx_size}
        pl.semaphore_signal(barrier, inc=1, device_id=device, device_id_type=MESH)

    loop(ctx_size - 1, greet)
    pl.semaphore_wait(barrier, ctx_size - 1)

    def place(k):
        if gather:
            at = k * ctx_size + me
            return at // 6, at % 6
        at = 6 * me + k
        return at % ctx_size, at // ctx_size

    def origin(k):
        if gather:
            return (6 * me + k) % ctx_size
        return (k * ctx_size + me) // 6

    def local(n, k, at):
        return pltpu.make_async_copy(sources[n].at[k], targets[n].at[at], sems.at[n, 2, k])

    def remote(n, k, at, device):
        return pltpu.make_async_remote_copy(
            src_ref=sources[n].at[k],
            dst_ref=targets[n].at[at],
            send_sem=sems.at[n, 0, k],
            recv_sem=sems.at[n, 1, at],
            device_id={"ctx": device},
            device_id_type=MESH,
        )

    for n in range(count):
        for k in range(6):
            device, at = place(k)

            @pl.when(device == me)
            def _():
                local(n, k, at).start()

            @pl.when(device != me)
            def _():
                remote(n, k, at, device).start()

    for n in range(count):
        for k in range(6):
            device, at = place(k)

            @pl.when(device == me)
            def _():
                local(n, k, at).wait()

            @pl.when(device != me)
            def _():
                remote(n, k, at, device).wait_send()

            @pl.when(origin(k) != me)
            def _():
                remote(n, k, k, (me + 1) % ctx_size).wait_recv()


def moved(arrays, mesh, gather):
    count = len(arrays)
    in_vmem = pl.BlockSpec(memory_space=pltpu.VMEM)
    return pl.pallas_call(
        functools.partial(move_kernel, mesh.shape["ctx"], gather, count),
        out_shape=tuple(jax.ShapeDtypeStruct(a.shape, a.dtype) for a in arrays),
        in_specs=[in_vmem] * count,
        out_specs=(in_vmem,) * count,
        scratch_shapes=[pltpu.SemaphoreType.DMA((count, 3, 6))],
        compiler_params=pltpu.CompilerParams(
            collective_id=2 if gather else 3, has_side_effects=True, vmem_limit_bytes=16 * 1024 * 1024
        ),
    )(*arrays)


def body(mesh, ends_in, begins, filled, *weights):
    meta = jnp.concatenate([begins, filled], 1).astype(F32)[:, :, None]
    meta = jnp.broadcast_to(jnp.pad(meta, ((0, 0), (0, 4), (0, 0))), (6, 8, 128))
    x_in, meta = moved((ends_in[0], meta), mesh, True)
    x, ends, small = layers(x_in, meta, weights, mesh)
    (ends_out,) = moved((ends.reshape(6, ROWS, WIDE),), mesh, False)
    qkv_grad, out_grad, up_grad, down_grad, small = reduced(x, small, mesh)

    def row(first, count=1):
        return small[first : first + count].reshape(1, count * WIDE)

    return (
        ends_out[None], row(128), row(129), qkv_grad[None], row(130, 3), small[None, :64],
        small[None, 64:128], out_grad[None], row(133), row(134), row(135), up_grad[None],
        row(136, 4), down_grad[None], row(140),
    )


def solution(mesh):
    placed = (
        P("section", None, ("dp", "ctx"), None),
        P(None, ("dp", "ctx")),
        P(None, ("dp", "ctx")),
        P("section", None),
        P("section", None),
        P("section", None, None),
        P("section", None),
        P("section", None, None),
        P("section", None, None),
        P("section", None, None),
        P("section", None),
        P("section", None),
        P("section", None),
        P("section", None, None),
        P("section", None),
        P("section", None, None),
        P("section", None),
    )
    return jax.shard_map(
        functools.partial(body, mesh),
        mesh=mesh,
        in_specs=placed,
        out_specs=(
            P("section", None, ("dp", "ctx"), None),
            P("section", None),
            P("section", None),
            P("section", None, None),
            P("section", None),
            P("section", None, None),
            P("section", None, None),
            P("section", None, None),
            P("section", None),
            P("section", None),
            P("section", None),
            P("section", None, None),
            P("section", None),
            P("section", None, None),
            P("section", None),
        ),
        check_vma=False,
    )
```

```python
import functools

import jax
import jax.numpy as jnp
from jax import lax
from jax.experimental import pallas as pl
from jax.experimental.pallas import tpu as pltpu
from jax.sharding import PartitionSpec as P

BLOCK = 64
ROWS = 128
HEADS = 12
PAIRS = 6
GROUP = 6
GROUP_BACK = 6
EPSILON = 1e-05
F32, BF16 = jnp.float32, jnp.bfloat16

MESH = pl.DeviceIdType.MESH
WIDE = 768
HALF = 384


def bit_length(size):
    return (size - 1).bit_length()


def bit_orders(ctx_size, dp_size):
    ctx_bits = [("ctx", k) for k in range(bit_length(ctx_size))]
    dp_bits = [("dp", k) for k in range(bit_length(dp_size))]

    def interleaved(first, second):
        order = []
        for k in range(max(len(first), len(second))):
            order += first[k : k + 1] + second[k : k + 1]
        return order

    return (interleaved(ctx_bits, dp_bits), interleaved(ctx_bits[::-1], dp_bits))


def halvings(rows, count):
    sizes, halved = [rows], []
    for _ in range(count):
        halved.append(sizes[-1] % 32 == 0)
        sizes.append(sizes[-1] // 2 if halved[-1] else sizes[-1])
    return sizes, halved


class Reduction:
    def __init__(self, rows, orders):
        self.rows, self.orders = rows, orders
        self.count = len(orders[0])
        self.sizes, self.halved = halvings(rows, self.count)
        self.steps = [("rs", s) for s in range(self.count)]
        self.steps += [("ag", s) for s in reversed(range(self.count)) if self.halved[s]]
        self.offsets, self.bits = [], []
        for order in orders:
            offset, offsets, bits = 0, [0], []
            for s, (axis, k) in enumerate(order):
                bit = (lax.axis_index(axis) // (1 << k)) % 2
                bits.append(bit)
                if self.halved[s]:
                    offset = offset + bit * self.sizes[s + 1]
                offsets.append(offset)
            self.offsets.append(offsets)
            self.bits.append(bits)

    def partner(self, part, s):
        axis, k = self.orders[part][s]
        return {axis: lax.axis_index(axis) + (1 << k) * (1 - 2 * self.bits[part][s])}

    def rows_at(self, offset, size):
        if isinstance(offset, int):
            return pl.ds(offset, size)
        return pl.ds(pl.multiple_of(offset, 16), size)

    def copy(self, buffer, whole, received, sems, part, step):
        kind, s = self.steps[step]
        columns = pl.ds(part * HALF, HALF)
        size = self.sizes[s + 1]
        if kind == "rs":
            offset = self.offsets[part][s]
            if self.halved[s]:
                offset = offset + (1 - self.bits[part][s]) * size
            source = buffer.at[self.rows_at(offset, size), columns]
            target = received[s]
        else:
            source = whole.at[self.rows_at(self.offsets[part][s + 1], size), columns]
            target = source
        return pltpu.make_async_remote_copy(
            src_ref=source,
            dst_ref=target,
            send_sem=sems[0],
            recv_sem=sems[1],
            device_id=self.partner(part, s),
            device_id_type=MESH,
        )

    def add(self, buffer, whole, received, part, step):
        kind, s = self.steps[step]
        if kind == "rs":
            size = self.sizes[s + 1]
            rows = self.rows_at(self.offsets[part][s + 1], size)
            columns = pl.ds(part * HALF, HALF)
            total = buffer[rows, columns].astype(jnp.float32) + received[s][...].astype(jnp.float32)
            target = whole if s + 1 == self.count else buffer
            target[rows, columns] = total.astype(jnp.bfloat16)


class Pieces:
    def __init__(self, ctx_size, gather):
        self.size, self.gather, self.me = ctx_size, gather, lax.axis_index("ctx")

    def place(self, k):
        if self.gather:
            at = k * self.size + self.me
            return at // 6, at % 6
        at = 6 * self.me + k
        return at % self.size, at // self.size

    def origin(self, k):
        if self.gather:
            return (6 * self.me + k) % self.size
        return (k * self.size + self.me) // 6

    def start(self, source, target, sems):
        for k in range(6):
            device, at = self.place(k)

            @pl.when(device == self.me)
            def _():
                self.local(source, target, sems, k, at).start()

            @pl.when(device != self.me)
            def _():
                self.remote(source, target, sems, k, at, device).start()

    def wait(self, source, target, sems):
        for k in range(6):
            device, at = self.place(k)

            @pl.when(device == self.me)
            def _():
                self.local(source, target, sems, k, at).wait()

            @pl.when(device != self.me)
            def _():
                self.remote(source, target, sems, k, at, device).wait_send()

            @pl.when(self.origin(k) != self.me)
            def _():
                self.remote(source, target, sems, k, k, (self.me + 1) % self.size).wait_recv()

    def local(self, source, target, sems, k, at):
        return pltpu.make_async_copy(source(k), target(at), sems.at[2, k])

    def remote(self, source, target, sems, k, at, device):
        return pltpu.make_async_remote_copy(
            src_ref=source(k),
            dst_ref=target(at),
            send_sem=sems.at[0, k],
            recv_sem=sems.at[1, at],
            device_id={"ctx": device},
            device_id_type=MESH,
        )


def block_rows(k):
    return pl.ds(k * ROWS if isinstance(k, int) else pl.multiple_of(k * ROWS, ROWS), ROWS)


def greet_ctx(barrier, ctx_size):
    me = lax.axis_index("ctx")

    def greet(k):
        device = {"ctx": (me + 1 + k) % ctx_size}
        pl.semaphore_signal(barrier, inc=1, device_id=device, device_id_type=MESH)

    loop(ctx_size - 1, greet)
    return ctx_size - 1


def reduce_kernel(
    orders, ctx_size, chunks, x_ref, small_ref, ends, sums, small_out, ends_out, *scratch
):
    count = len(orders[0])
    big, big_whole, little, little_whole = scratch[:4]
    scratch = scratch[4:]
    big_recv, little_recv = scratch[:count], scratch[count : 2 * count]
    left, right, send, recv, send_small, recv_small, load, store, moves = scratch[2 * count :]
    large, small = Reduction(WIDE, orders), Reduction(little.shape[0], orders)
    steps = len(large.steps)

    def operands(c):
        left_at = jnp.where(c < 4, c, jnp.where(c < 8, 4, jnp.where(c == 8, 5, 6)))
        right_at = jnp.where(c < 4, 7, c + 4)
        slot = c % 2
        return (
            pltpu.make_async_copy(x_ref.at[left_at], left.at[slot], load.at[slot, 0]),
            pltpu.make_async_copy(x_ref.at[right_at], right.at[slot], load.at[slot, 1]),
        )

    for copy in operands(0):
        copy.start()
    little[...] = small_ref[...].astype(BF16)

    barrier = pltpu.get_barrier_semaphore()
    greeted = greet_ctx(barrier, ctx_size)
    for s in range(count):
        if orders[0][s][0] != "ctx":
            pl.semaphore_signal(barrier, inc=1, device_id=large.partner(0, s), device_id_type=MESH)
            greeted += 1
    pl.semaphore_wait(barrier, greeted)

    def big_copy(c, part, step):
        received = [r.at[c, part] for r in big_recv]
        sems = (send.at[c, part, step], recv.at[c, part, step])
        return large.copy(big.at[c], big_whole.at[c], received, sems, part, step)

    def small_copy(part, step):
        received = [r.at[part] for r in little_recv]
        sems = (send_small.at[part, step], recv_small.at[part, step])
        return small.copy(little, little_whole, received, sems, part, step)

    for part in range(2):
        small_copy(part, 0).start()
    pieces = Pieces(ctx_size, False)
    given = (lambda k: ends.at[block_rows(k), :], lambda k: ends_out.at[k], moves)

    def tick(t, carry):
        @pl.when(t < chunks)
        def _():
            for copy in operands(t):
                copy.wait()

            @pl.when(t + 1 < chunks)
            def _():
                for copy in operands(t + 1):
                    copy.start()

            slot = t % 2
            big[t] = dot_tn(left[slot], right[slot]).astype(BF16)
            for part in range(2):
                big_copy(t, part, 0).start()

        @pl.when(t == chunks)
        def _():
            pieces.start(*given)

        for step in range(steps):
            c = t - 1 - step

            @pl.when((c >= 0) & (c < chunks))
            def _():
                for part in range(2):
                    big_copy(c, part, step).wait()
                    received = [r.at[c, part] for r in big_recv]
                    large.add(big.at[c], big_whole.at[c], received, part, step)
                    if step + 1 < steps:
                        big_copy(c, part, step + 1).start()
                if step + 1 == steps:
                    pltpu.make_async_copy(big_whole.at[c], sums.at[c], store).start()

            if step < len(small.steps):
                @pl.when(t == step)
                def _():
                    for part in range(2):
                        small_copy(part, step).wait()
                        received = [r.at[part] for r in little_recv]
                        small.add(little, little_whole, received, part, step)
                        if step + 1 < len(small.steps):
                            small_copy(part, step + 1).start()

        return carry

    lax.fori_loop(0, chunks + steps, tick, 0)
    small_out[...] = little_whole[...]
    pieces.wait(*given)
    pltpu.make_async_copy(big_whole, sums, store).wait()


def reduced(x, small, ends, mesh):
    orders = bit_orders(mesh.shape["ctx"], mesh.shape["dp"])
    count, chunks, tokens = len(orders[0]), 12, x.shape[1]
    sizes, _ = halvings(WIDE, count)
    small_rows = small.shape[0]
    small_sizes, small_halved = halvings(small_rows, count)
    steps = count + sum(halvings(WIDE, count)[1])
    small_steps = count + sum(small_halved)
    any_space = pl.BlockSpec(memory_space=pl.ANY)
    in_vmem = pl.BlockSpec(memory_space=pltpu.VMEM)
    return pl.pallas_call(
        functools.partial(reduce_kernel, orders, mesh.shape["ctx"], chunks),
        out_shape=(
            jax.ShapeDtypeStruct((chunks, WIDE, WIDE), BF16),
            jax.ShapeDtypeStruct((small_rows, WIDE), BF16),
            jax.ShapeDtypeStruct((6, ROWS, WIDE), BF16),
        ),
        in_specs=[any_space, in_vmem, in_vmem],
        out_specs=(any_space, in_vmem, in_vmem),
        scratch_shapes=[
            pltpu.VMEM((chunks, WIDE, WIDE), BF16),
            pltpu.VMEM((chunks, WIDE, WIDE), BF16),
            pltpu.VMEM((small_rows, WIDE), BF16),
            pltpu.VMEM((small_rows, WIDE), BF16),
            *(pltpu.VMEM((chunks, 2, size, HALF), BF16) for size in sizes[1:]),
            *(pltpu.VMEM((2, size, HALF), BF16) for size in small_sizes[1:]),
            pltpu.VMEM((2, tokens, WIDE), BF16),
            pltpu.VMEM((2, tokens, WIDE), BF16),
            pltpu.SemaphoreType.DMA((chunks, 2, steps)),
            pltpu.SemaphoreType.DMA((chunks, 2, steps)),
            pltpu.SemaphoreType.DMA((2, small_steps)),
            pltpu.SemaphoreType.DMA((2, small_steps)),
            pltpu.SemaphoreType.DMA((2, 2)),
            pltpu.SemaphoreType.DMA,
            pltpu.SemaphoreType.DMA((3, 6)),
        ],
        compiler_params=pltpu.CompilerParams(
            collective_id=0, has_side_effects=True, vmem_limit_bytes=60 * 1024 * 1024
        ),
    )(x, small, ends)


def finish_kernel(sums, little, ends, *refs):
    outs, (narrow, wide, passing, load, store, through) = refs[:15], refs[15:]
    (
        ends_out, first_gain, first_shift, qkv_w, qkv_b, map_q, map_k, out_w, out_b,
        second_gain, second_shift, up_w, up_b, down_w, down_b,
    ) = outs
    take = pltpu.make_async_copy(ends, passing, through.at[0])
    give = pltpu.make_async_copy(passing, ends_out.at[0], through.at[1])
    take.start()
    depth = narrow.shape[0]
    targets = [down_w.at[0, pl.ds(n * WIDE, WIDE), :] for n in range(4)]
    targets += [up_w.at[0, :, pl.ds(n * WIDE, WIDE)] for n in range(4)]
    targets += [out_w.at[0]]
    targets += [qkv_w.at[0, :, pl.ds(n * WIDE, WIDE)] for n in range(3)]

    def read(c):
        return pltpu.make_async_copy(sums.at[c], narrow.at[c % depth], load.at[c % depth])

    def write(c):
        return pltpu.make_async_copy(wide.at[c % depth], targets[c], store.at[c % depth])

    for c in range(depth):
        read(c).start()
    for target, first in (
        (first_gain, 128), (first_shift, 129), (out_b, 133), (second_gain, 134), (second_shift, 135), (down_b, 140),
    ):
        target[...] = little[first : first + 1, :].astype(F32)
    for target, first, count in ((qkv_b, 130, 3), (up_b, 136, 4)):
        for n in range(count):
            target[:, n * WIDE : n * WIDE + WIDE] = little[first + n : first + n + 1, :].astype(F32)
    map_q[0] = little[0:64, :].astype(F32)
    map_k[0] = little[64:128, :].astype(F32)
    take.wait()
    give.start()
    for c in range(len(targets)):
        read(c).wait()
        if c >= depth:
            write(c - depth).wait()

        def widen(k):
            at = tile(k, 256)
            wide[c % depth, at, :] = narrow[c % depth, at, :].astype(F32)

        loop(3, widen)
        write(c).start()
        if c + depth < len(targets):
            read(c + depth).start()
    for c in range(len(targets) - depth, len(targets)):
        write(c).wait()
    give.wait()


def finished(sums, little, ends, weights):
    any_space = pl.BlockSpec(memory_space=pl.ANY)
    in_vmem = pl.BlockSpec(memory_space=pltpu.VMEM)
    shapes = [jax.ShapeDtypeStruct((1,) + ends.shape, BF16)]
    shapes += [jax.ShapeDtypeStruct(weight.shape, F32) for weight in weights]
    large = (0, 3, 7, 11, 13)
    return pl.pallas_call(
        finish_kernel,
        out_shape=tuple(shapes),
        in_specs=[any_space, in_vmem, any_space],
        out_specs=tuple(any_space if n in large else in_vmem for n in range(15)),
        scratch_shapes=[
            pltpu.VMEM((3, WIDE, WIDE), BF16),
            pltpu.VMEM((3, WIDE, WIDE), F32),
            pltpu.VMEM(ends.shape, BF16),
            pltpu.SemaphoreType.DMA((3,)),
            pltpu.SemaphoreType.DMA((3,)),
            pltpu.SemaphoreType.DMA((2,)),
        ],
        compiler_params=pltpu.CompilerParams(vmem_limit_bytes=60 * 1024 * 1024),
    )(sums, little, ends)


def dot_nn(left, right):
    return jnp.dot(left, right, preferred_element_type=F32)


def dot_nt(left, right):
    return lax.dot_general(left, right, (((1,), (1,)), ((), ())), preferred_element_type=F32)


def dot_tn(left, right):
    return lax.dot_general(left, right, (((0,), (0,)), ((), ())), preferred_element_type=F32)


def high_low(values):
    high = values.astype(BF16)
    return high, (values - high.astype(F32)).astype(BF16)


def tile(index, size):
    return pl.ds(pl.multiple_of(index * size, size), size)


def loop(count, step, unroll=1):
    def body(k, carry):
        step(k)
        return carry

    lax.fori_loop(0, count, body, 0, unroll=unroll)


def low_lanes(rows):
    return lax.broadcasted_iota(jnp.int32, (rows, 128), 1) < 64


def normalised(rows):
    average = jnp.mean(rows, -1, keepdims=True)
    centred = rows - average
    scale = lax.rsqrt(jnp.mean(centred * centred, -1, keepdims=True) + EPSILON)
    return centred * scale, scale


def norm_input_grad(grad, standard, scale, gain):
    wide = grad * gain
    first = jnp.mean(wide, -1, keepdims=True)
    second = jnp.mean(wide * standard, -1, keepdims=True)
    return scale * (wide - first - standard * second)


def half_sums(values, low):
    first = jnp.sum(jnp.where(low, values, 0.0), -1, keepdims=True)
    second = jnp.sum(jnp.where(low, 0.0, values), -1, keepdims=True)
    return jnp.where(low, first, second)


def half_softmax(logits, low, ones):
    lowest = jnp.float32(-3e38)
    first = jnp.max(jnp.where(low, logits, lowest), -1, keepdims=True)
    second = jnp.max(jnp.where(low, lowest, logits), -1, keepdims=True)
    powers = jnp.exp(logits - jnp.where(low, first, second))
    high, rest = high_low(powers)
    return powers / dot_nn(jnp.concatenate([high, rest], 1), jnp.concatenate([ones, ones], 0))


def layers_kernel(ctx_size, *refs):
    (
        x_in, begins, filled, first_gain, first_shift, qkv_given, qkv_b, map_q_given, map_k_given,
        out_given, out_b, second_gain, second_shift, up_given, up_b, down_given, down_b,
        x_out, ends, small,
        qkv_w, out_w, up_w, down_w, map_q, map_k, pair_q, pair_k, meta_own, meta,
        rows, grad_in, normed, proj, phi_q, phi_k, att, att_wide, den, res, act, slope,
        states, back_state, back_in, back_out, grad_wide, branch,
        ones, mask, mask_t, bef, trail, x_sem, out_sem, remote, weight_sem, moves,
    ) = refs
    section, me = lax.axis_index("section"), lax.axis_index("ctx")
    has_before = (6 * me) % ctx_size != 0
    has_after = (6 * (me + 1)) % ctx_size != 0
    reach = (6 * me + 5) % ctx_size
    shift = jnp.where(reach <= 5, 5 - reach, 0)
    other = {"section": 1 - section}

    def weight(n):
        given, kept = ((qkv_given, qkv_w), (out_given, out_w), (up_given, up_w), (down_given, down_w))[n]
        return pltpu.make_async_copy(given.at[0], kept, weight_sem.at[n])

    def remote_copy(source, target, index, device):
        return pltpu.make_async_remote_copy(
            src_ref=source,
            dst_ref=target,
            send_sem=remote.at[index, 0],
            recv_sem=remote.at[index, 1],
            device_id=device,
            device_id_type=MESH,
        )

    forward_rows = remote_copy(branch, rows, 0, other)
    backward_rows = remote_copy(rows, grad_in, 1, other)
    state_on = remote_copy(states.at[6], states.at[0], 2, {"ctx": me + 1})
    state_back = remote_copy(back_out, back_in, 3, {"ctx": me - 1})
    pieces = Pieces(ctx_size, True)
    rows_moves = (lambda k: x_in.at[0, k], lambda k: rows.at[block_rows(k), :], moves.at[0])
    grad_moves = (lambda k: x_in.at[0, k], lambda k: grad_in.at[block_rows(k), :], moves.at[0])
    meta_moves = (lambda k: meta_own.at[k], lambda k: meta.at[k], moves.at[1])

    barrier = pltpu.get_barrier_semaphore()
    greeted = greet_ctx(barrier, ctx_size)
    pl.semaphore_signal(barrier, inc=1, device_id=other, device_id_type=MESH)
    for k in range(6):
        for n, source in ((0, begins), (2, filled)):
            for half in range(2):
                value = source[k : k + 1, half : half + 1].astype(F32)
                meta_own[k, n + half : n + half + 1, :] = jnp.broadcast_to(value, (1, 128))
    pl.semaphore_wait(barrier, greeted + 1)

    @pl.when(section == 0)
    def _():
        pieces.start(*rows_moves)

    pieces.start(*meta_moves)
    for n in range(4):
        weight(n).start()

    def put(source, index):
        pltpu.make_async_copy(source, x_out.at[index], x_sem.at[index]).start()

    def put_done(source, index):
        pltpu.make_async_copy(source, x_out.at[index], x_sem.at[index]).wait()

    low = low_lanes(ROWS)
    row_of = lax.broadcasted_iota(jnp.int32, (ROWS, 128), 0).astype(F32)
    lane_of = lax.broadcasted_iota(jnp.int32, (ROWS, 128), 1).astype(F32)
    ones[...] = ((row_of < 64) == (lane_of < 64)).astype(BF16)
    small[...] = jnp.zeros_like(small)
    left_lanes = low_lanes(64)
    for given, signed, plain in ((map_q_given, map_q, pair_q), (map_k_given, map_k, pair_k)):
        signed[...] = jnp.zeros_like(signed)
        for p in range(PAIRS):
            both = given[0, :, p * 128 : p * 128 + 128].astype(F32)
            turned = pltpu.roll(both, 64, 1)
            signed[p, :64, :128] = jnp.where(left_lanes, both, -turned).astype(BF16)
            signed[p, 64:, 128:] = jnp.where(left_lanes, turned, -both).astype(BF16)
            plain[p, :64, :] = jnp.where(left_lanes, both, 0.0).astype(BF16)
            plain[p, 64:, :] = jnp.where(left_lanes, 0.0, both).astype(BF16)

    def usable(tokens, filled_first, filled_second):
        return jnp.where(
            tokens < 64, (tokens < filled_first).astype(F32), (tokens - 64 < filled_second).astype(F32)
        )

    def prepare(j):
        start_first, start_second = meta[j, 0:1, :], meta[j, 1:2, :]
        filled_first, filled_second = meta[j, 2:3, :], meta[j, 3:4, :]
        cut = ((row_of >= 64) & (lane_of < 64)).astype(F32) * start_second
        seen = (lane_of <= row_of).astype(F32) * (1.0 - cut)
        mask[...] = seen * usable(lane_of, filled_first, filled_second)
        cut = ((lane_of >= 64) & (row_of < 64)).astype(F32) * start_second
        seen = (row_of <= lane_of).astype(F32) * (1.0 - cut)
        of_rows = usable(row_of, filled_first, filled_second)
        mask_t[...] = seen * of_rows
        kept = 1.0 - start_first
        bef[...] = jnp.where(row_of < 64, kept, kept * (1.0 - start_second)).astype(BF16)
        tail = jnp.where(row_of < 64, 1.0 - start_second, jnp.ones_like(start_second))
        trail[...] = (tail * of_rows).astype(BF16)
        return kept * (1.0 - start_second)

    @pl.when(jnp.logical_not(has_before))
    def _():
        states[0] = jnp.zeros_like(states[0])

    @pl.when(shift != 0)
    def _():
        states[shift] = jnp.zeros_like(states[0])

    @pl.when(section == 0)
    def _():
        pieces.wait(*rows_moves)

    @pl.when(section == 1)
    def _():
        forward_rows.wait_recv()
        pieces.start(*grad_moves)

    def first_norm(k):
        at = tile(k, 384)
        standard, _ = normalised(rows[at, :].astype(F32))
        normed[at, :] = (standard * first_gain[...].astype(F32) + first_shift[...].astype(F32)).astype(BF16)

    loop(2, first_norm)

    def project(k):
        at = tile(k, 256)
        proj[:, at] = (dot_nn(normed[...], qkv_w[:, at]) + qkv_b[:, at].astype(F32)).astype(BF16)

    weight(0).wait()
    loop(9, project)
    put(normed, 6)

    def features(p):
        low = low_lanes(6 * ROWS)
        for source, table, target in ((0, map_q, phi_q), (6, map_k, phi_k)):
            logits = dot_nn(proj[:, tile(source + p, 128)], table[p])
            for half in range(2):
                phi = half_softmax(logits[:, half * 128 : half * 128 + 128], low, ones[...])
                target[:, tile(2 * p + half, 128)] = phi.astype(BF16)

    loop(PAIRS, features)

    def attend(k):
        j = (shift + k) % 6

        @pl.when((j == 0) & has_before)
        def _():
            state_on.wait_recv()

        keep = prepare(j)
        at = tile(j, ROWS)

        def group(g):
            stores = []
            for p in [g * GROUP + q for q in range(GROUP)]:
                values = proj[at, tile(12 + p, 128)]
                results = []
                for half in range(2):
                    h = 2 * p + half
                    own = low if half == 0 else jnp.logical_not(low)
                    extended = jnp.where(own, values, jnp.ones_like(values))
                    queries, keys = phi_q[at, tile(h, 128)], phi_k[at, tile(h, 128)]
                    high, rest = high_low(dot_nt(queries, keys) * mask[...])
                    state = states[j, h]
                    state_high, state_low = high_low(state)
                    early = queries * bef[...]
                    results.append(
                        dot_nn(
                            jnp.concatenate([high, rest, early, early], 1),
                            jnp.concatenate([extended, extended, state_high, state_low], 0),
                        )
                    )
                    later = keep * state + dot_tn(keys * trail[...], extended)
                    stores.append((states, (j + 1, h), later))
                top = jnp.where(low, results[0], results[1])
                bottom = pltpu.roll(jnp.where(low, results[1], results[0]), 64, 1)
                share = top / bottom
                here = (at, tile(p, 128))
                stores += [(att_wide, here, share), (den, here, bottom), (att, here, share.astype(BF16))]
            for target, place, value in stores:
                target[place] = value

        loop(PAIRS // GROUP, group)

        @pl.when((j == 5) & has_after)
        def _():
            state_on.start()

    pieces.wait(*meta_moves)
    loop(6, attend)
    put(att, 5)

    def branch_out(k):
        at = tile(k, 256)
        total = dot_nn(att[...], out_w[:, at]) + out_b[:, at].astype(F32)
        res[:, at] = rows[:, at].astype(F32) + total

    weight(1).wait()
    loop(3, branch_out)
    put_done(normed, 6)

    def second_norm(k):
        at = tile(k, 384)
        standard, _ = normalised(res[at, :])
        normed[at, :] = (standard * second_gain[...].astype(F32) + second_shift[...].astype(F32)).astype(BF16)

    loop(2, second_norm)
    put(normed, 4)

    def feed(k):
        at = tile(k, 256)
        hidden = dot_nn(normed[...], up_w[:, at]) + up_b[:, at].astype(F32)
        square = hidden * hidden
        inner = hidden * (0.7978845608028654 + 0.0356774081363 * square)
        bent = jnp.tanh(inner)
        half = 0.5 * (1.0 + bent)
        act[:, at] = (hidden * half).astype(BF16)
        steep = 1.5957691216057308 + 0.2140644489 * square
        slope[:, at] = (half + hidden * half * (1.0 - half) * steep).astype(BF16)

    weight(2).wait()
    loop(12, feed)
    for n in range(4):
        put(act.at[:, pl.ds(n * WIDE, WIDE)], n)

    def settle(k):
        at = tile(k, 256)
        total = res[:, at] + dot_nn(act[...], down_w[:, at]) + down_b[:, at].astype(F32)
        branch[:, at] = total.astype(BF16)

    weight(3).wait()
    loop(3, settle)

    @pl.when(section == 0)
    def _():
        forward_rows.start()
        forward_rows.wait_send()
        backward_rows.wait_recv()

    @pl.when(section == 1)
    def _():
        pieces.wait(*grad_moves)
        copy = pltpu.make_async_copy(branch, ends, out_sem)
        copy.start()
        copy.wait()

    put(grad_in, 7)

    def column_sums(values):
        return jnp.sum(values.astype(F32), 0, keepdims=True)

    small[140:141, :] = column_sums(grad_in[...])

    def feed_back(k):
        at = tile(k, 256)
        grads = dot_nt(grad_in[...], down_w[at, :])
        grads = (grads * slope[:, at].astype(F32)).astype(BF16)
        slope[:, at] = grads

    loop(12, feed_back)
    for n in range(4):
        put(slope.at[:, pl.ds(n * WIDE, WIDE)], 8 + n)
        small[136 + n : 137 + n, :] = column_sums(slope[:, n * WIDE : n * WIDE + WIDE])

    def second_grad(k):
        at = tile(k, 256)
        grad_wide[:, at] = dot_nt(slope[...], up_w[at, :])

    loop(3, second_grad)

    def second_back(k):
        at = tile(k, 384)
        grads = grad_wide[at, :]
        standard, scale = normalised(res[at, :])
        small[134:135, :] += jnp.sum(grads * standard, 0, keepdims=True)
        small[135:136, :] += jnp.sum(grads, 0, keepdims=True)
        grads = norm_input_grad(grads, standard, scale, second_gain[...].astype(F32))
        grads = grad_in[at, :].astype(F32) + grads
        res[at, :] = grads
        rounded = grads.astype(BF16)
        branch[at, :] = rounded
        small[133:134, :] += column_sums(rounded)

    loop(2, second_back)
    put(branch, 12)

    def attended_grad(k):
        at = tile(k, 256)
        grad_wide[:, at] = dot_nt(branch[...], out_w[at, :])

    loop(3, attended_grad)
    for n in range(4):
        put_done(act.at[:, pl.ds(n * WIDE, WIDE)], n)

    put_done(att, 5)
    back_state[...] = jnp.zeros_like(back_state)

    def attend_back(k):
        j = (shift + 5 - k) % 6

        @pl.when(j == 5)
        def _():
            @pl.when(has_after)
            def _():
                state_back.wait_recv()
                back_state[...] = back_in[...]

            @pl.when(jnp.logical_not(has_after))
            def _():
                back_state[...] = jnp.zeros_like(back_state)

        keep = prepare(j)
        at = tile(j, ROWS)

        def group(g):
            stores = []
            for p in [g * GROUP_BACK + q for q in range(GROUP_BACK)]:
                values = proj[at, tile(12 + p, 128)]
                grads = (grad_wide[at, tile(p, 128)] / den[at, tile(p, 128)]).astype(BF16)
                sums = -half_sums(grads.astype(F32) * att_wide[at, tile(p, 128)], low)
                other_sums = pltpu.roll(sums, 64, 1)
                lanes = lax.broadcasted_iota(jnp.int32, (ROWS, 128), 1) % 64
                one = other_sums.astype(BF16).astype(F32)
                two = (other_sums - one).astype(BF16).astype(F32)
                three = other_sums - one - two
                spread = jnp.where(lanes == 0, one, jnp.where(lanes == 1, two, jnp.where(lanes == 2, three, 0.0)))
                spread = spread.astype(BF16)
                value_grads, query_grads, key_grads = [], [], []
                for half in range(2):
                    h = 2 * p + half
                    own = low if half == 0 else jnp.logical_not(low)
                    extended = jnp.where(own, values, jnp.ones_like(values))
                    grads_ext = jnp.where(own, grads, spread)
                    queries, keys = phi_q[at, tile(h, 128)], phi_k[at, tile(h, 128)]
                    high, rest = high_low(dot_nt(grads_ext, extended) * mask[...])
                    state_high, state_low = high_low(states[j, h])
                    query_grad = dot_nn(
                        jnp.concatenate([high, rest], 1), jnp.concatenate([keys, keys], 0)
                    )
                    query_grad += bef[...].astype(F32) * dot_nt(
                        jnp.concatenate([grads_ext, grads_ext], 1),
                        jnp.concatenate([state_high, state_low], 1),
                    )
                    high, rest = high_low(dot_nt(extended, grads_ext) * mask_t[...])
                    later = back_state[h]
                    later_high, later_low = high_low(later)
                    key_grad = dot_nn(
                        jnp.concatenate([high, rest], 1), jnp.concatenate([queries, queries], 0)
                    )
                    key_grad += trail[...].astype(F32) * dot_nt(
                        jnp.concatenate([extended, extended], 1),
                        jnp.concatenate([later_high, later_low], 1),
                    )
                    scores_t = (dot_nt(keys, queries) * mask_t[...]).astype(BF16)
                    value_grads.append(
                        dot_nn(
                            jnp.concatenate([scores_t, keys * trail[...]], 1),
                            jnp.concatenate([grads_ext, later_high], 0),
                        )
                    )
                    stores.append((back_state, h, keep * later + dot_tn(queries * bef[...], grads_ext)))
                    for phi, grad, kept in ((queries, query_grad, query_grads), (keys, key_grad, key_grads)):
                        phi = phi.astype(F32)
                        kept.append(phi * (grad - half_sums(phi * grad, low)))
                value_grad = jnp.where(low, value_grads[0], value_grads[1]).astype(BF16)
                stores.append((act, (at, tile(12 + p, 128)), value_grad))
                for kept, target, first in ((query_grads, act, 18), (key_grads, att, 0)):
                    left = kept[0] - pltpu.roll(kept[0], 64, 1)
                    right = pltpu.roll(kept[1], 64, 1) - kept[1]
                    both = jnp.where(low, left, right).astype(BF16)
                    stores.append((target, (at, tile(first + p, 128)), both))
            for target, place, value in stores:
                target[place] = value

        loop(PAIRS // GROUP_BACK, group)

        @pl.when((j == 0) & has_before)
        def _():
            back_out[...] = back_state[...]
            state_back.start()

    loop(6, attend_back)

    def maps_back(p):
        lanes = tile(p, 128)
        first = lax.broadcasted_iota(jnp.int32, (64, 128), 1) < 64
        for offset, target, source, table, at in ((0, act, 18, pair_q, 0), (6, att, 0, pair_k, 64)):
            logit_grads = target[:, tile(source + p, 128)]
            act[:, tile(offset + p, 128)] = dot_nt(logit_grads, table[p]).astype(BF16)
            product = dot_tn(proj[:, tile(offset + p, 128)], logit_grads)
            small[at : at + 64, lanes] = jnp.where(first, product[:64], product[64:])

    loop(PAIRS, maps_back)
    for n in range(3):
        put(act.at[:, pl.ds(n * WIDE, WIDE)], 13 + n)
        small[130 + n : 131 + n, :] = column_sums(act[:, n * WIDE : n * WIDE + WIDE])

    def first_grad(k):
        at = tile(k, 256)
        grad_wide[:, at] = dot_nt(act[:, : 3 * WIDE], qkv_w[at, :])

    loop(3, first_grad)

    def first_back(k):
        at = tile(k, 384)
        grads = grad_wide[at, :]
        standard, scale = normalised(rows[at, :].astype(F32))
        small[128:129, :] += jnp.sum(grads * standard, 0, keepdims=True)
        small[129:130, :] += jnp.sum(grads, 0, keepdims=True)
        grads = norm_input_grad(grads, standard, scale, first_gain[...].astype(F32))
        rows[at, :] = (res[at, :] + grads).astype(BF16)

    loop(2, first_back)

    @pl.when(section == 1)
    def _():
        backward_rows.start()
        backward_rows.wait_send()

    @pl.when(section == 0)
    def _():
        copy = pltpu.make_async_copy(rows, ends, out_sem)
        copy.start()
        copy.wait()

    put_done(normed, 4)
    put_done(grad_in, 7)
    put_done(branch, 12)
    for n in range(4):
        put_done(slope.at[:, pl.ds(n * WIDE, WIDE)], 8 + n)
    for n in range(3):
        put_done(act.at[:, pl.ds(n * WIDE, WIDE)], 13 + n)

    @pl.when(has_after)
    def _():
        state_on.wait_send()

    @pl.when(has_before)
    def _():
        state_back.wait_send()


def layers(ends_in, begins, filled, weights, mesh):
    tokens = 6 * ROWS
    any_space = pl.BlockSpec(memory_space=pl.ANY)
    in_vmem = pl.BlockSpec(memory_space=pltpu.VMEM)
    large = (2, 6, 10, 12)
    return pl.pallas_call(
        functools.partial(layers_kernel, mesh.shape["ctx"]),
        out_shape=(
            jax.ShapeDtypeStruct((16, tokens, WIDE), BF16),
            jax.ShapeDtypeStruct((tokens, WIDE), BF16),
            jax.ShapeDtypeStruct((256, WIDE), F32),
        ),
        in_specs=[any_space] + [in_vmem] * 2 + [any_space if n in large else in_vmem for n in range(14)],
        out_specs=(any_space, any_space, in_vmem),
        scratch_shapes=[
            pltpu.VMEM((WIDE, 3 * WIDE), BF16),
            pltpu.VMEM((WIDE, WIDE), BF16),
            pltpu.VMEM((WIDE, 4 * WIDE), BF16),
            pltpu.VMEM((4 * WIDE, WIDE), BF16),
            pltpu.VMEM((PAIRS, 128, 256), BF16),
            pltpu.VMEM((PAIRS, 128, 256), BF16),
            pltpu.VMEM((PAIRS, 128, 128), BF16),
            pltpu.VMEM((PAIRS, 128, 128), BF16),
            pltpu.VMEM((6, 8, 128), F32),
            pltpu.VMEM((6, 8, 128), F32),
            pltpu.VMEM((tokens, WIDE), BF16),
            pltpu.VMEM((tokens, WIDE), BF16),
            pltpu.VMEM((tokens, WIDE), BF16),
            pltpu.VMEM((tokens, 3 * WIDE), BF16),
            pltpu.VMEM((tokens, 2 * WIDE), BF16),
            pltpu.VMEM((tokens, 2 * WIDE), BF16),
            pltpu.VMEM((tokens, WIDE), BF16),
            pltpu.VMEM((tokens, WIDE), F32),
            pltpu.VMEM((tokens, WIDE), F32),
            pltpu.VMEM((tokens, WIDE), F32),
            pltpu.VMEM((tokens, 4 * WIDE), BF16),
            pltpu.VMEM((tokens, 4 * WIDE), BF16),
            pltpu.VMEM((7, HEADS, 128, 128), F32),
            pltpu.VMEM((HEADS, 128, 128), F32),
            pltpu.VMEM((HEADS, 128, 128), F32),
            pltpu.VMEM((HEADS, 128, 128), F32),
            pltpu.VMEM((tokens, WIDE), F32),
            pltpu.VMEM((tokens, WIDE), BF16),
            pltpu.VMEM((128, 128), BF16),
            pltpu.VMEM((128, 128), F32),
            pltpu.VMEM((128, 128), F32),
            pltpu.VMEM((128, 128), BF16),
            pltpu.VMEM((128, 128), BF16),
            pltpu.SemaphoreType.DMA((16,)),
            pltpu.SemaphoreType.DMA,
            pltpu.SemaphoreType.DMA((4, 2)),
            pltpu.SemaphoreType.DMA((4,)),
            pltpu.SemaphoreType.DMA((2, 3, 6)),
        ],
        compiler_params=pltpu.CompilerParams(
            collective_id=1, has_side_effects=True, vmem_limit_bytes=60 * 1024 * 1024
        ),
    )(ends_in, begins, filled, *weights)


def body(mesh, ends_in, begins, filled, *weights):
    x, ends, small = layers(ends_in, begins, filled, weights, mesh)
    sums, small, ends = reduced(x, small, ends, mesh)
    return finished(sums, small, ends, weights)


def solution(mesh):
    placed = (
        P("section", None, ("dp", "ctx"), None),
        P(None, ("dp", "ctx")),
        P(None, ("dp", "ctx")),
        P("section", None),
        P("section", None),
        P("section", None, None),
        P("section", None),
        P("section", None, None),
        P("section", None, None),
        P("section", None, None),
        P("section", None),
        P("section", None),
        P("section", None),
        P("section", None, None),
        P("section", None),
        P("section", None, None),
        P("section", None),
    )
    return jax.shard_map(
        functools.partial(body, mesh),
        mesh=mesh,
        in_specs=placed,
        out_specs=(
            P("section", None, ("dp", "ctx"), None),
            P("section", None),
            P("section", None),
            P("section", None, None),
            P("section", None),
            P("section", None, None),
            P("section", None, None),
            P("section", None, None),
            P("section", None),
            P("section", None),
            P("section", None),
            P("section", None, None),
            P("section", None),
            P("section", None, None),
            P("section", None),
        ),
        check_vma=False,
    )
```

```python
import functools

import jax
import jax.numpy as jnp
from jax import lax
from jax.experimental import pallas as pl
from jax.experimental.pallas import tpu as pltpu
from jax.sharding import PartitionSpec as P

BLOCK = 64
ROWS = 128
HEADS = 12
PAIRS = 6
GROUP = 6
GROUP_BACK = 6
EPSILON = 1e-05
F32, BF16 = jnp.float32, jnp.bfloat16

MESH = pl.DeviceIdType.MESH
WIDE = 768
HALF = 384


def bit_length(size):
    return (size - 1).bit_length()


def bit_orders(ctx_size, dp_size):
    ctx_bits = [("ctx", k) for k in range(bit_length(ctx_size))]
    dp_bits = [("dp", k) for k in range(bit_length(dp_size))]

    def interleaved(first, second):
        order = []
        for k in range(max(len(first), len(second))):
            order += first[k : k + 1] + second[k : k + 1]
        return order

    return (interleaved(ctx_bits, dp_bits), interleaved(ctx_bits[::-1], dp_bits))


def halvings(rows, count):
    sizes, halved = [rows], []
    for _ in range(count):
        halved.append(sizes[-1] % 32 == 0)
        sizes.append(sizes[-1] // 2 if halved[-1] else sizes[-1])
    return sizes, halved


class Reduction:
    def __init__(self, rows, orders):
        self.rows, self.orders = rows, orders
        self.count = len(orders[0])
        self.sizes, self.halved = halvings(rows, self.count)
        self.steps = [("rs", s) for s in range(self.count)]
        self.steps += [("ag", s) for s in reversed(range(self.count)) if self.halved[s]]
        self.offsets, self.bits = [], []
        for order in orders:
            offset, offsets, bits = 0, [0], []
            for s, (axis, k) in enumerate(order):
                bit = (lax.axis_index(axis) // (1 << k)) % 2
                bits.append(bit)
                if self.halved[s]:
                    offset = offset + bit * self.sizes[s + 1]
                offsets.append(offset)
            self.offsets.append(offsets)
            self.bits.append(bits)

    def partner(self, part, s):
        axis, k = self.orders[part][s]
        return {axis: lax.axis_index(axis) + (1 << k) * (1 - 2 * self.bits[part][s])}

    def rows_at(self, offset, size):
        if isinstance(offset, int):
            return pl.ds(offset, size)
        return pl.ds(pl.multiple_of(offset, 16), size)

    def copy(self, buffer, whole, received, sems, part, step):
        kind, s = self.steps[step]
        columns = pl.ds(part * HALF, HALF)
        size = self.sizes[s + 1]
        if kind == "rs":
            offset = self.offsets[part][s]
            if self.halved[s]:
                offset = offset + (1 - self.bits[part][s]) * size
            source = buffer.at[self.rows_at(offset, size), columns]
            target = received[s]
        else:
            source = whole.at[self.rows_at(self.offsets[part][s + 1], size), columns]
            target = source
        return pltpu.make_async_remote_copy(
            src_ref=source,
            dst_ref=target,
            send_sem=sems[0],
            recv_sem=sems[1],
            device_id=self.partner(part, s),
            device_id_type=MESH,
        )

    def add(self, buffer, whole, received, part, step):
        kind, s = self.steps[step]
        if kind == "rs":
            size = self.sizes[s + 1]
            rows = self.rows_at(self.offsets[part][s + 1], size)
            columns = pl.ds(part * HALF, HALF)
            total = buffer[rows, columns].astype(jnp.float32) + received[s][...].astype(jnp.float32)
            target = whole if s + 1 == self.count else buffer
            target[rows, columns] = total.astype(jnp.bfloat16)


class Pieces:
    def __init__(self, ctx_size, gather):
        self.size, self.gather, self.me = ctx_size, gather, lax.axis_index("ctx")

    def place(self, k):
        if self.gather:
            at = k * self.size + self.me
            return at // 6, at % 6
        at = 6 * self.me + k
        return at % self.size, at // self.size

    def origin(self, k):
        if self.gather:
            return (6 * self.me + k) % self.size
        return (k * self.size + self.me) // 6

    def start(self, source, target, sems):
        for k in range(6):
            device, at = self.place(k)

            @pl.when(device == self.me)
            def _():
                self.local(source, target, sems, k, at).start()

            @pl.when(device != self.me)
            def _():
                self.remote(source, target, sems, k, at, device).start()

    def wait(self, source, target, sems):
        for k in range(6):
            device, at = self.place(k)

            @pl.when(device == self.me)
            def _():
                self.local(source, target, sems, k, at).wait()

            @pl.when(device != self.me)
            def _():
                self.remote(source, target, sems, k, at, device).wait_send()

            @pl.when(self.origin(k) != self.me)
            def _():
                self.remote(source, target, sems, k, k, (self.me + 1) % self.size).wait_recv()

    def local(self, source, target, sems, k, at):
        return pltpu.make_async_copy(source(k), target(at), sems.at[2, k])

    def remote(self, source, target, sems, k, at, device):
        return pltpu.make_async_remote_copy(
            src_ref=source(k),
            dst_ref=target(at),
            send_sem=sems.at[0, k],
            recv_sem=sems.at[1, at],
            device_id={"ctx": device},
            device_id_type=MESH,
        )


def block_rows(k):
    return pl.ds(k * ROWS if isinstance(k, int) else pl.multiple_of(k * ROWS, ROWS), ROWS)


def greet_ctx(barrier, ctx_size):
    me = lax.axis_index("ctx")

    def greet(k):
        device = {"ctx": (me + 1 + k) % ctx_size}
        pl.semaphore_signal(barrier, inc=1, device_id=device, device_id_type=MESH)

    loop(ctx_size - 1, greet)
    return ctx_size - 1


def reduce_kernel(
    orders, ctx_size, chunks, x_ref, small_ref, ends, sums, small_out, ends_out, *scratch
):
    count = len(orders[0])
    big, big_whole, little, little_whole = scratch[:4]
    scratch = scratch[4:]
    big_recv, little_recv = scratch[:count], scratch[count : 2 * count]
    left, right, send, recv, send_small, recv_small, load, store, moves = scratch[2 * count :]
    large, small = Reduction(WIDE, orders), Reduction(little.shape[0], orders)
    steps = len(large.steps)

    def operands(c):
        left_at = jnp.where(c < 4, c, jnp.where(c < 8, 4, jnp.where(c == 8, 5, 6)))
        right_at = jnp.where(c < 4, 7, c + 4)
        slot = c % 2
        return (
            pltpu.make_async_copy(x_ref.at[left_at], left.at[slot], load.at[slot, 0]),
            pltpu.make_async_copy(x_ref.at[right_at], right.at[slot], load.at[slot, 1]),
        )

    for copy in operands(0):
        copy.start()
    little[...] = small_ref[...].astype(BF16)

    barrier = pltpu.get_barrier_semaphore()
    greeted = greet_ctx(barrier, ctx_size)
    for s in range(count):
        if orders[0][s][0] != "ctx":
            pl.semaphore_signal(barrier, inc=1, device_id=large.partner(0, s), device_id_type=MESH)
            greeted += 1
    pl.semaphore_wait(barrier, greeted)

    def big_copy(c, part, step):
        received = [r.at[c, part] for r in big_recv]
        sems = (send.at[c, part, step], recv.at[c, part, step])
        return large.copy(big.at[c], big_whole.at[c], received, sems, part, step)

    def small_copy(part, step):
        received = [r.at[part] for r in little_recv]
        sems = (send_small.at[part, step], recv_small.at[part, step])
        return small.copy(little, little_whole, received, sems, part, step)

    for part in range(2):
        small_copy(part, 0).start()
    section = lax.axis_index("section")
    pieces = Pieces(ctx_size, False)
    given = (lambda k: ends.at[block_rows(k), :], lambda k: ends_out.at[k], moves)

    def tick(t, carry):
        @pl.when(t < chunks)
        def _():
            for copy in operands(t):
                copy.wait()

            @pl.when(t + 1 < chunks)
            def _():
                for copy in operands(t + 1):
                    copy.start()

            slot = t % 2
            big[t] = dot_tn(left[slot], right[slot]).astype(BF16)
            for part in range(2):
                big_copy(t, part, 0).start()

        @pl.when((t == chunks) & (section == 0))
        def _():
            pieces.start(*given)

        for step in range(steps):
            c = t - 1 - step

            @pl.when((c >= 0) & (c < chunks))
            def _():
                for part in range(2):
                    big_copy(c, part, step).wait()
                    received = [r.at[c, part] for r in big_recv]
                    large.add(big.at[c], big_whole.at[c], received, part, step)
                    if step + 1 < steps:
                        big_copy(c, part, step + 1).start()
                if step + 1 == steps:
                    pltpu.make_async_copy(big_whole.at[c], sums.at[c], store).start()

            if step < len(small.steps):
                @pl.when(t == step)
                def _():
                    for part in range(2):
                        small_copy(part, step).wait()
                        received = [r.at[part] for r in little_recv]
                        small.add(little, little_whole, received, part, step)
                        if step + 1 < len(small.steps):
                            small_copy(part, step + 1).start()

        return carry

    lax.fori_loop(0, chunks + steps, tick, 0)
    small_out[...] = little_whole[...]

    @pl.when(section == 0)
    def _():
        pieces.wait(*given)

    @pl.when(section == 1)
    def _():
        for k in range(6):
            ends_out[k] = ends[block_rows(k), :]

    pltpu.make_async_copy(big_whole, sums, store).wait()


def reduced(x, small, ends, mesh):
    orders = bit_orders(mesh.shape["ctx"], mesh.shape["dp"])
    count, chunks, tokens = len(orders[0]), 12, x.shape[1]
    sizes, _ = halvings(WIDE, count)
    small_rows = small.shape[0]
    small_sizes, small_halved = halvings(small_rows, count)
    steps = count + sum(halvings(WIDE, count)[1])
    small_steps = count + sum(small_halved)
    any_space = pl.BlockSpec(memory_space=pl.ANY)
    in_vmem = pl.BlockSpec(memory_space=pltpu.VMEM)
    return pl.pallas_call(
        functools.partial(reduce_kernel, orders, mesh.shape["ctx"], chunks),
        out_shape=(
            jax.ShapeDtypeStruct((chunks, WIDE, WIDE), BF16),
            jax.ShapeDtypeStruct((small_rows, WIDE), BF16),
            jax.ShapeDtypeStruct((6, ROWS, WIDE), BF16),
        ),
        in_specs=[any_space, in_vmem, in_vmem],
        out_specs=(any_space, in_vmem, in_vmem),
        scratch_shapes=[
            pltpu.VMEM((chunks, WIDE, WIDE), BF16),
            pltpu.VMEM((chunks, WIDE, WIDE), BF16),
            pltpu.VMEM((small_rows, WIDE), BF16),
            pltpu.VMEM((small_rows, WIDE), BF16),
            *(pltpu.VMEM((chunks, 2, size, HALF), BF16) for size in sizes[1:]),
            *(pltpu.VMEM((2, size, HALF), BF16) for size in small_sizes[1:]),
            pltpu.VMEM((2, tokens, WIDE), BF16),
            pltpu.VMEM((2, tokens, WIDE), BF16),
            pltpu.SemaphoreType.DMA((chunks, 2, steps)),
            pltpu.SemaphoreType.DMA((chunks, 2, steps)),
            pltpu.SemaphoreType.DMA((2, small_steps)),
            pltpu.SemaphoreType.DMA((2, small_steps)),
            pltpu.SemaphoreType.DMA((2, 2)),
            pltpu.SemaphoreType.DMA,
            pltpu.SemaphoreType.DMA((3, 6)),
        ],
        compiler_params=pltpu.CompilerParams(
            collective_id=0, has_side_effects=True, vmem_limit_bytes=60 * 1024 * 1024
        ),
    )(x, small, ends)


def finish_kernel(sums, little, ends, *refs):
    outs, (narrow, wide, passing, load, store, through) = refs[:15], refs[15:]
    (
        ends_out, first_gain, first_shift, qkv_w, qkv_b, map_q, map_k, out_w, out_b,
        second_gain, second_shift, up_w, up_b, down_w, down_b,
    ) = outs
    take = pltpu.make_async_copy(ends, passing, through.at[0])
    give = pltpu.make_async_copy(passing, ends_out.at[0], through.at[1])
    take.start()
    depth = narrow.shape[0]
    targets = [down_w.at[0, pl.ds(n * WIDE, WIDE), :] for n in range(4)]
    targets += [up_w.at[0, :, pl.ds(n * WIDE, WIDE)] for n in range(4)]
    targets += [out_w.at[0]]
    targets += [qkv_w.at[0, :, pl.ds(n * WIDE, WIDE)] for n in range(3)]

    def read(c):
        return pltpu.make_async_copy(sums.at[c], narrow.at[c % depth], load.at[c % depth])

    def write(c):
        return pltpu.make_async_copy(wide.at[c % depth], targets[c], store.at[c % depth])

    for c in range(depth):
        read(c).start()
    for target, first in (
        (first_gain, 128), (first_shift, 129), (out_b, 133), (second_gain, 134), (second_shift, 135), (down_b, 140),
    ):
        target[...] = little[first : first + 1, :].astype(F32)
    for target, first, count in ((qkv_b, 130, 3), (up_b, 136, 4)):
        for n in range(count):
            target[:, n * WIDE : n * WIDE + WIDE] = little[first + n : first + n + 1, :].astype(F32)
    map_q[0] = little[0:64, :].astype(F32)
    map_k[0] = little[64:128, :].astype(F32)
    take.wait()
    give.start()
    for c in range(len(targets)):
        read(c).wait()
        if c >= depth:
            write(c - depth).wait()

        def widen(k):
            at = tile(k, 256)
            wide[c % depth, at, :] = narrow[c % depth, at, :].astype(F32)

        loop(3, widen)
        write(c).start()
        if c + depth < len(targets):
            read(c + depth).start()
    for c in range(len(targets) - depth, len(targets)):
        write(c).wait()
    give.wait()


def finished(sums, little, ends, weights):
    any_space = pl.BlockSpec(memory_space=pl.ANY)
    in_vmem = pl.BlockSpec(memory_space=pltpu.VMEM)
    shapes = [jax.ShapeDtypeStruct((1,) + ends.shape, BF16)]
    shapes += [jax.ShapeDtypeStruct(weight.shape, F32) for weight in weights]
    large = (0, 3, 7, 11, 13)
    return pl.pallas_call(
        finish_kernel,
        out_shape=tuple(shapes),
        in_specs=[any_space, in_vmem, any_space],
        out_specs=tuple(any_space if n in large else in_vmem for n in range(15)),
        scratch_shapes=[
            pltpu.VMEM((3, WIDE, WIDE), BF16),
            pltpu.VMEM((3, WIDE, WIDE), F32),
            pltpu.VMEM(ends.shape, BF16),
            pltpu.SemaphoreType.DMA((3,)),
            pltpu.SemaphoreType.DMA((3,)),
            pltpu.SemaphoreType.DMA((2,)),
        ],
        compiler_params=pltpu.CompilerParams(vmem_limit_bytes=60 * 1024 * 1024),
    )(sums, little, ends)


def dot_nn(left, right):
    return jnp.dot(left, right, preferred_element_type=F32)


def dot_nt(left, right):
    return lax.dot_general(left, right, (((1,), (1,)), ((), ())), preferred_element_type=F32)


def dot_tn(left, right):
    return lax.dot_general(left, right, (((0,), (0,)), ((), ())), preferred_element_type=F32)


def high_low(values):
    high = values.astype(BF16)
    return high, (values - high.astype(F32)).astype(BF16)


def tile(index, size):
    return pl.ds(pl.multiple_of(index * size, size), size)


def loop(count, step, unroll=1):
    def body(k, carry):
        step(k)
        return carry

    lax.fori_loop(0, count, body, 0, unroll=unroll)


def low_lanes(rows):
    return lax.broadcasted_iota(jnp.int32, (rows, 128), 1) < 64


def normalised(rows):
    average = jnp.mean(rows, -1, keepdims=True)
    centred = rows - average
    scale = lax.rsqrt(jnp.mean(centred * centred, -1, keepdims=True) + EPSILON)
    return centred * scale, scale


def norm_input_grad(grad, standard, scale, gain):
    wide = grad * gain
    first = jnp.mean(wide, -1, keepdims=True)
    second = jnp.mean(wide * standard, -1, keepdims=True)
    return scale * (wide - first - standard * second)


def half_sums(values, low):
    first = jnp.sum(jnp.where(low, values, 0.0), -1, keepdims=True)
    second = jnp.sum(jnp.where(low, 0.0, values), -1, keepdims=True)
    return jnp.where(low, first, second)


def half_softmax(logits, low, ones):
    lowest = jnp.float32(-3e38)
    first = jnp.max(jnp.where(low, logits, lowest), -1, keepdims=True)
    second = jnp.max(jnp.where(low, lowest, logits), -1, keepdims=True)
    powers = jnp.exp(logits - jnp.where(low, first, second))
    high, rest = high_low(powers)
    return powers / dot_nn(jnp.concatenate([high, rest], 1), jnp.concatenate([ones, ones], 0))


def layers_kernel(ctx_size, *refs):
    (
        x_in, flags, first_gain, first_shift, qkv_given, qkv_b, map_q_given, map_k_given,
        out_given, out_b, second_gain, second_shift, up_given, up_b, down_given, down_b,
        x_out, ends, small,
        qkv_w, out_w, up_w, down_w, map_q, map_k, pair_q, pair_k, meta_own, meta,
        rows, grad_in, normed, proj, phi_q, phi_k, att, att_wide, den, res, act, slope,
        states, pack_in, pack_out, back_state, back_in, back_out, grad_wide, branch,
        ones, mask, mask_t, bef, trail, x_sem, out_sem, remote, weight_sem, moves,
    ) = refs
    section, me = lax.axis_index("section"), lax.axis_index("ctx")
    has_before = (6 * me) % ctx_size != 0
    has_after = (6 * (me + 1)) % ctx_size != 0
    reach = (6 * me + 5) % ctx_size
    shift = jnp.where(reach <= 5, 5 - reach, 0)
    other = {"section": 1 - section}

    def weight(n):
        given, kept = ((qkv_given, qkv_w), (out_given, out_w), (up_given, up_w), (down_given, down_w))[n]
        return pltpu.make_async_copy(given.at[0], kept, weight_sem.at[n])

    def remote_copy(source, target, index, device):
        return pltpu.make_async_remote_copy(
            src_ref=source,
            dst_ref=target,
            send_sem=remote.at[index, 0],
            recv_sem=remote.at[index, 1],
            device_id=device,
            device_id_type=MESH,
        )

    def forward_rows(k):
        at = tile(k, 384)
        return remote_copy(branch.at[at, :], rows.at[at, :], k, other)

    def backward_rows(k):
        at = tile(k, 384)
        return remote_copy(rows.at[at, :], grad_in.at[at, :], 2 + k, other)

    state_on = remote_copy(pack_out, pack_in, 4, {"ctx": me + 1})
    state_back = remote_copy(back_out, back_in, 5, {"ctx": me - 1})
    pieces = Pieces(ctx_size, True)
    rows_moves = (lambda k: x_in.at[0, k], lambda k: rows.at[block_rows(k), :], moves.at[0])
    grad_moves = (lambda k: x_in.at[0, k], lambda k: grad_in.at[block_rows(k), :], moves.at[0])
    back_pieces = Pieces(ctx_size, False)
    ends_moves = (lambda k: branch.at[block_rows(k), :], lambda k: ends.at[block_rows(k), :], moves.at[2])
    meta_moves = (lambda k: meta_own.at[k], lambda k: meta.at[k], moves.at[1])

    barrier = pltpu.get_barrier_semaphore()
    greeted = greet_ctx(barrier, ctx_size)
    pl.semaphore_signal(barrier, inc=1, device_id=other, device_id_type=MESH)
    for k in range(6):
        for n in range(4):
            value = flags[k : k + 1, n : n + 1].astype(F32)
            meta_own[k, n : n + 1, :] = jnp.broadcast_to(value, (1, 128))
    pl.semaphore_wait(barrier, greeted + 1)

    @pl.when(section == 0)
    def _():
        pieces.start(*rows_moves)

    pieces.start(*meta_moves)
    for n in range(4):
        weight(n).start()

    def put(source, index):
        pltpu.make_async_copy(source, x_out.at[index], x_sem.at[index]).start()

    def put_done(source, index):
        pltpu.make_async_copy(source, x_out.at[index], x_sem.at[index]).wait()

    low = low_lanes(ROWS)
    row_of = lax.broadcasted_iota(jnp.int32, (ROWS, 128), 0).astype(F32)
    lane_of = lax.broadcasted_iota(jnp.int32, (ROWS, 128), 1).astype(F32)
    ones[...] = ((row_of < 64) == (lane_of < 64)).astype(BF16)
    small[...] = jnp.zeros_like(small)
    left_lanes = low_lanes(64)
    for given, signed, plain in ((map_q_given, map_q, pair_q), (map_k_given, map_k, pair_k)):
        signed[...] = jnp.zeros_like(signed)
        for p in range(PAIRS):
            both = given[0, :, p * 128 : p * 128 + 128].astype(F32)
            turned = pltpu.roll(both, 64, 1)
            signed[p, :64, :128] = jnp.where(left_lanes, both, -turned).astype(BF16)
            signed[p, 64:, 128:] = jnp.where(left_lanes, turned, -both).astype(BF16)
            plain[p, :64, :] = jnp.where(left_lanes, both, 0.0).astype(BF16)
            plain[p, 64:, :] = jnp.where(left_lanes, 0.0, both).astype(BF16)

    def usable(tokens, filled_first, filled_second):
        return jnp.where(
            tokens < 64, (tokens < filled_first).astype(F32), (tokens - 64 < filled_second).astype(F32)
        )

    def prepare(j):
        start_first, start_second = meta[j, 0:1, :], meta[j, 1:2, :]
        filled_first, filled_second = meta[j, 2:3, :], meta[j, 3:4, :]
        cut = ((row_of >= 64) & (lane_of < 64)).astype(F32) * start_second
        seen = (lane_of <= row_of).astype(F32) * (1.0 - cut)
        mask[...] = seen * usable(lane_of, filled_first, filled_second)
        cut = ((lane_of >= 64) & (row_of < 64)).astype(F32) * start_second
        seen = (row_of <= lane_of).astype(F32) * (1.0 - cut)
        of_rows = usable(row_of, filled_first, filled_second)
        mask_t[...] = seen * of_rows
        kept = 1.0 - start_first
        bef[...] = jnp.where(row_of < 64, kept, kept * (1.0 - start_second)).astype(BF16)
        tail = jnp.where(row_of < 64, 1.0 - start_second, jnp.ones_like(start_second))
        trail[...] = (tail * of_rows).astype(BF16)
        return kept * (1.0 - start_second)

    def pack(source, target):
        sums = jnp.zeros((128, 128), F32)
        for p in range(PAIRS):
            first, second = source(2 * p), source(2 * p + 1)
            target[p] = jnp.where(low, first, second)
            first = jnp.sum(jnp.where(low, 0.0, first), -1, keepdims=True)
            second = jnp.sum(jnp.where(low, second, 0.0), -1, keepdims=True)
            sums = jnp.where(lane_of == 2 * p, first, jnp.where(lane_of == 2 * p + 1, second, sums))
        target[PAIRS] = sums

    def unpack(source, store, share):
        sums = source[PAIRS]
        for p in range(PAIRS):
            both = source[p]
            first = jnp.sum(jnp.where(lane_of == 2 * p, sums, 0.0), -1, keepdims=True)
            second = jnp.sum(jnp.where(lane_of == 2 * p + 1, sums, 0.0), -1, keepdims=True)
            store(2 * p, jnp.where(low, both, first * share))
            store(2 * p + 1, jnp.where(low, second * share, both))

    @pl.when(jnp.logical_not(has_before))
    def _():
        states[0] = jnp.zeros_like(states[0])

    @pl.when(shift != 0)
    def _():
        states[shift] = jnp.zeros_like(states[0])

    @pl.when(section == 0)
    def _():
        pieces.wait(*rows_moves)

    @pl.when(section == 1)
    def _():
        forward_rows(0).wait_recv()
        pieces.start(*grad_moves)

    def first_norm(k):
        @pl.when((section == 1) & (k == 1))
        def _():
            forward_rows(1).wait_recv()

        at = tile(k, 384)
        standard, _ = normalised(rows[at, :].astype(F32))
        normed[at, :] = (standard * first_gain[...].astype(F32) + first_shift[...].astype(F32)).astype(BF16)

    loop(2, first_norm)

    def project(k):
        at = tile(k, 768)
        proj[:, at] = (dot_nn(normed[...], qkv_w[:, at]) + qkv_b[:, at].astype(F32)).astype(BF16)

    weight(0).wait()
    loop(3, project)
    put(normed, 6)

    def features(p):
        low = low_lanes(6 * ROWS)
        for source, table, target in ((0, map_q, phi_q), (6, map_k, phi_k)):
            logits = dot_nn(proj[:, tile(source + p, 128)], table[p])
            for half in range(2):
                phi = half_softmax(logits[:, half * 128 : half * 128 + 128], low, ones[...])
                target[:, tile(2 * p + half, 128)] = phi.astype(BF16)

    loop(PAIRS, features)

    def attend(k):
        j = (shift + k) % 6

        @pl.when((j == 0) & has_before)
        def _():
            state_on.wait_recv()

            def keep_state(h, value):
                states[0, h] = value

            unpack(pack_in, keep_state, 0.015625)

        keep = prepare(j)
        at = tile(j, ROWS)

        def group(g):
            stores = []
            for p in [g * GROUP + q for q in range(GROUP)]:
                values = proj[at, tile(12 + p, 128)]
                results = []
                for half in range(2):
                    h = 2 * p + half
                    own = low if half == 0 else jnp.logical_not(low)
                    extended = jnp.where(own, values, jnp.ones_like(values))
                    queries, keys = phi_q[at, tile(h, 128)], phi_k[at, tile(h, 128)]
                    high, rest = high_low(dot_nt(queries, keys) * mask[...])
                    state = states[j, h]
                    state_high, state_low = high_low(state)
                    early = queries * bef[...]
                    results.append(
                        dot_nn(
                            jnp.concatenate([high, rest, early, early], 1),
                            jnp.concatenate([extended, extended, state_high, state_low], 0),
                        )
                    )
                    later = keep * state + dot_tn(keys * trail[...], extended)
                    stores.append((states, (j + 1, h), later))
                top = jnp.where(low, results[0], results[1])
                bottom = pltpu.roll(jnp.where(low, results[1], results[0]), 64, 1)
                share = top / bottom
                here = (at, tile(p, 128))
                stores += [(att_wide, here, share), (den, here, bottom), (att, here, share.astype(BF16))]
            for target, place, value in stores:
                target[place] = value

        loop(PAIRS // GROUP, group)

        @pl.when((j == 5) & has_after)
        def _():
            pack(lambda h: states[6, h], pack_out)
            state_on.start()

    pieces.wait(*meta_moves)
    loop(6, attend)
    put(att, 5)

    def branch_out(k):
        at = tile(k, 256)
        total = dot_nn(att[...], out_w[:, at]) + out_b[:, at].astype(F32)
        res[:, at] = rows[:, at].astype(F32) + total

    weight(1).wait()
    loop(3, branch_out)
    put_done(normed, 6)

    def second_norm(k):
        at = tile(k, 384)
        standard, _ = normalised(res[at, :])
        normed[at, :] = (standard * second_gain[...].astype(F32) + second_shift[...].astype(F32)).astype(BF16)

    loop(2, second_norm)
    put(normed, 4)

    def feed(k):
        at = tile(k, 256)
        hidden = dot_nn(normed[...], up_w[:, at]) + up_b[:, at].astype(F32)
        square = hidden * hidden
        inner = hidden * (0.7978845608028654 + 0.0356774081363 * square)
        bent = jnp.tanh(inner)
        half = 0.5 * (1.0 + bent)
        act[:, at] = (hidden * half).astype(BF16)
        steep = 1.5957691216057308 + 0.2140644489 * square
        slope[:, at] = (half + hidden * half * (1.0 - half) * steep).astype(BF16)

    weight(2).wait()
    loop(12, feed)
    for n in range(4):
        put(act.at[:, pl.ds(n * WIDE, WIDE)], n)

    def settle(k):
        at = tile(k, 384)
        total = res[at, :] + dot_nn(act[at, :], down_w[...]) + down_b[...].astype(F32)
        branch[at, :] = total.astype(BF16)

        @pl.when(section == 0)
        def _():
            forward_rows(k).start()

    weight(3).wait()
    loop(2, settle)

    @pl.when(section == 0)
    def _():
        for k in range(2):
            forward_rows(k).wait_send()
        for k in range(2):
            backward_rows(k).wait_recv()

    @pl.when(section == 1)
    def _():
        back_pieces.start(*ends_moves)
        pieces.wait(*grad_moves)

    put(grad_in, 7)

    def column_sums(values):
        return jnp.sum(values.astype(F32), 0, keepdims=True)

    small[140:141, :] = column_sums(grad_in[...])

    def feed_back(k):
        at = tile(k, 512)
        grads = dot_nt(grad_in[...], down_w[at, :])
        grads = (grads * slope[:, at].astype(F32)).astype(BF16)
        slope[:, at] = grads

    loop(6, feed_back)
    for n in range(4):
        put(slope.at[:, pl.ds(n * WIDE, WIDE)], 8 + n)
        small[136 + n : 137 + n, :] = column_sums(slope[:, n * WIDE : n * WIDE + WIDE])

    def second_grad(k):
        at = tile(k, 256)
        grad_wide[:, at] = dot_nt(slope[...], up_w[at, :])

    loop(3, second_grad)

    def second_back(k):
        at = tile(k, 384)
        grads = grad_wide[at, :]
        standard, scale = normalised(res[at, :])
        small[134:135, :] += jnp.sum(grads * standard, 0, keepdims=True)
        small[135:136, :] += jnp.sum(grads, 0, keepdims=True)
        grads = norm_input_grad(grads, standard, scale, second_gain[...].astype(F32))
        grads = grad_in[at, :].astype(F32) + grads
        res[at, :] = grads
        rounded = grads.astype(BF16)
        branch[at, :] = rounded
        small[133:134, :] += column_sums(rounded)

    @pl.when(section == 1)
    def _():
        back_pieces.wait(*ends_moves)

    loop(2, second_back)
    put(branch, 12)

    def attended_grad(k):
        at = tile(k, 256)
        grad_wide[:, at] = dot_nt(branch[...], out_w[at, :])

    loop(3, attended_grad)
    for n in range(4):
        put_done(act.at[:, pl.ds(n * WIDE, WIDE)], n)

    put_done(att, 5)
    back_state[...] = jnp.zeros_like(back_state)

    def attend_back(k):
        j = (shift + 5 - k) % 6

        @pl.when(j == 5)
        def _():
            @pl.when(has_after)
            def _():
                state_back.wait_recv()

                def keep_state(h, value):
                    back_state[h] = value

                first_lane = ((lane_of == 0) | (lane_of == 64)).astype(F32)
                unpack(back_in, keep_state, first_lane)

            @pl.when(jnp.logical_not(has_after))
            def _():
                back_state[...] = jnp.zeros_like(back_state)

        keep = prepare(j)
        at = tile(j, ROWS)

        def group(g):
            stores = []
            for p in [g * GROUP_BACK + q for q in range(GROUP_BACK)]:
                values = proj[at, tile(12 + p, 128)]
                grads = (grad_wide[at, tile(p, 128)] / den[at, tile(p, 128)]).astype(BF16)
                sums = -half_sums(grads.astype(F32) * att_wide[at, tile(p, 128)], low)
                other_sums = pltpu.roll(sums, 64, 1)
                lanes = lax.broadcasted_iota(jnp.int32, (ROWS, 128), 1) % 64
                one = other_sums.astype(BF16).astype(F32)
                two = (other_sums - one).astype(BF16).astype(F32)
                three = other_sums - one - two
                spread = jnp.where(lanes == 0, one, jnp.where(lanes == 1, two, jnp.where(lanes == 2, three, 0.0)))
                spread = spread.astype(BF16)
                value_grads, query_grads, key_grads = [], [], []
                for half in range(2):
                    h = 2 * p + half
                    own = low if half == 0 else jnp.logical_not(low)
                    extended = jnp.where(own, values, jnp.ones_like(values))
                    grads_ext = jnp.where(own, grads, spread)
                    queries, keys = phi_q[at, tile(h, 128)], phi_k[at, tile(h, 128)]
                    high, rest = high_low(dot_nt(grads_ext, extended) * mask[...])
                    state_high, state_low = high_low(states[j, h])
                    query_grad = dot_nn(
                        jnp.concatenate([high, rest], 1), jnp.concatenate([keys, keys], 0)
                    )
                    query_grad += bef[...].astype(F32) * dot_nt(
                        jnp.concatenate([grads_ext, grads_ext], 1),
                        jnp.concatenate([state_high, state_low], 1),
                    )
                    high, rest = high_low(dot_nt(extended, grads_ext) * mask_t[...])
                    later = back_state[h]
                    later_high, later_low = high_low(later)
                    key_grad = dot_nn(
                        jnp.concatenate([high, rest], 1), jnp.concatenate([queries, queries], 0)
                    )
                    key_grad += trail[...].astype(F32) * dot_nt(
                        jnp.concatenate([extended, extended], 1),
                        jnp.concatenate([later_high, later_low], 1),
                    )
                    scores_t = (dot_nt(keys, queries) * mask_t[...]).astype(BF16)
                    value_grads.append(
                        dot_nn(
                            jnp.concatenate([scores_t, keys * trail[...]], 1),
                            jnp.concatenate([grads_ext, later_high], 0),
                        )
                    )
                    stores.append((back_state, h, keep * later + dot_tn(queries * bef[...], grads_ext)))
                    for phi, grad, kept in ((queries, query_grad, query_grads), (keys, key_grad, key_grads)):
                        phi = phi.astype(F32)
                        kept.append(phi * (grad - half_sums(phi * grad, low)))
                value_grad = jnp.where(low, value_grads[0], value_grads[1]).astype(BF16)
                stores.append((act, (at, tile(12 + p, 128)), value_grad))
                for kept, target, first in ((query_grads, act, 18), (key_grads, att, 0)):
                    left = kept[0] - pltpu.roll(kept[0], 64, 1)
                    right = pltpu.roll(kept[1], 64, 1) - kept[1]
                    both = jnp.where(low, left, right).astype(BF16)
                    stores.append((target, (at, tile(first + p, 128)), both))
            for target, place, value in stores:
                target[place] = value

        loop(PAIRS // GROUP_BACK, group)

        @pl.when((j == 0) & has_before)
        def _():
            pack(lambda h: back_state[h], back_out)
            state_back.start()

    loop(6, attend_back)

    def maps_back(p):
        lanes = tile(p, 128)
        first = lax.broadcasted_iota(jnp.int32, (64, 128), 1) < 64
        for offset, target, source, table, at in ((0, act, 18, pair_q, 0), (6, att, 0, pair_k, 64)):
            logit_grads = target[:, tile(source + p, 128)]
            act[:, tile(offset + p, 128)] = dot_nt(logit_grads, table[p]).astype(BF16)
            product = dot_tn(proj[:, tile(offset + p, 128)], logit_grads)
            small[at : at + 64, lanes] = jnp.where(first, product[:64], product[64:])

    loop(PAIRS, maps_back)
    for n in range(3):
        put(act.at[:, pl.ds(n * WIDE, WIDE)], 13 + n)
        small[130 + n : 131 + n, :] = column_sums(act[:, n * WIDE : n * WIDE + WIDE])

    def first_grad(k):
        at = tile(k, 256)
        grad_wide[:, at] = dot_nt(act[:, : 3 * WIDE], qkv_w[at, :])

    loop(3, first_grad)

    def first_back(k):
        at = tile(k, 384)
        grads = grad_wide[at, :]
        standard, scale = normalised(rows[at, :].astype(F32))
        small[128:129, :] += jnp.sum(grads * standard, 0, keepdims=True)
        small[129:130, :] += jnp.sum(grads, 0, keepdims=True)
        grads = norm_input_grad(grads, standard, scale, first_gain[...].astype(F32))
        rows[at, :] = (res[at, :] + grads).astype(BF16)

        @pl.when(section == 1)
        def _():
            backward_rows(k).start()

    loop(2, first_back)

    @pl.when(section == 0)
    def _():
        copy = pltpu.make_async_copy(rows, ends, out_sem)
        copy.start()
        copy.wait()

    put_done(normed, 4)
    put_done(grad_in, 7)
    put_done(branch, 12)
    for n in range(4):
        put_done(slope.at[:, pl.ds(n * WIDE, WIDE)], 8 + n)
    for n in range(3):
        put_done(act.at[:, pl.ds(n * WIDE, WIDE)], 13 + n)

    @pl.when(section == 1)
    def _():
        for k in range(2):
            backward_rows(k).wait_send()

    @pl.when(has_after)
    def _():
        state_on.wait_send()

    @pl.when(has_before)
    def _():
        state_back.wait_send()


def layers(ends_in, begins, filled, weights, mesh):
    tokens = 6 * ROWS
    any_space = pl.BlockSpec(memory_space=pl.ANY)
    in_vmem = pl.BlockSpec(memory_space=pltpu.VMEM)
    large = (2, 6, 10, 12)
    return pl.pallas_call(
        functools.partial(layers_kernel, mesh.shape["ctx"]),
        out_shape=(
            jax.ShapeDtypeStruct((16, tokens, WIDE), BF16),
            jax.ShapeDtypeStruct((tokens, WIDE), BF16),
            jax.ShapeDtypeStruct((256, WIDE), F32),
        ),
        in_specs=[any_space, in_vmem] + [any_space if n in large else in_vmem for n in range(14)],
        out_specs=(any_space, any_space, in_vmem),
        scratch_shapes=[
            pltpu.VMEM((WIDE, 3 * WIDE), BF16),
            pltpu.VMEM((WIDE, WIDE), BF16),
            pltpu.VMEM((WIDE, 4 * WIDE), BF16),
            pltpu.VMEM((4 * WIDE, WIDE), BF16),
            pltpu.VMEM((PAIRS, 128, 256), BF16),
            pltpu.VMEM((PAIRS, 128, 256), BF16),
            pltpu.VMEM((PAIRS, 128, 128), BF16),
            pltpu.VMEM((PAIRS, 128, 128), BF16),
            pltpu.VMEM((6, 8, 128), F32),
            pltpu.VMEM((6, 8, 128), F32),
            pltpu.VMEM((tokens, WIDE), BF16),
            pltpu.VMEM((tokens, WIDE), BF16),
            pltpu.VMEM((tokens, WIDE), BF16),
            pltpu.VMEM((tokens, 3 * WIDE), BF16),
            pltpu.VMEM((tokens, 2 * WIDE), BF16),
            pltpu.VMEM((tokens, 2 * WIDE), BF16),
            pltpu.VMEM((tokens, WIDE), BF16),
            pltpu.VMEM((tokens, WIDE), F32),
            pltpu.VMEM((tokens, WIDE), F32),
            pltpu.VMEM((tokens, WIDE), F32),
            pltpu.VMEM((tokens, 4 * WIDE), BF16),
            pltpu.VMEM((tokens, 4 * WIDE), BF16),
            pltpu.VMEM((7, HEADS, 128, 128), F32),
            pltpu.VMEM((PAIRS + 1, 128, 128), F32),
            pltpu.VMEM((PAIRS + 1, 128, 128), F32),
            pltpu.VMEM((HEADS, 128, 128), F32),
            pltpu.VMEM((PAIRS + 1, 128, 128), F32),
            pltpu.VMEM((PAIRS + 1, 128, 128), F32),
            pltpu.VMEM((tokens, WIDE), F32),
            pltpu.VMEM((tokens, WIDE), BF16),
            pltpu.VMEM((128, 128), BF16),
            pltpu.VMEM((128, 128), F32),
            pltpu.VMEM((128, 128), F32),
            pltpu.VMEM((128, 128), BF16),
            pltpu.VMEM((128, 128), BF16),
            pltpu.SemaphoreType.DMA((16,)),
            pltpu.SemaphoreType.DMA,
            pltpu.SemaphoreType.DMA((6, 2)),
            pltpu.SemaphoreType.DMA((4,)),
            pltpu.SemaphoreType.DMA((3, 3, 6)),
        ],
        compiler_params=pltpu.CompilerParams(
            collective_id=1, has_side_effects=True, vmem_limit_bytes=60 * 1024 * 1024
        ),
    )(ends_in, jnp.concatenate([begins, filled], 1), *weights)


def body(mesh, ends_in, begins, filled, *weights):
    x, ends, small = layers(ends_in, begins, filled, weights, mesh)
    sums, small, ends = reduced(x, small, ends, mesh)
    return finished(sums, small, ends, weights)


def solution(mesh):
    placed = (
        P("section", None, ("dp", "ctx"), None),
        P(None, ("dp", "ctx")),
        P(None, ("dp", "ctx")),
        P("section", None),
        P("section", None),
        P("section", None, None),
        P("section", None),
        P("section", None, None),
        P("section", None, None),
        P("section", None, None),
        P("section", None),
        P("section", None),
        P("section", None),
        P("section", None, None),
        P("section", None),
        P("section", None, None),
        P("section", None),
    )
    return jax.shard_map(
        functools.partial(body, mesh),
        mesh=mesh,
        in_specs=placed,
        out_specs=(
            P("section", None, ("dp", "ctx"), None),
            P("section", None),
            P("section", None),
            P("section", None, None),
            P("section", None),
            P("section", None, None),
            P("section", None, None),
            P("section", None, None),
            P("section", None),
            P("section", None),
            P("section", None),
            P("section", None, None),
            P("section", None),
            P("section", None, None),
            P("section", None),
        ),
        check_vma=False,
    )
```

```python
import functools

import jax
import jax.numpy as jnp
from jax import lax
from jax.experimental import pallas as pl
from jax.experimental.pallas import tpu as pltpu
from jax.sharding import PartitionSpec as P

BLOCK = 64
ROWS = 128
HEADS = 12
PAIRS = 6
GROUP = 6
GROUP_BACK = 6
EPSILON = 1e-05
F32, BF16 = jnp.float32, jnp.bfloat16

MESH = pl.DeviceIdType.MESH
WIDE = 768
HALF = 384


def bit_length(size):
    return (size - 1).bit_length()


def bit_orders(ctx_size, dp_size):
    ctx_bits = [("ctx", k) for k in range(bit_length(ctx_size))]
    dp_bits = [("dp", k) for k in range(bit_length(dp_size))]

    def interleaved(first, second):
        order = []
        for k in range(max(len(first), len(second))):
            order += first[k : k + 1] + second[k : k + 1]
        return order

    return (interleaved(ctx_bits, dp_bits), interleaved(ctx_bits[::-1], dp_bits))


def halvings(rows, count):
    sizes, halved = [rows], []
    for _ in range(count):
        halved.append(sizes[-1] % 32 == 0)
        sizes.append(sizes[-1] // 2 if halved[-1] else sizes[-1])
    return sizes, halved


class Reduction:
    def __init__(self, rows, orders):
        self.rows, self.orders = rows, orders
        self.count = len(orders[0])
        self.sizes, self.halved = halvings(rows, self.count)
        self.steps = [("rs", s) for s in range(self.count)]
        self.steps += [("ag", s) for s in reversed(range(self.count)) if self.halved[s]]
        self.offsets, self.bits = [], []
        for order in orders:
            offset, offsets, bits = 0, [0], []
            for s, (axis, k) in enumerate(order):
                bit = (lax.axis_index(axis) // (1 << k)) % 2
                bits.append(bit)
                if self.halved[s]:
                    offset = offset + bit * self.sizes[s + 1]
                offsets.append(offset)
            self.offsets.append(offsets)
            self.bits.append(bits)

    def partner(self, part, s):
        axis, k = self.orders[part][s]
        return {axis: lax.axis_index(axis) + (1 << k) * (1 - 2 * self.bits[part][s])}

    def rows_at(self, offset, size):
        if isinstance(offset, int):
            return pl.ds(offset, size)
        return pl.ds(pl.multiple_of(offset, 16), size)

    def copy(self, buffer, whole, received, sems, part, step):
        kind, s = self.steps[step]
        columns = pl.ds(part * HALF, HALF)
        size = self.sizes[s + 1]
        if kind == "rs":
            offset = self.offsets[part][s]
            if self.halved[s]:
                offset = offset + (1 - self.bits[part][s]) * size
            source = buffer.at[self.rows_at(offset, size), columns]
            target = received[s]
        else:
            source = whole.at[self.rows_at(self.offsets[part][s + 1], size), columns]
            target = source
        return pltpu.make_async_remote_copy(
            src_ref=source,
            dst_ref=target,
            send_sem=sems[0],
            recv_sem=sems[1],
            device_id=self.partner(part, s),
            device_id_type=MESH,
        )

    def add(self, buffer, whole, received, part, step):
        kind, s = self.steps[step]
        if kind == "rs":
            size = self.sizes[s + 1]
            rows = self.rows_at(self.offsets[part][s + 1], size)
            columns = pl.ds(part * HALF, HALF)
            total = buffer[rows, columns].astype(jnp.float32) + received[s][...].astype(jnp.float32)
            target = whole if s + 1 == self.count else buffer
            target[rows, columns] = total.astype(jnp.bfloat16)


class Pieces:
    def __init__(self, ctx_size, gather):
        self.size, self.gather, self.me = ctx_size, gather, lax.axis_index("ctx")

    def place(self, k):
        if self.gather:
            at = k * self.size + self.me
            return at // 6, at % 6
        at = 6 * self.me + k
        return at % self.size, at // self.size

    def origin(self, k):
        if self.gather:
            return (6 * self.me + k) % self.size
        return (k * self.size + self.me) // 6

    def start(self, source, target, sems):
        for k in range(6):
            device, at = self.place(k)

            @pl.when(device == self.me)
            def _():
                self.local(source, target, sems, k, at).start()

            @pl.when(device != self.me)
            def _():
                self.remote(source, target, sems, k, at, device).start()

    def wait(self, source, target, sems):
        for k in range(6):
            device, at = self.place(k)

            @pl.when(device == self.me)
            def _():
                self.local(source, target, sems, k, at).wait()

            @pl.when(device != self.me)
            def _():
                self.remote(source, target, sems, k, at, device).wait_send()

            @pl.when(self.origin(k) != self.me)
            def _():
                self.remote(source, target, sems, k, k, (self.me + 1) % self.size).wait_recv()

    def local(self, source, target, sems, k, at):
        return pltpu.make_async_copy(source(k), target(at), sems.at[2, k])

    def remote(self, source, target, sems, k, at, device):
        return pltpu.make_async_remote_copy(
            src_ref=source(k),
            dst_ref=target(at),
            send_sem=sems.at[0, k],
            recv_sem=sems.at[1, at],
            device_id={"ctx": device},
            device_id_type=MESH,
        )


def block_rows(k):
    return pl.ds(k * ROWS if isinstance(k, int) else pl.multiple_of(k * ROWS, ROWS), ROWS)


def greet_ctx(barrier, ctx_size):
    me = lax.axis_index("ctx")

    def greet(k):
        device = {"ctx": (me + 1 + k) % ctx_size}
        pl.semaphore_signal(barrier, inc=1, device_id=device, device_id_type=MESH)

    loop(ctx_size - 1, greet)
    return ctx_size - 1


def reduce_kernel(
    orders, ctx_size, chunks, x_ref, small_ref, ends, sums, small_out, ends_out, *scratch
):
    count = len(orders[0])
    big, big_whole, little, little_whole = scratch[:4]
    scratch = scratch[4:]
    big_recv, little_recv = scratch[:count], scratch[count : 2 * count]
    left, right, send, recv, send_small, recv_small, load, store, moves = scratch[2 * count :]
    large, small = Reduction(WIDE, orders), Reduction(little.shape[0], orders)
    steps = len(large.steps)

    def operands(c):
        left_at = jnp.where(c < 4, c, jnp.where(c < 8, 4, jnp.where(c == 8, 5, 6)))
        right_at = jnp.where(c < 4, 7, c + 4)
        slot = c % 2
        return (
            pltpu.make_async_copy(x_ref.at[left_at], left.at[slot], load.at[slot, 0]),
            pltpu.make_async_copy(x_ref.at[right_at], right.at[slot], load.at[slot, 1]),
        )

    for copy in operands(0):
        copy.start()
    little[...] = small_ref[...].astype(BF16)

    barrier = pltpu.get_barrier_semaphore()
    greeted = greet_ctx(barrier, ctx_size)
    for s in range(count):
        if orders[0][s][0] != "ctx":
            pl.semaphore_signal(barrier, inc=1, device_id=large.partner(0, s), device_id_type=MESH)
            greeted += 1
    pl.semaphore_wait(barrier, greeted)

    def big_copy(c, part, step):
        received = [r.at[c, part] for r in big_recv]
        sems = (send.at[c, part, step], recv.at[c, part, step])
        return large.copy(big.at[c], big_whole.at[c], received, sems, part, step)

    def small_copy(part, step):
        received = [r.at[part] for r in little_recv]
        sems = (send_small.at[part, step], recv_small.at[part, step])
        return small.copy(little, little_whole, received, sems, part, step)

    for part in range(2):
        small_copy(part, 0).start()
    section = lax.axis_index("section")
    pieces = Pieces(ctx_size, False)
    given = (lambda k: ends.at[block_rows(k), :], lambda k: ends_out.at[k], moves)

    def tick(t, carry):
        @pl.when(t < chunks)
        def _():
            for copy in operands(t):
                copy.wait()

            @pl.when(t + 1 < chunks)
            def _():
                for copy in operands(t + 1):
                    copy.start()

            slot = t % 2
            big[t] = dot_tn(left[slot], right[slot]).astype(BF16)
            for part in range(2):
                big_copy(t, part, 0).start()

        @pl.when((t == chunks) & (section == 0))
        def _():
            pieces.start(*given)

        for step in range(steps):
            c = t - 1 - step

            @pl.when((c >= 0) & (c < chunks))
            def _():
                for part in range(2):
                    big_copy(c, part, step).wait()
                    received = [r.at[c, part] for r in big_recv]
                    large.add(big.at[c], big_whole.at[c], received, part, step)
                    if step + 1 < steps:
                        big_copy(c, part, step + 1).start()
                if step + 1 == steps:
                    pltpu.make_async_copy(big_whole.at[c], sums.at[c], store).start()

            if step < len(small.steps):
                @pl.when(t == step)
                def _():
                    for part in range(2):
                        small_copy(part, step).wait()
                        received = [r.at[part] for r in little_recv]
                        small.add(little, little_whole, received, part, step)
                        if step + 1 < len(small.steps):
                            small_copy(part, step + 1).start()

        return carry

    lax.fori_loop(0, chunks + steps, tick, 0)
    small_out[...] = little_whole[...]

    @pl.when(section == 0)
    def _():
        pieces.wait(*given)

    @pl.when(section == 1)
    def _():
        for k in range(6):
            ends_out[k] = ends[block_rows(k), :]

    pltpu.make_async_copy(big_whole, sums, store).wait()


def reduced(x, small, ends, mesh):
    orders = bit_orders(mesh.shape["ctx"], mesh.shape["dp"])
    count, chunks, tokens = len(orders[0]), 12, x.shape[1]
    sizes, _ = halvings(WIDE, count)
    small_rows = small.shape[0]
    small_sizes, small_halved = halvings(small_rows, count)
    steps = count + sum(halvings(WIDE, count)[1])
    small_steps = count + sum(small_halved)
    any_space = pl.BlockSpec(memory_space=pl.ANY)
    in_vmem = pl.BlockSpec(memory_space=pltpu.VMEM)
    return pl.pallas_call(
        functools.partial(reduce_kernel, orders, mesh.shape["ctx"], chunks),
        out_shape=(
            jax.ShapeDtypeStruct((chunks, WIDE, WIDE), BF16),
            jax.ShapeDtypeStruct((small_rows, WIDE), BF16),
            jax.ShapeDtypeStruct((6, ROWS, WIDE), BF16),
        ),
        in_specs=[any_space, in_vmem, in_vmem],
        out_specs=(any_space, in_vmem, in_vmem),
        scratch_shapes=[
            pltpu.VMEM((chunks, WIDE, WIDE), BF16),
            pltpu.VMEM((chunks, WIDE, WIDE), BF16),
            pltpu.VMEM((small_rows, WIDE), BF16),
            pltpu.VMEM((small_rows, WIDE), BF16),
            *(pltpu.VMEM((chunks, 2, size, HALF), BF16) for size in sizes[1:]),
            *(pltpu.VMEM((2, size, HALF), BF16) for size in small_sizes[1:]),
            pltpu.VMEM((2, tokens, WIDE), BF16),
            pltpu.VMEM((2, tokens, WIDE), BF16),
            pltpu.SemaphoreType.DMA((chunks, 2, steps)),
            pltpu.SemaphoreType.DMA((chunks, 2, steps)),
            pltpu.SemaphoreType.DMA((2, small_steps)),
            pltpu.SemaphoreType.DMA((2, small_steps)),
            pltpu.SemaphoreType.DMA((2, 2)),
            pltpu.SemaphoreType.DMA,
            pltpu.SemaphoreType.DMA((3, 6)),
        ],
        compiler_params=pltpu.CompilerParams(
            collective_id=0, has_side_effects=True, vmem_limit_bytes=60 * 1024 * 1024
        ),
    )(x, small, ends)


def finish_kernel(sums, little, ends, *refs):
    outs, (narrow, wide, passing, load, store, through) = refs[:15], refs[15:]
    (
        ends_out, first_gain, first_shift, qkv_w, qkv_b, map_q, map_k, out_w, out_b,
        second_gain, second_shift, up_w, up_b, down_w, down_b,
    ) = outs
    take = pltpu.make_async_copy(ends, passing, through.at[0])
    give = pltpu.make_async_copy(passing, ends_out.at[0], through.at[1])
    take.start()
    depth = narrow.shape[0]
    targets = [down_w.at[0, pl.ds(n * WIDE, WIDE), :] for n in range(4)]
    targets += [up_w.at[0, :, pl.ds(n * WIDE, WIDE)] for n in range(4)]
    targets += [out_w.at[0]]
    targets += [qkv_w.at[0, :, pl.ds(n * WIDE, WIDE)] for n in range(3)]

    def read(c):
        return pltpu.make_async_copy(sums.at[c], narrow.at[c % depth], load.at[c % depth])

    def write(c):
        return pltpu.make_async_copy(wide.at[c % depth], targets[c], store.at[c % depth])

    for c in range(depth):
        read(c).start()
    for target, first in (
        (first_gain, 128), (first_shift, 129), (out_b, 133), (second_gain, 134), (second_shift, 135), (down_b, 140),
    ):
        target[...] = little[first : first + 1, :].astype(F32)
    for target, first, count in ((qkv_b, 130, 3), (up_b, 136, 4)):
        for n in range(count):
            target[:, n * WIDE : n * WIDE + WIDE] = little[first + n : first + n + 1, :].astype(F32)
    map_q[0] = little[0:64, :].astype(F32)
    map_k[0] = little[64:128, :].astype(F32)
    take.wait()
    give.start()
    for c in range(len(targets)):
        read(c).wait()
        if c >= depth:
            write(c - depth).wait()

        def widen(k):
            at = tile(k, 256)
            wide[c % depth, at, :] = narrow[c % depth, at, :].astype(F32)

        loop(3, widen)
        write(c).start()
        if c + depth < len(targets):
            read(c + depth).start()
    for c in range(len(targets) - depth, len(targets)):
        write(c).wait()
    give.wait()


def finished(sums, little, ends, weights):
    any_space = pl.BlockSpec(memory_space=pl.ANY)
    in_vmem = pl.BlockSpec(memory_space=pltpu.VMEM)
    shapes = [jax.ShapeDtypeStruct((1,) + ends.shape, BF16)]
    shapes += [jax.ShapeDtypeStruct(weight.shape, F32) for weight in weights]
    large = (0, 3, 7, 11, 13)
    return pl.pallas_call(
        finish_kernel,
        out_shape=tuple(shapes),
        in_specs=[any_space, in_vmem, any_space],
        out_specs=tuple(any_space if n in large else in_vmem for n in range(15)),
        scratch_shapes=[
            pltpu.VMEM((3, WIDE, WIDE), BF16),
            pltpu.VMEM((3, WIDE, WIDE), F32),
            pltpu.VMEM(ends.shape, BF16),
            pltpu.SemaphoreType.DMA((3,)),
            pltpu.SemaphoreType.DMA((3,)),
            pltpu.SemaphoreType.DMA((2,)),
        ],
        compiler_params=pltpu.CompilerParams(vmem_limit_bytes=60 * 1024 * 1024),
    )(sums, little, ends)


def dot_nn(left, right):
    return jnp.dot(left, right, preferred_element_type=F32)


def dot_nt(left, right):
    return lax.dot_general(left, right, (((1,), (1,)), ((), ())), preferred_element_type=F32)


def dot_tn(left, right):
    return lax.dot_general(left, right, (((0,), (0,)), ((), ())), preferred_element_type=F32)


def high_low(values):
    high = values.astype(BF16)
    return high, (values - high.astype(F32)).astype(BF16)


def tile(index, size):
    return pl.ds(pl.multiple_of(index * size, size), size)


def loop(count, step, unroll=1):
    def body(k, carry):
        step(k)
        return carry

    lax.fori_loop(0, count, body, 0, unroll=unroll)


def low_lanes(rows):
    return lax.broadcasted_iota(jnp.int32, (rows, 128), 1) < 64


def normalised(rows):
    average = jnp.mean(rows, -1, keepdims=True)
    centred = rows - average
    scale = lax.rsqrt(jnp.mean(centred * centred, -1, keepdims=True) + EPSILON)
    return centred * scale, scale


def norm_input_grad(grad, standard, scale, gain):
    wide = grad * gain
    first = jnp.mean(wide, -1, keepdims=True)
    second = jnp.mean(wide * standard, -1, keepdims=True)
    return scale * (wide - first - standard * second)


def half_sums(values, low):
    first = jnp.sum(jnp.where(low, values, 0.0), -1, keepdims=True)
    second = jnp.sum(jnp.where(low, 0.0, values), -1, keepdims=True)
    return jnp.where(low, first, second)


def half_softmax(logits, low, ones):
    lowest = jnp.float32(-3e38)
    first = jnp.max(jnp.where(low, logits, lowest), -1, keepdims=True)
    second = jnp.max(jnp.where(low, lowest, logits), -1, keepdims=True)
    powers = jnp.exp(logits - jnp.where(low, first, second))
    high, rest = high_low(powers)
    return powers / dot_nn(jnp.concatenate([high, rest], 1), jnp.concatenate([ones, ones], 0))


def layers_kernel(ctx_size, *refs):
    (
        x_in, flags, first_gain, first_shift, qkv_given, qkv_b, map_q_given, map_k_given,
        out_given, out_b, second_gain, second_shift, up_given, up_b, down_given, down_b,
        x_out, ends, small,
        qkv_w, out_w, up_w, down_w, map_q, map_k, pair_q, pair_k, meta_own, meta,
        rows, grad_in, normed, proj, phi_q, phi_k, att, att_wide, den, res, act, slope,
        states, pack_in, pack_out, back_state, back_in, grad_wide, branch, branch_grad,
        ones, mask, mask_t, bef, trail, x_sem, out_sem, remote, weight_sem, moves,
    ) = refs
    section, me = lax.axis_index("section"), lax.axis_index("ctx")
    has_before = (6 * me) % ctx_size != 0
    has_after = (6 * (me + 1)) % ctx_size != 0
    reach = (6 * me + 5) % ctx_size
    shift = jnp.where(reach <= 5, 5 - reach, 0)
    other = {"section": 1 - section}

    def weight(n):
        given, kept = ((qkv_given, qkv_w), (out_given, out_w), (up_given, up_w), (down_given, down_w))[n]
        return pltpu.make_async_copy(given.at[0], kept, weight_sem.at[n])

    def remote_copy(source, target, index, device):
        return pltpu.make_async_remote_copy(
            src_ref=source,
            dst_ref=target,
            send_sem=remote.at[index, 0],
            recv_sem=remote.at[index, 1],
            device_id=device,
            device_id_type=MESH,
        )

    def forward_rows(k):
        at = tile(k, 384)
        return remote_copy(branch.at[at, :], rows.at[at, :], k, other)

    def backward_rows(k):
        at = tile(k, 384)
        return remote_copy(rows.at[at, :], grad_in.at[at, :], 2 + k, other)

    state_on = remote_copy(pack_out, pack_in, 4, {"ctx": me + 1})
    state_back = remote_copy(pack_out, back_in, 5, {"ctx": me - 1})
    pieces = Pieces(ctx_size, True)
    rows_moves = (lambda k: x_in.at[0, k], lambda k: rows.at[block_rows(k), :], moves.at[0])
    grad_moves = (lambda k: x_in.at[0, k], lambda k: grad_in.at[block_rows(k), :], moves.at[0])
    back_pieces = Pieces(ctx_size, False)
    ends_moves = (lambda k: branch.at[block_rows(k), :], lambda k: ends.at[block_rows(k), :], moves.at[2])
    meta_moves = (lambda k: meta_own.at[k], lambda k: meta.at[k], moves.at[1])

    barrier = pltpu.get_barrier_semaphore()
    greeted = greet_ctx(barrier, ctx_size)
    pl.semaphore_signal(barrier, inc=1, device_id=other, device_id_type=MESH)
    for k in range(6):
        for n in range(4):
            value = flags[k : k + 1, n : n + 1].astype(F32)
            meta_own[k, n : n + 1, :] = jnp.broadcast_to(value, (1, 128))
    pl.semaphore_wait(barrier, greeted + 1)

    @pl.when(section == 0)
    def _():
        pieces.start(*rows_moves)

    pieces.start(*meta_moves)
    for n in range(4):
        weight(n).start()

    def put(source, index):
        pltpu.make_async_copy(source, x_out.at[index], x_sem.at[index]).start()

    def put_done(source, index):
        pltpu.make_async_copy(source, x_out.at[index], x_sem.at[index]).wait()

    low = low_lanes(ROWS)
    row_of = lax.broadcasted_iota(jnp.int32, (ROWS, 128), 0).astype(F32)
    lane_of = lax.broadcasted_iota(jnp.int32, (ROWS, 128), 1).astype(F32)
    ones[...] = ((row_of < 64) == (lane_of < 64)).astype(BF16)
    small[...] = jnp.zeros_like(small)
    left_lanes = low_lanes(64)
    for given, signed, plain in ((map_q_given, map_q, pair_q), (map_k_given, map_k, pair_k)):
        signed[...] = jnp.zeros_like(signed)
        for p in range(PAIRS):
            both = given[0, :, p * 128 : p * 128 + 128].astype(F32)
            turned = pltpu.roll(both, 64, 1)
            signed[p, :64, :128] = jnp.where(left_lanes, both, -turned).astype(BF16)
            signed[p, 64:, 128:] = jnp.where(left_lanes, turned, -both).astype(BF16)
            plain[p, :64, :] = jnp.where(left_lanes, both, 0.0).astype(BF16)
            plain[p, 64:, :] = jnp.where(left_lanes, 0.0, both).astype(BF16)

    def usable(tokens, filled_first, filled_second):
        return jnp.where(
            tokens < 64, (tokens < filled_first).astype(F32), (tokens - 64 < filled_second).astype(F32)
        )

    def prepare(j):
        start_first, start_second = meta[j, 0:1, :], meta[j, 1:2, :]
        filled_first, filled_second = meta[j, 2:3, :], meta[j, 3:4, :]
        cut = ((row_of >= 64) & (lane_of < 64)).astype(F32) * start_second
        seen = (lane_of <= row_of).astype(F32) * (1.0 - cut)
        mask[...] = seen * usable(lane_of, filled_first, filled_second)
        cut = ((lane_of >= 64) & (row_of < 64)).astype(F32) * start_second
        seen = (row_of <= lane_of).astype(F32) * (1.0 - cut)
        of_rows = usable(row_of, filled_first, filled_second)
        mask_t[...] = seen * of_rows
        kept = 1.0 - start_first
        bef[...] = jnp.where(row_of < 64, kept, kept * (1.0 - start_second)).astype(BF16)
        tail = jnp.where(row_of < 64, 1.0 - start_second, jnp.ones_like(start_second))
        trail[...] = (tail * of_rows).astype(BF16)
        return kept * (1.0 - start_second)

    def pack(source, target):
        sums = jnp.zeros((128, 128), F32)
        for p in range(PAIRS):
            first, second = source(2 * p), source(2 * p + 1)
            target[p] = jnp.where(low, first, second)
            first = jnp.sum(jnp.where(low, 0.0, first), -1, keepdims=True)
            second = jnp.sum(jnp.where(low, second, 0.0), -1, keepdims=True)
            sums = jnp.where(lane_of == 2 * p, first, jnp.where(lane_of == 2 * p + 1, second, sums))
        target[PAIRS] = sums

    def unpack(source, store, share):
        sums = source[PAIRS]
        for p in range(PAIRS):
            both = source[p]
            first = jnp.sum(jnp.where(lane_of == 2 * p, sums, 0.0), -1, keepdims=True)
            second = jnp.sum(jnp.where(lane_of == 2 * p + 1, sums, 0.0), -1, keepdims=True)
            store(2 * p, jnp.where(low, both, first * share))
            store(2 * p + 1, jnp.where(low, second * share, both))

    @pl.when(jnp.logical_not(has_before))
    def _():
        states[0] = jnp.zeros_like(states[0])

    @pl.when(shift != 0)
    def _():
        states[shift] = jnp.zeros_like(states[0])

    @pl.when(section == 0)
    def _():
        pieces.wait(*rows_moves)

    @pl.when(section == 1)
    def _():
        forward_rows(0).wait_recv()
        pieces.start(*grad_moves)

    def first_norm(k):
        @pl.when((section == 1) & (k == 1))
        def _():
            forward_rows(1).wait_recv()

        at = tile(k, 384)
        standard, _ = normalised(rows[at, :].astype(F32))
        normed[at, :] = (standard * first_gain[...].astype(F32) + first_shift[...].astype(F32)).astype(BF16)

    loop(2, first_norm)

    def project(k):
        at = tile(k, 768)
        proj[:, at] = (dot_nn(normed[...], qkv_w[:, at]) + qkv_b[:, at].astype(F32)).astype(BF16)

    weight(0).wait()
    loop(3, project)
    put(normed, 6)

    def features(p):
        low = low_lanes(6 * ROWS)
        for source, table, target in ((0, map_q, phi_q), (6, map_k, phi_k)):
            logits = dot_nn(proj[:, tile(source + p, 128)], table[p])
            for half in range(2):
                phi = half_softmax(logits[:, half * 128 : half * 128 + 128], low, ones[...])
                target[:, tile(2 * p + half, 128)] = phi.astype(BF16)

    loop(PAIRS, features)

    def attend(k):
        j = (shift + k) % 6

        @pl.when((j == 0) & has_before)
        def _():
            state_on.wait_recv()

            def keep_state(h, value):
                states[0, h] = value

            unpack(pack_in, keep_state, 0.015625)

        keep = prepare(j)
        at = tile(j, ROWS)

        def group(g):
            stores = []
            for p in [g * GROUP + q for q in range(GROUP)]:
                values = proj[at, tile(12 + p, 128)]
                results = []
                for half in range(2):
                    h = 2 * p + half
                    own = low if half == 0 else jnp.logical_not(low)
                    extended = jnp.where(own, values, jnp.ones_like(values))
                    queries, keys = phi_q[at, tile(h, 128)], phi_k[at, tile(h, 128)]
                    high, rest = high_low(dot_nt(queries, keys) * mask[...])
                    state = states[j, h]
                    state_high, state_low = high_low(state)
                    early = queries * bef[...]
                    results.append(
                        dot_nn(
                            jnp.concatenate([high, rest, early, early], 1),
                            jnp.concatenate([extended, extended, state_high, state_low], 0),
                        )
                    )
                    later = keep * state + dot_tn(keys * trail[...], extended)
                    stores.append((states, (j + 1, h), later))
                top = jnp.where(low, results[0], results[1])
                bottom = pltpu.roll(jnp.where(low, results[1], results[0]), 64, 1)
                share = top / bottom
                here = (at, tile(p, 128))
                stores += [(att_wide, here, share), (den, here, bottom), (att, here, share.astype(BF16))]
            for target, place, value in stores:
                target[place] = value

        loop(PAIRS // GROUP, group)

        @pl.when((j == 5) & has_after)
        def _():
            pack(lambda h: states[6, h], pack_out)
            state_on.start()

    pieces.wait(*meta_moves)
    loop(6, attend)
    put(att, 5)

    def branch_out(k):
        at = tile(k, 256)
        total = dot_nn(att[...], out_w[:, at]) + out_b[:, at].astype(F32)
        res[:, at] = rows[:, at].astype(F32) + total

    weight(1).wait()
    loop(3, branch_out)
    put_done(normed, 6)

    def second_norm(k):
        at = tile(k, 384)
        standard, _ = normalised(res[at, :])
        normed[at, :] = (standard * second_gain[...].astype(F32) + second_shift[...].astype(F32)).astype(BF16)

    loop(2, second_norm)
    put(normed, 4)

    def feed(k):
        at = tile(k, 256)
        hidden = dot_nn(normed[...], up_w[:, at]) + up_b[:, at].astype(F32)
        square = hidden * hidden
        inner = hidden * (0.7978845608028654 + 0.0356774081363 * square)
        bent = jnp.tanh(inner)
        half = 0.5 * (1.0 + bent)
        act[:, at] = (hidden * half).astype(BF16)
        steep = 1.5957691216057308 + 0.2140644489 * square
        slope[:, at] = (half + hidden * half * (1.0 - half) * steep).astype(BF16)

    weight(2).wait()
    loop(12, feed)
    for n in range(4):
        put(act.at[:, pl.ds(n * WIDE, WIDE)], n)

    def settle(k):
        at = tile(k, 384)
        total = res[at, :] + dot_nn(act[at, :], down_w[...]) + down_b[...].astype(F32)
        branch[at, :] = total.astype(BF16)

        @pl.when(section == 0)
        def _():
            forward_rows(k).start()

    weight(3).wait()
    loop(2, settle)

    @pl.when(section == 0)
    def _():
        for k in range(2):
            forward_rows(k).wait_send()
        for k in range(2):
            backward_rows(k).wait_recv()

    @pl.when(section == 1)
    def _():
        back_pieces.start(*ends_moves)
        pieces.wait(*grad_moves)

    put(grad_in, 7)

    def column_sums(values):
        return jnp.sum(values.astype(F32), 0, keepdims=True)

    small[140:141, :] = column_sums(grad_in[...])

    def feed_back(k):
        at = tile(k, 512)
        grads = dot_nt(grad_in[...], down_w[at, :])
        grads = (grads * slope[:, at].astype(F32)).astype(BF16)
        slope[:, at] = grads

    loop(6, feed_back)
    for n in range(4):
        put(slope.at[:, pl.ds(n * WIDE, WIDE)], 8 + n)
        small[136 + n : 137 + n, :] = column_sums(slope[:, n * WIDE : n * WIDE + WIDE])

    def second_grad(k):
        at = tile(k, 256)
        grad_wide[:, at] = dot_nt(slope[...], up_w[at, :])

    loop(3, second_grad)

    def second_back(k):
        at = tile(k, 384)
        grads = grad_wide[at, :]
        standard, scale = normalised(res[at, :])
        small[134:135, :] += jnp.sum(grads * standard, 0, keepdims=True)
        small[135:136, :] += jnp.sum(grads, 0, keepdims=True)
        grads = norm_input_grad(grads, standard, scale, second_gain[...].astype(F32))
        grads = grad_in[at, :].astype(F32) + grads
        res[at, :] = grads
        rounded = grads.astype(BF16)
        branch_grad[at, :] = rounded
        small[133:134, :] += column_sums(rounded)

    loop(2, second_back)
    put(branch_grad, 12)

    def attended_grad(k):
        at = tile(k, 256)
        grad_wide[:, at] = dot_nt(branch_grad[...], out_w[at, :])

    loop(3, attended_grad)
    for n in range(4):
        put_done(act.at[:, pl.ds(n * WIDE, WIDE)], n)

    put_done(att, 5)
    @pl.when(has_after)
    def _():
        state_on.wait_send()

    back_state[...] = jnp.zeros_like(back_state)

    def attend_back(k):
        j = (shift + 5 - k) % 6

        @pl.when(j == 5)
        def _():
            @pl.when(has_after)
            def _():
                state_back.wait_recv()

                def keep_state(h, value):
                    back_state[h] = value

                first_lane = ((lane_of == 0) | (lane_of == 64)).astype(F32)
                unpack(back_in, keep_state, first_lane)

            @pl.when(jnp.logical_not(has_after))
            def _():
                back_state[...] = jnp.zeros_like(back_state)

        keep = prepare(j)
        at = tile(j, ROWS)

        def group(g):
            stores = []
            for p in [g * GROUP_BACK + q for q in range(GROUP_BACK)]:
                values = proj[at, tile(12 + p, 128)]
                grads = (grad_wide[at, tile(p, 128)] / den[at, tile(p, 128)]).astype(BF16)
                sums = -half_sums(grads.astype(F32) * att_wide[at, tile(p, 128)], low)
                other_sums = pltpu.roll(sums, 64, 1)
                lanes = lax.broadcasted_iota(jnp.int32, (ROWS, 128), 1) % 64
                one = other_sums.astype(BF16).astype(F32)
                two = (other_sums - one).astype(BF16).astype(F32)
                three = other_sums - one - two
                spread = jnp.where(lanes == 0, one, jnp.where(lanes == 1, two, jnp.where(lanes == 2, three, 0.0)))
                spread = spread.astype(BF16)
                value_grads, query_grads, key_grads = [], [], []
                for half in range(2):
                    h = 2 * p + half
                    own = low if half == 0 else jnp.logical_not(low)
                    extended = jnp.where(own, values, jnp.ones_like(values))
                    grads_ext = jnp.where(own, grads, spread)
                    queries, keys = phi_q[at, tile(h, 128)], phi_k[at, tile(h, 128)]
                    high, rest = high_low(dot_nt(grads_ext, extended) * mask[...])
                    state_high, state_low = high_low(states[j, h])
                    query_grad = dot_nn(
                        jnp.concatenate([high, rest], 1), jnp.concatenate([keys, keys], 0)
                    )
                    query_grad += bef[...].astype(F32) * dot_nt(
                        jnp.concatenate([grads_ext, grads_ext], 1),
                        jnp.concatenate([state_high, state_low], 1),
                    )
                    high, rest = high_low(dot_nt(extended, grads_ext) * mask_t[...])
                    later = back_state[h]
                    later_high, later_low = high_low(later)
                    key_grad = dot_nn(
                        jnp.concatenate([high, rest], 1), jnp.concatenate([queries, queries], 0)
                    )
                    key_grad += trail[...].astype(F32) * dot_nt(
                        jnp.concatenate([extended, extended], 1),
                        jnp.concatenate([later_high, later_low], 1),
                    )
                    scores_t = (dot_nt(keys, queries) * mask_t[...]).astype(BF16)
                    value_grads.append(
                        dot_nn(
                            jnp.concatenate([scores_t, keys * trail[...]], 1),
                            jnp.concatenate([grads_ext, later_high], 0),
                        )
                    )
                    stores.append((back_state, h, keep * later + dot_tn(queries * bef[...], grads_ext)))
                    for phi, grad, kept in ((queries, query_grad, query_grads), (keys, key_grad, key_grads)):
                        phi = phi.astype(F32)
                        kept.append(phi * (grad - half_sums(phi * grad, low)))
                value_grad = jnp.where(low, value_grads[0], value_grads[1]).astype(BF16)
                stores.append((act, (at, tile(12 + p, 128)), value_grad))
                for kept, target, first in ((query_grads, act, 18), (key_grads, att, 0)):
                    left = kept[0] - pltpu.roll(kept[0], 64, 1)
                    right = pltpu.roll(kept[1], 64, 1) - kept[1]
                    both = jnp.where(low, left, right).astype(BF16)
                    stores.append((target, (at, tile(first + p, 128)), both))
            for target, place, value in stores:
                target[place] = value

        loop(PAIRS // GROUP_BACK, group)

        @pl.when((j == 0) & has_before)
        def _():
            pack(lambda h: back_state[h], pack_out)
            state_back.start()

    loop(6, attend_back)

    def maps_back(p):
        lanes = tile(p, 128)
        first = lax.broadcasted_iota(jnp.int32, (64, 128), 1) < 64
        for offset, target, source, table, at in ((0, act, 18, pair_q, 0), (6, att, 0, pair_k, 64)):
            logit_grads = target[:, tile(source + p, 128)]
            act[:, tile(offset + p, 128)] = dot_nt(logit_grads, table[p]).astype(BF16)
            product = dot_tn(proj[:, tile(offset + p, 128)], logit_grads)
            small[at : at + 64, lanes] = jnp.where(first, product[:64], product[64:])

    loop(PAIRS, maps_back)
    for n in range(3):
        put(act.at[:, pl.ds(n * WIDE, WIDE)], 13 + n)
        small[130 + n : 131 + n, :] = column_sums(act[:, n * WIDE : n * WIDE + WIDE])

    def first_grad(k):
        at = tile(k, 256)
        grad_wide[:, at] = dot_nt(act[:, : 3 * WIDE], qkv_w[at, :])

    loop(3, first_grad)

    def first_back(k):
        at = tile(k, 384)
        grads = grad_wide[at, :]
        standard, scale = normalised(rows[at, :].astype(F32))
        small[128:129, :] += jnp.sum(grads * standard, 0, keepdims=True)
        small[129:130, :] += jnp.sum(grads, 0, keepdims=True)
        grads = norm_input_grad(grads, standard, scale, first_gain[...].astype(F32))
        rows[at, :] = (res[at, :] + grads).astype(BF16)

        @pl.when(section == 1)
        def _():
            backward_rows(k).start()

    loop(2, first_back)

    @pl.when(section == 0)
    def _():
        copy = pltpu.make_async_copy(rows, ends, out_sem)
        copy.start()
        copy.wait()

    put_done(normed, 4)
    put_done(grad_in, 7)
    put_done(branch_grad, 12)
    for n in range(4):
        put_done(slope.at[:, pl.ds(n * WIDE, WIDE)], 8 + n)
    for n in range(3):
        put_done(act.at[:, pl.ds(n * WIDE, WIDE)], 13 + n)

    @pl.when(section == 1)
    def _():
        back_pieces.wait(*ends_moves)
        for k in range(2):
            backward_rows(k).wait_send()

    @pl.when(has_before)
    def _():
        state_back.wait_send()


def layers(ends_in, begins, filled, weights, mesh):
    tokens = 6 * ROWS
    any_space = pl.BlockSpec(memory_space=pl.ANY)
    in_vmem = pl.BlockSpec(memory_space=pltpu.VMEM)
    large = (2, 6, 10, 12)
    return pl.pallas_call(
        functools.partial(layers_kernel, mesh.shape["ctx"]),
        out_shape=(
            jax.ShapeDtypeStruct((16, tokens, WIDE), BF16),
            jax.ShapeDtypeStruct((tokens, WIDE), BF16),
            jax.ShapeDtypeStruct((256, WIDE), F32),
        ),
        in_specs=[any_space, in_vmem] + [any_space if n in large else in_vmem for n in range(14)],
        out_specs=(any_space, any_space, in_vmem),
        scratch_shapes=[
            pltpu.VMEM((WIDE, 3 * WIDE), BF16),
            pltpu.VMEM((WIDE, WIDE), BF16),
            pltpu.VMEM((WIDE, 4 * WIDE), BF16),
            pltpu.VMEM((4 * WIDE, WIDE), BF16),
            pltpu.VMEM((PAIRS, 128, 256), BF16),
            pltpu.VMEM((PAIRS, 128, 256), BF16),
            pltpu.VMEM((PAIRS, 128, 128), BF16),
            pltpu.VMEM((PAIRS, 128, 128), BF16),
            pltpu.VMEM((6, 8, 128), F32),
            pltpu.VMEM((6, 8, 128), F32),
            pltpu.VMEM((tokens, WIDE), BF16),
            pltpu.VMEM((tokens, WIDE), BF16),
            pltpu.VMEM((tokens, WIDE), BF16),
            pltpu.VMEM((tokens, 3 * WIDE), BF16),
            pltpu.VMEM((tokens, 2 * WIDE), BF16),
            pltpu.VMEM((tokens, 2 * WIDE), BF16),
            pltpu.VMEM((tokens, WIDE), BF16),
            pltpu.VMEM((tokens, WIDE), F32),
            pltpu.VMEM((tokens, WIDE), F32),
            pltpu.VMEM((tokens, WIDE), F32),
            pltpu.VMEM((tokens, 4 * WIDE), BF16),
            pltpu.VMEM((tokens, 4 * WIDE), BF16),
            pltpu.VMEM((7, HEADS, 128, 128), F32),
            pltpu.VMEM((PAIRS + 1, 128, 128), F32),
            pltpu.VMEM((PAIRS + 1, 128, 128), F32),
            pltpu.VMEM((HEADS, 128, 128), F32),
            pltpu.VMEM((PAIRS + 1, 128, 128), F32),
            pltpu.VMEM((tokens, WIDE), F32),
            pltpu.VMEM((tokens, WIDE), BF16),
            pltpu.VMEM((tokens, WIDE), BF16),
            pltpu.VMEM((128, 128), BF16),
            pltpu.VMEM((128, 128), F32),
            pltpu.VMEM((128, 128), F32),
            pltpu.VMEM((128, 128), BF16),
            pltpu.VMEM((128, 128), BF16),
            pltpu.SemaphoreType.DMA((16,)),
            pltpu.SemaphoreType.DMA,
            pltpu.SemaphoreType.DMA((6, 2)),
            pltpu.SemaphoreType.DMA((4,)),
            pltpu.SemaphoreType.DMA((3, 3, 6)),
        ],
        compiler_params=pltpu.CompilerParams(
            collective_id=1, has_side_effects=True, vmem_limit_bytes=60 * 1024 * 1024
        ),
    )(ends_in, jnp.concatenate([begins, filled], 1), *weights)


def body(mesh, ends_in, begins, filled, *weights):
    x, ends, small = layers(ends_in, begins, filled, weights, mesh)
    sums, small, ends = reduced(x, small, ends, mesh)
    return finished(sums, small, ends, weights)


def solution(mesh):
    placed = (
        P("section", None, ("dp", "ctx"), None),
        P(None, ("dp", "ctx")),
        P(None, ("dp", "ctx")),
        P("section", None),
        P("section", None),
        P("section", None, None),
        P("section", None),
        P("section", None, None),
        P("section", None, None),
        P("section", None, None),
        P("section", None),
        P("section", None),
        P("section", None),
        P("section", None, None),
        P("section", None),
        P("section", None, None),
        P("section", None),
    )
    return jax.shard_map(
        functools.partial(body, mesh),
        mesh=mesh,
        in_specs=placed,
        out_specs=(
            P("section", None, ("dp", "ctx"), None),
            P("section", None),
            P("section", None),
            P("section", None, None),
            P("section", None),
            P("section", None, None),
            P("section", None, None),
            P("section", None, None),
            P("section", None),
            P("section", None),
            P("section", None),
            P("section", None, None),
            P("section", None),
            P("section", None, None),
            P("section", None),
        ),
        check_vma=False,
    )
```

```python
import functools

import jax
import jax.numpy as jnp
from jax import lax
from jax.experimental import pallas as pl
from jax.experimental.pallas import tpu as pltpu
from jax.sharding import PartitionSpec as P

BLOCK = 64
ROWS = 128
HEADS = 12
PAIRS = 6
GROUP = 6
GROUP_BACK = 6
EPSILON = 1e-05
F32, BF16 = jnp.float32, jnp.bfloat16

MESH = pl.DeviceIdType.MESH
WIDE = 768
HALF = 384


def bit_length(size):
    return (size - 1).bit_length()


def bit_orders(ctx_size, dp_size):
    ctx_bits = [("ctx", k) for k in range(bit_length(ctx_size))]
    dp_bits = [("dp", k) for k in range(bit_length(dp_size))]

    def interleaved(first, second):
        order = []
        for k in range(max(len(first), len(second))):
            order += first[k : k + 1] + second[k : k + 1]
        return order

    return (interleaved(ctx_bits, dp_bits), interleaved(ctx_bits[::-1], dp_bits))


def halvings(rows, count):
    sizes, halved = [rows], []
    for _ in range(count):
        halved.append(sizes[-1] % 32 == 0)
        sizes.append(sizes[-1] // 2 if halved[-1] else sizes[-1])
    return sizes, halved


class Reduction:
    def __init__(self, rows, orders):
        self.rows, self.orders = rows, orders
        self.count = len(orders[0])
        self.sizes, self.halved = halvings(rows, self.count)
        self.steps = [("rs", s) for s in range(self.count)]
        self.steps += [("ag", s) for s in reversed(range(self.count)) if self.halved[s]]
        self.offsets, self.bits = [], []
        for order in orders:
            offset, offsets, bits = 0, [0], []
            for s, (axis, k) in enumerate(order):
                bit = (lax.axis_index(axis) // (1 << k)) % 2
                bits.append(bit)
                if self.halved[s]:
                    offset = offset + bit * self.sizes[s + 1]
                offsets.append(offset)
            self.offsets.append(offsets)
            self.bits.append(bits)

    def partner(self, part, s):
        axis, k = self.orders[part][s]
        return {axis: lax.axis_index(axis) + (1 << k) * (1 - 2 * self.bits[part][s])}

    def rows_at(self, offset, size):
        if isinstance(offset, int):
            return pl.ds(offset, size)
        return pl.ds(pl.multiple_of(offset, 16), size)

    def copy(self, buffer, whole, received, sems, part, step):
        kind, s = self.steps[step]
        columns = pl.ds(part * HALF, HALF)
        size = self.sizes[s + 1]
        if kind == "rs":
            offset = self.offsets[part][s]
            if self.halved[s]:
                offset = offset + (1 - self.bits[part][s]) * size
            source = buffer.at[self.rows_at(offset, size), columns]
            target = received[s]
        else:
            source = whole.at[self.rows_at(self.offsets[part][s + 1], size), columns]
            target = source
        return pltpu.make_async_remote_copy(
            src_ref=source,
            dst_ref=target,
            send_sem=sems[0],
            recv_sem=sems[1],
            device_id=self.partner(part, s),
            device_id_type=MESH,
        )

    def add(self, buffer, whole, received, part, step):
        kind, s = self.steps[step]
        if kind == "rs":
            size = self.sizes[s + 1]
            rows = self.rows_at(self.offsets[part][s + 1], size)
            columns = pl.ds(part * HALF, HALF)
            total = buffer[rows, columns].astype(jnp.float32) + received[s][...].astype(jnp.float32)
            target = whole if s + 1 == self.count else buffer
            target[rows, columns] = total.astype(jnp.bfloat16)


class Pieces:
    def __init__(self, ctx_size, gather):
        self.size, self.gather, self.me = ctx_size, gather, lax.axis_index("ctx")

    def place(self, k):
        if self.gather:
            at = k * self.size + self.me
            return at // 6, at % 6
        at = 6 * self.me + k
        return at % self.size, at // self.size

    def origin(self, k):
        if self.gather:
            return (6 * self.me + k) % self.size
        return (k * self.size + self.me) // 6

    def start(self, source, target, sems):
        for k in range(6):
            device, at = self.place(k)

            @pl.when(device == self.me)
            def _():
                self.local(source, target, sems, k, at).start()

            @pl.when(device != self.me)
            def _():
                self.remote(source, target, sems, k, at, device).start()

    def wait(self, source, target, sems):
        for k in range(6):
            device, at = self.place(k)

            @pl.when(device == self.me)
            def _():
                self.local(source, target, sems, k, at).wait()

            @pl.when(device != self.me)
            def _():
                self.remote(source, target, sems, k, at, device).wait_send()

            @pl.when(self.origin(k) != self.me)
            def _():
                self.remote(source, target, sems, k, k, (self.me + 1) % self.size).wait_recv()

    def local(self, source, target, sems, k, at):
        return pltpu.make_async_copy(source(k), target(at), sems.at[2, k])

    def remote(self, source, target, sems, k, at, device):
        return pltpu.make_async_remote_copy(
            src_ref=source(k),
            dst_ref=target(at),
            send_sem=sems.at[0, k],
            recv_sem=sems.at[1, at],
            device_id={"ctx": device},
            device_id_type=MESH,
        )


def block_rows(k):
    return pl.ds(k * ROWS if isinstance(k, int) else pl.multiple_of(k * ROWS, ROWS), ROWS)


def greet_ctx(barrier, ctx_size):
    me = lax.axis_index("ctx")

    def greet(k):
        device = {"ctx": (me + 1 + k) % ctx_size}
        pl.semaphore_signal(barrier, inc=1, device_id=device, device_id_type=MESH)

    loop(ctx_size - 1, greet)
    return ctx_size - 1


def reduce_kernel(
    orders, ctx_size, chunks, x_ref, small_ref, ends, sums, small_out, ends_out, *scratch
):
    count = len(orders[0])
    big, big_whole, little, little_whole = scratch[:4]
    scratch = scratch[4:]
    big_recv, little_recv = scratch[:count], scratch[count : 2 * count]
    left, right, send, recv, send_small, recv_small, load, store, moves = scratch[2 * count :]
    large, small = Reduction(WIDE, orders), Reduction(little.shape[0], orders)
    steps = len(large.steps)

    def operands(c):
        left_at = jnp.where(c < 4, c, jnp.where(c < 8, 4, jnp.where(c == 8, 5, 6)))
        right_at = jnp.where(c < 4, 7, c + 4)
        slot = c % 2
        return (
            pltpu.make_async_copy(x_ref.at[left_at], left.at[slot], load.at[slot, 0]),
            pltpu.make_async_copy(x_ref.at[right_at], right.at[slot], load.at[slot, 1]),
        )

    for copy in operands(0):
        copy.start()
    little[...] = small_ref[...].astype(BF16)

    barrier = pltpu.get_barrier_semaphore()
    greeted = greet_ctx(barrier, ctx_size)
    for s in range(count):
        if orders[0][s][0] != "ctx":
            pl.semaphore_signal(barrier, inc=1, device_id=large.partner(0, s), device_id_type=MESH)
            greeted += 1
    pl.semaphore_wait(barrier, greeted)

    def big_copy(c, part, step):
        received = [r.at[c, part] for r in big_recv]
        sems = (send.at[c, part, step], recv.at[c, part, step])
        return large.copy(big.at[c], big_whole.at[c], received, sems, part, step)

    def small_copy(part, step):
        received = [r.at[part] for r in little_recv]
        sems = (send_small.at[part, step], recv_small.at[part, step])
        return small.copy(little, little_whole, received, sems, part, step)

    for part in range(2):
        small_copy(part, 0).start()
    section = lax.axis_index("section")
    pieces = Pieces(ctx_size, False)
    given = (lambda k: ends.at[block_rows(k), :], lambda k: ends_out.at[k], moves)

    def tick(t, carry):
        @pl.when(t < chunks)
        def _():
            for copy in operands(t):
                copy.wait()

            @pl.when(t + 1 < chunks)
            def _():
                for copy in operands(t + 1):
                    copy.start()

            slot = t % 2
            big[t] = dot_tn(left[slot], right[slot]).astype(BF16)
            for part in range(2):
                big_copy(t, part, 0).start()

        @pl.when((t == chunks) & (section == 0))
        def _():
            pieces.start(*given)

        for step in range(steps):
            c = t - 2 - step

            @pl.when((c >= 0) & (c < chunks))
            def _():
                for part in range(2):
                    big_copy(c, part, step).wait()
                    received = [r.at[c, part] for r in big_recv]
                    large.add(big.at[c], big_whole.at[c], received, part, step)
                    if step + 1 < steps:
                        big_copy(c, part, step + 1).start()
                if step + 1 == steps:
                    pltpu.make_async_copy(big_whole.at[c], sums.at[c], store).start()

            if step < len(small.steps):
                @pl.when(t == step)
                def _():
                    for part in range(2):
                        small_copy(part, step).wait()
                        received = [r.at[part] for r in little_recv]
                        small.add(little, little_whole, received, part, step)
                        if step + 1 < len(small.steps):
                            small_copy(part, step + 1).start()

        return carry

    lax.fori_loop(0, chunks + steps + 1, tick, 0)
    small_out[...] = little_whole[...]

    @pl.when(section == 0)
    def _():
        pieces.wait(*given)

    @pl.when(section == 1)
    def _():
        for k in range(6):
            ends_out[k] = ends[block_rows(k), :]

    pltpu.make_async_copy(big_whole, sums, store).wait()


def reduced(x, small, ends, mesh):
    orders = bit_orders(mesh.shape["ctx"], mesh.shape["dp"])
    count, chunks, tokens = len(orders[0]), 12, x.shape[1]
    sizes, _ = halvings(WIDE, count)
    small_rows = small.shape[0]
    small_sizes, small_halved = halvings(small_rows, count)
    steps = count + sum(halvings(WIDE, count)[1])
    small_steps = count + sum(small_halved)
    any_space = pl.BlockSpec(memory_space=pl.ANY)
    in_vmem = pl.BlockSpec(memory_space=pltpu.VMEM)
    return pl.pallas_call(
        functools.partial(reduce_kernel, orders, mesh.shape["ctx"], chunks),
        out_shape=(
            jax.ShapeDtypeStruct((chunks, WIDE, WIDE), BF16),
            jax.ShapeDtypeStruct((small_rows, WIDE), BF16),
            jax.ShapeDtypeStruct((6, ROWS, WIDE), BF16),
        ),
        in_specs=[any_space, in_vmem, in_vmem],
        out_specs=(any_space, in_vmem, in_vmem),
        scratch_shapes=[
            pltpu.VMEM((chunks, WIDE, WIDE), BF16),
            pltpu.VMEM((chunks, WIDE, WIDE), BF16),
            pltpu.VMEM((small_rows, WIDE), BF16),
            pltpu.VMEM((small_rows, WIDE), BF16),
            *(pltpu.VMEM((chunks, 2, size, HALF), BF16) for size in sizes[1:]),
            *(pltpu.VMEM((2, size, HALF), BF16) for size in small_sizes[1:]),
            pltpu.VMEM((2, tokens, WIDE), BF16),
            pltpu.VMEM((2, tokens, WIDE), BF16),
            pltpu.SemaphoreType.DMA((chunks, 2, steps)),
            pltpu.SemaphoreType.DMA((chunks, 2, steps)),
            pltpu.SemaphoreType.DMA((2, small_steps)),
            pltpu.SemaphoreType.DMA((2, small_steps)),
            pltpu.SemaphoreType.DMA((2, 2)),
            pltpu.SemaphoreType.DMA,
            pltpu.SemaphoreType.DMA((3, 6)),
        ],
        compiler_params=pltpu.CompilerParams(
            collective_id=0, has_side_effects=True, vmem_limit_bytes=60 * 1024 * 1024
        ),
    )(x, small, ends)


def finish_kernel(sums, little, ends, *refs):
    outs, (narrow, wide, passing, load, store, through) = refs[:15], refs[15:]
    (
        ends_out, first_gain, first_shift, qkv_w, qkv_b, map_q, map_k, out_w, out_b,
        second_gain, second_shift, up_w, up_b, down_w, down_b,
    ) = outs
    take = pltpu.make_async_copy(ends, passing, through.at[0])
    give = pltpu.make_async_copy(passing, ends_out.at[0], through.at[1])
    take.start()
    depth = narrow.shape[0]
    targets = [down_w.at[0, pl.ds(n * WIDE, WIDE), :] for n in range(4)]
    targets += [up_w.at[0, :, pl.ds(n * WIDE, WIDE)] for n in range(4)]
    targets += [out_w.at[0]]
    targets += [qkv_w.at[0, :, pl.ds(n * WIDE, WIDE)] for n in range(3)]

    def read(c):
        return pltpu.make_async_copy(sums.at[c], narrow.at[c % depth], load.at[c % depth])

    def write(c):
        return pltpu.make_async_copy(wide.at[c % depth], targets[c], store.at[c % depth])

    for c in range(depth):
        read(c).start()
    for target, first in (
        (first_gain, 128), (first_shift, 129), (out_b, 133), (second_gain, 134), (second_shift, 135), (down_b, 140),
    ):
        target[...] = little[first : first + 1, :].astype(F32)
    for target, first, count in ((qkv_b, 130, 3), (up_b, 136, 4)):
        for n in range(count):
            target[:, n * WIDE : n * WIDE + WIDE] = little[first + n : first + n + 1, :].astype(F32)
    map_q[0] = little[0:64, :].astype(F32)
    map_k[0] = little[64:128, :].astype(F32)
    take.wait()
    give.start()
    for c in range(len(targets)):
        read(c).wait()
        if c >= depth:
            write(c - depth).wait()

        def widen(k):
            at = tile(k, 256)
            wide[c % depth, at, :] = narrow[c % depth, at, :].astype(F32)

        loop(3, widen)
        write(c).start()
        if c + depth < len(targets):
            read(c + depth).start()
    for c in range(len(targets) - depth, len(targets)):
        write(c).wait()
    give.wait()


def finished(sums, little, ends, weights):
    any_space = pl.BlockSpec(memory_space=pl.ANY)
    in_vmem = pl.BlockSpec(memory_space=pltpu.VMEM)
    shapes = [jax.ShapeDtypeStruct((1,) + ends.shape, BF16)]
    shapes += [jax.ShapeDtypeStruct(weight.shape, F32) for weight in weights]
    large = (0, 3, 7, 11, 13)
    return pl.pallas_call(
        finish_kernel,
        out_shape=tuple(shapes),
        in_specs=[any_space, in_vmem, any_space],
        out_specs=tuple(any_space if n in large else in_vmem for n in range(15)),
        scratch_shapes=[
            pltpu.VMEM((6, WIDE, WIDE), BF16),
            pltpu.VMEM((6, WIDE, WIDE), F32),
            pltpu.VMEM(ends.shape, BF16),
            pltpu.SemaphoreType.DMA((6,)),
            pltpu.SemaphoreType.DMA((6,)),
            pltpu.SemaphoreType.DMA((2,)),
        ],
        compiler_params=pltpu.CompilerParams(vmem_limit_bytes=60 * 1024 * 1024),
    )(sums, little, ends)


def dot_nn(left, right):
    return jnp.dot(left, right, preferred_element_type=F32)


def dot_nt(left, right):
    return lax.dot_general(left, right, (((1,), (1,)), ((), ())), preferred_element_type=F32)


def dot_tn(left, right):
    return lax.dot_general(left, right, (((0,), (0,)), ((), ())), preferred_element_type=F32)


def high_low(values):
    high = values.astype(BF16)
    return high, (values - high.astype(F32)).astype(BF16)


def tile(index, size):
    return pl.ds(pl.multiple_of(index * size, size), size)


def loop(count, step, unroll=1):
    def body(k, carry):
        step(k)
        return carry

    lax.fori_loop(0, count, body, 0, unroll=unroll)


def low_lanes(rows):
    return lax.broadcasted_iota(jnp.int32, (rows, 128), 1) < 64


def normalised(rows):
    average = jnp.mean(rows, -1, keepdims=True)
    centred = rows - average
    scale = lax.rsqrt(jnp.mean(centred * centred, -1, keepdims=True) + EPSILON)
    return centred * scale, scale


def norm_input_grad(grad, standard, scale, gain):
    wide = grad * gain
    first = jnp.mean(wide, -1, keepdims=True)
    second = jnp.mean(wide * standard, -1, keepdims=True)
    return scale * (wide - first - standard * second)


def half_sums(values, low):
    first = jnp.sum(jnp.where(low, values, 0.0), -1, keepdims=True)
    second = jnp.sum(jnp.where(low, 0.0, values), -1, keepdims=True)
    return jnp.where(low, first, second)


def half_softmax(logits, low, ones):
    lowest = jnp.float32(-3e38)
    first = jnp.max(jnp.where(low, logits, lowest), -1, keepdims=True)
    second = jnp.max(jnp.where(low, lowest, logits), -1, keepdims=True)
    powers = jnp.exp(logits - jnp.where(low, first, second))
    high, rest = high_low(powers)
    return powers / dot_nn(jnp.concatenate([high, rest], 1), jnp.concatenate([ones, ones], 0))


def layers_kernel(ctx_size, *refs):
    (
        x_in, flags, first_gain, first_shift, qkv_given, qkv_b, map_q_given, map_k_given,
        out_given, out_b, second_gain, second_shift, up_given, up_b, down_given, down_b,
        x_out, ends, small,
        qkv_w, out_w, up_w, down_w, map_q, map_k, pair_q, pair_k, meta_own, meta,
        rows, grad_in, normed, proj, phi_q, phi_k, att, att_wide, den, res, act, slope,
        states, pack_in, pack_out, back_state, back_in, grad_wide, branch, branch_grad,
        ones, mask, mask_t, bef, trail, x_sem, out_sem, remote, weight_sem, moves,
    ) = refs
    section, me = lax.axis_index("section"), lax.axis_index("ctx")
    has_before = (6 * me) % ctx_size != 0
    has_after = (6 * (me + 1)) % ctx_size != 0
    reach = (6 * me + 5) % ctx_size
    shift = jnp.where(reach <= 5, 5 - reach, 0)
    other = {"section": 1 - section}

    def weight(n):
        given, kept = ((qkv_given, qkv_w), (out_given, out_w), (up_given, up_w), (down_given, down_w))[n]
        return pltpu.make_async_copy(given.at[0], kept, weight_sem.at[n])

    def remote_copy(source, target, index, device):
        return pltpu.make_async_remote_copy(
            src_ref=source,
            dst_ref=target,
            send_sem=remote.at[index, 0],
            recv_sem=remote.at[index, 1],
            device_id=device,
            device_id_type=MESH,
        )

    def forward_rows(k):
        at = tile(k, 384)
        return remote_copy(branch.at[at, :], rows.at[at, :], k, other)

    def backward_rows(k):
        at = tile(k, 384)
        return remote_copy(rows.at[at, :], grad_in.at[at, :], 2 + k, other)

    state_on = remote_copy(pack_out, pack_in, 4, {"ctx": me + 1})
    state_back = remote_copy(pack_out, back_in, 5, {"ctx": me - 1})
    pieces = Pieces(ctx_size, True)
    rows_moves = (lambda k: x_in.at[0, k], lambda k: rows.at[block_rows(k), :], moves.at[0])
    grad_moves = (lambda k: x_in.at[0, k], lambda k: grad_in.at[block_rows(k), :], moves.at[0])
    back_pieces = Pieces(ctx_size, False)
    ends_moves = (lambda k: branch.at[block_rows(k), :], lambda k: ends.at[block_rows(k), :], moves.at[2])
    meta_moves = (lambda k: meta_own.at[k], lambda k: meta.at[k], moves.at[1])

    barrier = pltpu.get_barrier_semaphore()
    greeted = greet_ctx(barrier, ctx_size)
    pl.semaphore_signal(barrier, inc=1, device_id=other, device_id_type=MESH)
    for k in range(6):
        for n in range(4):
            value = flags[k : k + 1, n : n + 1].astype(F32)
            meta_own[k, n : n + 1, :] = jnp.broadcast_to(value, (1, 128))
    pl.semaphore_wait(barrier, greeted + 1)

    @pl.when(section == 0)
    def _():
        pieces.start(*rows_moves)

    pieces.start(*meta_moves)
    for n in range(4):
        weight(n).start()

    def put(source, index):
        pltpu.make_async_copy(source, x_out.at[index], x_sem.at[index]).start()

    def put_done(source, index):
        pltpu.make_async_copy(source, x_out.at[index], x_sem.at[index]).wait()

    low = low_lanes(ROWS)
    row_of = lax.broadcasted_iota(jnp.int32, (ROWS, 128), 0).astype(F32)
    lane_of = lax.broadcasted_iota(jnp.int32, (ROWS, 128), 1).astype(F32)
    ones[...] = ((row_of < 64) == (lane_of < 64)).astype(BF16)
    small[...] = jnp.zeros_like(small)
    left_lanes = low_lanes(64)
    for given, signed, plain in ((map_q_given, map_q, pair_q), (map_k_given, map_k, pair_k)):
        signed[...] = jnp.zeros_like(signed)
        for p in range(PAIRS):
            both = given[0, :, p * 128 : p * 128 + 128].astype(F32)
            turned = pltpu.roll(both, 64, 1)
            signed[p, :64, :128] = jnp.where(left_lanes, both, -turned).astype(BF16)
            signed[p, 64:, 128:] = jnp.where(left_lanes, turned, -both).astype(BF16)
            plain[p, :64, :] = jnp.where(left_lanes, both, 0.0).astype(BF16)
            plain[p, 64:, :] = jnp.where(left_lanes, 0.0, both).astype(BF16)

    def usable(tokens, filled_first, filled_second):
        return jnp.where(
            tokens < 64, (tokens < filled_first).astype(F32), (tokens - 64 < filled_second).astype(F32)
        )

    def prepare(j):
        start_first, start_second = meta[j, 0:1, :], meta[j, 1:2, :]
        filled_first, filled_second = meta[j, 2:3, :], meta[j, 3:4, :]
        cut = ((row_of >= 64) & (lane_of < 64)).astype(F32) * start_second
        seen = (lane_of <= row_of).astype(F32) * (1.0 - cut)
        mask[...] = seen * usable(lane_of, filled_first, filled_second)
        cut = ((lane_of >= 64) & (row_of < 64)).astype(F32) * start_second
        seen = (row_of <= lane_of).astype(F32) * (1.0 - cut)
        of_rows = usable(row_of, filled_first, filled_second)
        mask_t[...] = seen * of_rows
        kept = 1.0 - start_first
        bef[...] = jnp.where(row_of < 64, kept, kept * (1.0 - start_second)).astype(BF16)
        tail = jnp.where(row_of < 64, 1.0 - start_second, jnp.ones_like(start_second))
        trail[...] = (tail * of_rows).astype(BF16)
        return kept * (1.0 - start_second)

    def pack(source, target):
        sums = jnp.zeros((128, 128), F32)
        for p in range(PAIRS):
            first, second = source(2 * p), source(2 * p + 1)
            target[p] = jnp.where(low, first, second)
            first = jnp.sum(jnp.where(low, 0.0, first), -1, keepdims=True)
            second = jnp.sum(jnp.where(low, second, 0.0), -1, keepdims=True)
            sums = jnp.where(lane_of == 2 * p, first, jnp.where(lane_of == 2 * p + 1, second, sums))
        target[PAIRS] = sums

    def unpack(source, store, share):
        sums = source[PAIRS]
        for p in range(PAIRS):
            both = source[p]
            first = jnp.sum(jnp.where(lane_of == 2 * p, sums, 0.0), -1, keepdims=True)
            second = jnp.sum(jnp.where(lane_of == 2 * p + 1, sums, 0.0), -1, keepdims=True)
            store(2 * p, jnp.where(low, both, first * share))
            store(2 * p + 1, jnp.where(low, second * share, both))

    @pl.when(jnp.logical_not(has_before))
    def _():
        states[0] = jnp.zeros_like(states[0])

    @pl.when(shift != 0)
    def _():
        states[shift] = jnp.zeros_like(states[0])

    @pl.when(section == 0)
    def _():
        pieces.wait(*rows_moves)

    @pl.when(section == 1)
    def _():
        forward_rows(0).wait_recv()
        pieces.start(*grad_moves)

    def first_norm(k):
        @pl.when((section == 1) & (k == 1))
        def _():
            forward_rows(1).wait_recv()

        at = tile(k, 384)
        standard, _ = normalised(rows[at, :].astype(F32))
        normed[at, :] = (standard * first_gain[...].astype(F32) + first_shift[...].astype(F32)).astype(BF16)

    loop(2, first_norm)

    def project(k):
        at = tile(k, 768)
        proj[:, at] = (dot_nn(normed[...], qkv_w[:, at]) + qkv_b[:, at].astype(F32)).astype(BF16)

    weight(0).wait()
    loop(3, project)
    put(normed, 6)

    def features(p):
        low = low_lanes(6 * ROWS)
        for source, table, target in ((0, map_q, phi_q), (6, map_k, phi_k)):
            logits = dot_nn(proj[:, tile(source + p, 128)], table[p])
            for half in range(2):
                phi = half_softmax(logits[:, half * 128 : half * 128 + 128], low, ones[...])
                target[:, tile(2 * p + half, 128)] = phi.astype(BF16)

    loop(PAIRS, features)

    def attend(k):
        j = (shift + k) % 6

        @pl.when((j == 0) & has_before)
        def _():
            state_on.wait_recv()

            def keep_state(h, value):
                states[0, h] = value

            unpack(pack_in, keep_state, 0.015625)

        keep = prepare(j)
        at = tile(j, ROWS)

        def group(g):
            stores = []
            for p in [g * GROUP + q for q in range(GROUP)]:
                values = proj[at, tile(12 + p, 128)]
                results = []
                for half in range(2):
                    h = 2 * p + half
                    own = low if half == 0 else jnp.logical_not(low)
                    extended = jnp.where(own, values, jnp.ones_like(values))
                    queries, keys = phi_q[at, tile(h, 128)], phi_k[at, tile(h, 128)]
                    high, rest = high_low(dot_nt(queries, keys) * mask[...])
                    state = states[j, h]
                    state_high, state_low = high_low(state)
                    early = queries * bef[...]
                    results.append(
                        dot_nn(
                            jnp.concatenate([high, rest, early, early], 1),
                            jnp.concatenate([extended, extended, state_high, state_low], 0),
                        )
                    )
                    later = keep * state + dot_tn(keys * trail[...], extended)
                    stores.append((states, (j + 1, h), later))
                top = jnp.where(low, results[0], results[1])
                bottom = pltpu.roll(jnp.where(low, results[1], results[0]), 64, 1)
                share = top / bottom
                here = (at, tile(p, 128))
                stores += [(att_wide, here, share), (den, here, bottom), (att, here, share.astype(BF16))]
            for target, place, value in stores:
                target[place] = value

        loop(PAIRS // GROUP, group)

        @pl.when((j == 5) & has_after)
        def _():
            pack(lambda h: states[6, h], pack_out)
            state_on.start()

    pieces.wait(*meta_moves)
    loop(6, attend)
    put(att, 5)

    def branch_out(k):
        at = tile(k, 256)
        total = dot_nn(att[...], out_w[:, at]) + out_b[:, at].astype(F32)
        res[:, at] = rows[:, at].astype(F32) + total

    weight(1).wait()
    loop(3, branch_out)
    put_done(normed, 6)

    def second_norm(k):
        at = tile(k, 384)
        standard, _ = normalised(res[at, :])
        normed[at, :] = (standard * second_gain[...].astype(F32) + second_shift[...].astype(F32)).astype(BF16)

    loop(2, second_norm)
    put(normed, 4)

    def feed(k):
        at = tile(k, 256)
        hidden = dot_nn(normed[...], up_w[:, at]) + up_b[:, at].astype(F32)
        square = hidden * hidden
        inner = hidden * (0.7978845608028654 + 0.0356774081363 * square)
        bent = jnp.tanh(inner)
        half = 0.5 * (1.0 + bent)
        act[:, at] = (hidden * half).astype(BF16)
        steep = 1.5957691216057308 + 0.2140644489 * square
        slope[:, at] = (half + hidden * half * (1.0 - half) * steep).astype(BF16)

    weight(2).wait()
    loop(12, feed)
    for n in range(4):
        put(act.at[:, pl.ds(n * WIDE, WIDE)], n)

    def settle(k):
        at = tile(k, 384)
        total = res[at, :] + dot_nn(act[at, :], down_w[...]) + down_b[...].astype(F32)
        branch[at, :] = total.astype(BF16)

        @pl.when(section == 0)
        def _():
            forward_rows(k).start()

    weight(3).wait()
    loop(2, settle)

    @pl.when(section == 0)
    def _():
        for k in range(2):
            forward_rows(k).wait_send()
        for k in range(2):
            backward_rows(k).wait_recv()

    @pl.when(section == 1)
    def _():
        back_pieces.start(*ends_moves)
        pieces.wait(*grad_moves)

    put(grad_in, 7)

    def column_sums(values):
        return jnp.sum(values.astype(F32), 0, keepdims=True)

    small[140:141, :] = column_sums(grad_in[...])

    def feed_back(k):
        at = tile(k, 512)
        grads = dot_nt(grad_in[...], down_w[at, :])
        grads = (grads * slope[:, at].astype(F32)).astype(BF16)
        slope[:, at] = grads

    loop(6, feed_back)
    for n in range(4):
        put(slope.at[:, pl.ds(n * WIDE, WIDE)], 8 + n)
        small[136 + n : 137 + n, :] = column_sums(slope[:, n * WIDE : n * WIDE + WIDE])

    def second_grad(k):
        at = tile(k, 256)
        grad_wide[:, at] = dot_nt(slope[...], up_w[at, :])

    loop(3, second_grad)

    def second_back(k):
        at = tile(k, 384)
        grads = grad_wide[at, :]
        standard, scale = normalised(res[at, :])
        small[134:135, :] += jnp.sum(grads * standard, 0, keepdims=True)
        small[135:136, :] += jnp.sum(grads, 0, keepdims=True)
        grads = norm_input_grad(grads, standard, scale, second_gain[...].astype(F32))
        grads = grad_in[at, :].astype(F32) + grads
        res[at, :] = grads
        rounded = grads.astype(BF16)
        branch_grad[at, :] = rounded
        small[133:134, :] += column_sums(rounded)

    loop(2, second_back)
    put(branch_grad, 12)

    def attended_grad(k):
        at = tile(k, 256)
        grad_wide[:, at] = dot_nt(branch_grad[...], out_w[at, :])

    loop(3, attended_grad)
    for n in range(4):
        put_done(act.at[:, pl.ds(n * WIDE, WIDE)], n)

    put_done(att, 5)
    @pl.when(has_after)
    def _():
        state_on.wait_send()

    back_state[...] = jnp.zeros_like(back_state)

    def attend_back(k):
        j = (shift + 5 - k) % 6

        @pl.when(j == 5)
        def _():
            @pl.when(has_after)
            def _():
                state_back.wait_recv()

                def keep_state(h, value):
                    back_state[h] = value

                first_lane = ((lane_of == 0) | (lane_of == 64)).astype(F32)
                unpack(back_in, keep_state, first_lane)

            @pl.when(jnp.logical_not(has_after))
            def _():
                back_state[...] = jnp.zeros_like(back_state)

        keep = prepare(j)
        at = tile(j, ROWS)

        def group(g):
            stores = []
            for p in [g * GROUP_BACK + q for q in range(GROUP_BACK)]:
                values = proj[at, tile(12 + p, 128)]
                grads = (grad_wide[at, tile(p, 128)] / den[at, tile(p, 128)]).astype(BF16)
                sums = -half_sums(grads.astype(F32) * att_wide[at, tile(p, 128)], low)
                other_sums = pltpu.roll(sums, 64, 1)
                lanes = lax.broadcasted_iota(jnp.int32, (ROWS, 128), 1) % 64
                one = other_sums.astype(BF16).astype(F32)
                two = (other_sums - one).astype(BF16).astype(F32)
                three = other_sums - one - two
                spread = jnp.where(lanes == 0, one, jnp.where(lanes == 1, two, jnp.where(lanes == 2, three, 0.0)))
                spread = spread.astype(BF16)
                value_grads, query_grads, key_grads = [], [], []
                for half in range(2):
                    h = 2 * p + half
                    own = low if half == 0 else jnp.logical_not(low)
                    extended = jnp.where(own, values, jnp.ones_like(values))
                    grads_ext = jnp.where(own, grads, spread)
                    queries, keys = phi_q[at, tile(h, 128)], phi_k[at, tile(h, 128)]
                    high, rest = high_low(dot_nt(grads_ext, extended) * mask[...])
                    state_high, state_low = high_low(states[j, h])
                    query_grad = dot_nn(
                        jnp.concatenate([high, rest], 1), jnp.concatenate([keys, keys], 0)
                    )
                    query_grad += bef[...].astype(F32) * dot_nt(
                        jnp.concatenate([grads_ext, grads_ext], 1),
                        jnp.concatenate([state_high, state_low], 1),
                    )
                    high, rest = high_low(dot_nt(extended, grads_ext) * mask_t[...])
                    later = back_state[h]
                    later_high, later_low = high_low(later)
                    key_grad = dot_nn(
                        jnp.concatenate([high, rest], 1), jnp.concatenate([queries, queries], 0)
                    )
                    key_grad += trail[...].astype(F32) * dot_nt(
                        jnp.concatenate([extended, extended], 1),
                        jnp.concatenate([later_high, later_low], 1),
                    )
                    scores_t = (dot_nt(keys, queries) * mask_t[...]).astype(BF16)
                    value_grads.append(
                        dot_nn(
                            jnp.concatenate([scores_t, keys * trail[...]], 1),
                            jnp.concatenate([grads_ext, later_high], 0),
                        )
                    )
                    stores.append((back_state, h, keep * later + dot_tn(queries * bef[...], grads_ext)))
                    for phi, grad, kept in ((queries, query_grad, query_grads), (keys, key_grad, key_grads)):
                        phi = phi.astype(F32)
                        kept.append(phi * (grad - half_sums(phi * grad, low)))
                value_grad = jnp.where(low, value_grads[0], value_grads[1]).astype(BF16)
                stores.append((act, (at, tile(12 + p, 128)), value_grad))
                for kept, target, first in ((query_grads, act, 18), (key_grads, att, 0)):
                    left = kept[0] - pltpu.roll(kept[0], 64, 1)
                    right = pltpu.roll(kept[1], 64, 1) - kept[1]
                    both = jnp.where(low, left, right).astype(BF16)
                    stores.append((target, (at, tile(first + p, 128)), both))
            for target, place, value in stores:
                target[place] = value

        loop(PAIRS // GROUP_BACK, group)

        @pl.when((j == 0) & has_before)
        def _():
            pack(lambda h: back_state[h], pack_out)
            state_back.start()

    loop(6, attend_back)

    def maps_back(p):
        lanes = tile(p, 128)
        first = lax.broadcasted_iota(jnp.int32, (64, 128), 1) < 64
        for offset, target, source, table, at in ((0, act, 18, pair_q, 0), (6, att, 0, pair_k, 64)):
            logit_grads = target[:, tile(source + p, 128)]
            act[:, tile(offset + p, 128)] = dot_nt(logit_grads, table[p]).astype(BF16)
            product = dot_tn(proj[:, tile(offset + p, 128)], logit_grads)
            small[at : at + 64, lanes] = jnp.where(first, product[:64], product[64:])

    loop(PAIRS, maps_back)
    for n in range(3):
        put(act.at[:, pl.ds(n * WIDE, WIDE)], 13 + n)
        small[130 + n : 131 + n, :] = column_sums(act[:, n * WIDE : n * WIDE + WIDE])

    def first_grad(k):
        at = tile(k, 256)
        grad_wide[:, at] = dot_nt(act[:, : 3 * WIDE], qkv_w[at, :])

    loop(3, first_grad)

    def first_back(k):
        at = tile(k, 384)
        grads = grad_wide[at, :]
        standard, scale = normalised(rows[at, :].astype(F32))
        small[128:129, :] += jnp.sum(grads * standard, 0, keepdims=True)
        small[129:130, :] += jnp.sum(grads, 0, keepdims=True)
        grads = norm_input_grad(grads, standard, scale, first_gain[...].astype(F32))
        rows[at, :] = (res[at, :] + grads).astype(BF16)

        @pl.when(section == 1)
        def _():
            backward_rows(k).start()

    loop(2, first_back)

    @pl.when(section == 0)
    def _():
        copy = pltpu.make_async_copy(rows, ends, out_sem)
        copy.start()
        copy.wait()

    put_done(normed, 4)
    put_done(grad_in, 7)
    put_done(branch_grad, 12)
    for n in range(4):
        put_done(slope.at[:, pl.ds(n * WIDE, WIDE)], 8 + n)
    for n in range(3):
        put_done(act.at[:, pl.ds(n * WIDE, WIDE)], 13 + n)

    @pl.when(section == 1)
    def _():
        back_pieces.wait(*ends_moves)
        for k in range(2):
            backward_rows(k).wait_send()

    @pl.when(has_before)
    def _():
        state_back.wait_send()


def layers(ends_in, begins, filled, weights, mesh):
    tokens = 6 * ROWS
    any_space = pl.BlockSpec(memory_space=pl.ANY)
    in_vmem = pl.BlockSpec(memory_space=pltpu.VMEM)
    large = (2, 6, 10, 12)
    return pl.pallas_call(
        functools.partial(layers_kernel, mesh.shape["ctx"]),
        out_shape=(
            jax.ShapeDtypeStruct((16, tokens, WIDE), BF16),
            jax.ShapeDtypeStruct((tokens, WIDE), BF16),
            jax.ShapeDtypeStruct((256, WIDE), F32),
        ),
        in_specs=[any_space, in_vmem] + [any_space if n in large else in_vmem for n in range(14)],
        out_specs=(any_space, any_space, in_vmem),
        scratch_shapes=[
            pltpu.VMEM((WIDE, 3 * WIDE), BF16),
            pltpu.VMEM((WIDE, WIDE), BF16),
            pltpu.VMEM((WIDE, 4 * WIDE), BF16),
            pltpu.VMEM((4 * WIDE, WIDE), BF16),
            pltpu.VMEM((PAIRS, 128, 256), BF16),
            pltpu.VMEM((PAIRS, 128, 256), BF16),
            pltpu.VMEM((PAIRS, 128, 128), BF16),
            pltpu.VMEM((PAIRS, 128, 128), BF16),
            pltpu.VMEM((6, 8, 128), F32),
            pltpu.VMEM((6, 8, 128), F32),
            pltpu.VMEM((tokens, WIDE), BF16),
            pltpu.VMEM((tokens, WIDE), BF16),
            pltpu.VMEM((tokens, WIDE), BF16),
            pltpu.VMEM((tokens, 3 * WIDE), BF16),
            pltpu.VMEM((tokens, 2 * WIDE), BF16),
            pltpu.VMEM((tokens, 2 * WIDE), BF16),
            pltpu.VMEM((tokens, WIDE), BF16),
            pltpu.VMEM((tokens, WIDE), F32),
            pltpu.VMEM((tokens, WIDE), F32),
            pltpu.VMEM((tokens, WIDE), F32),
            pltpu.VMEM((tokens, 4 * WIDE), BF16),
            pltpu.VMEM((tokens, 4 * WIDE), BF16),
            pltpu.VMEM((7, HEADS, 128, 128), F32),
            pltpu.VMEM((PAIRS + 1, 128, 128), F32),
            pltpu.VMEM((PAIRS + 1, 128, 128), F32),
            pltpu.VMEM((HEADS, 128, 128), F32),
            pltpu.VMEM((PAIRS + 1, 128, 128), F32),
            pltpu.VMEM((tokens, WIDE), F32),
            pltpu.VMEM((tokens, WIDE), BF16),
            pltpu.VMEM((tokens, WIDE), BF16),
            pltpu.VMEM((128, 128), BF16),
            pltpu.VMEM((128, 128), F32),
            pltpu.VMEM((128, 128), F32),
            pltpu.VMEM((128, 128), BF16),
            pltpu.VMEM((128, 128), BF16),
            pltpu.SemaphoreType.DMA((16,)),
            pltpu.SemaphoreType.DMA,
            pltpu.SemaphoreType.DMA((6, 2)),
            pltpu.SemaphoreType.DMA((4,)),
            pltpu.SemaphoreType.DMA((3, 3, 6)),
        ],
        compiler_params=pltpu.CompilerParams(
            collective_id=1, has_side_effects=True, vmem_limit_bytes=60 * 1024 * 1024
        ),
    )(ends_in, jnp.concatenate([begins, filled], 1), *weights)


def body(mesh, ends_in, begins, filled, *weights):
    x, ends, small = layers(ends_in, begins, filled, weights, mesh)
    sums, small, ends = reduced(x, small, ends, mesh)
    return finished(sums, small, ends, weights)


def solution(mesh):
    placed = (
        P("section", None, ("dp", "ctx"), None),
        P(None, ("dp", "ctx")),
        P(None, ("dp", "ctx")),
        P("section", None),
        P("section", None),
        P("section", None, None),
        P("section", None),
        P("section", None, None),
        P("section", None, None),
        P("section", None, None),
        P("section", None),
        P("section", None),
        P("section", None),
        P("section", None, None),
        P("section", None),
        P("section", None, None),
        P("section", None),
    )
    return jax.shard_map(
        functools.partial(body, mesh),
        mesh=mesh,
        in_specs=placed,
        out_specs=(
            P("section", None, ("dp", "ctx"), None),
            P("section", None),
            P("section", None),
            P("section", None, None),
            P("section", None),
            P("section", None, None),
            P("section", None, None),
            P("section", None, None),
            P("section", None),
            P("section", None),
            P("section", None),
            P("section", None, None),
            P("section", None),
            P("section", None, None),
            P("section", None),
        ),
        check_vma=False,
    )
```
